256 devices in a mesh: tm: 16 (over y_lo, x, core), row: 16 (over z, y_hi).
Axes of the slice: x: 4, y: 4 (y_hi: 2, y_lo: 2; y = y_hi * 2 + y_lo), z: 8, core: 2. Of those that a mesh axis runs over, the one named last changes fastest.
Arguments:
- fields: bfloat16 [2, 16, 2, 1024, 1024], P(None, 'tm', None, 'row'), may hold values from -2 to 2
- mom_table: int32 [2, 1, 4], replicated, may hold values from 0 to 1
Outputs:
- products: bfloat16 [2, 1, 16, 2, 1024, 1024], P(None, None, 'tm', None, 'row')
- correlator: float32 [2, 1, 16, 2], P(None, None, 'tm')
The draws below stay inside these ranges and needn't reach their ends.
Inputs may be any that keep to these rules, and one draw needn't show every extreme that they name: `mom_table`: momentum indices of the fields.
All inputs are finite; a program needn't handle non-finite values.
Results may differ from the reference program's by a relative error of at most 0.0052.
Values may be sent and summed in bfloat16 or wider, within the bound.
No kernel may reach another device: no remote copies, remote signals or barrier semaphores. Data moves between devices by JAX's collectives and lax.ppermute only.
A program may use at most 128 MiB of HBM per device.

```python
import jax
import jax.numpy as jnp
from jax import lax

NMODE = 1024
NMOM = 2
ROUNDS = 2
NCOMB = 1
NT = 16


def plant(array, key, least, largest):
    place = [jax.random.randint(jax.random.fold_in(key, axis), (), 0, length) for axis, length in enumerate(array.shape)]
    widest = array.shape.index(max(array.shape))
    neighbour = place[:widest] + [(place[widest] + 1) % array.shape[widest]] + place[widest + 1:]
    return array.at[tuple(place)].set(least).at[tuple(neighbour)].set(largest)


def steps_of(rng, extent, pieces, low, largest):
    gain = 1.0
    for position, parts in pieces:
        draws = jax.random.uniform(jax.random.fold_in(jax.random.fold_in(rng, 6), position), (parts,), jnp.float32, low / len(pieces), largest / len(pieces))
        gain = gain * jnp.repeat(jnp.exp(draws), extent[position] // parts).reshape((-1,) + (1,) * (len(extent) - 1 - position))
    return gain


def gaussian(own_key, extent, deviation, most, cuts=(), dtype=jnp.bfloat16):
    level = steps_of(own_key, extent, cuts, -0.22, 0.18) if cuts else 1.0
    result = jax.random.normal(own_key, extent, jnp.float32) * deviation * level
    return jnp.minimum(jnp.maximum(result, -most), most).astype(dtype)


def setup_inputs(seed: int = 0) -> dict:
    streams_of = jax.random.split(jax.random.key(seed), 3)
    fields = gaussian(streams_of[0], (NMOM, NT, 2, NMODE, NMODE), 0.15, 2.0, ((1, 16), (3, 16)))
    mom_table = plant(jax.random.randint(streams_of[1], (ROUNDS, NCOMB, 4), 0, NMOM), jax.random.fold_in(streams_of[1], 1), 0, NMOM - 1).astype(jnp.int32)
    return dict(fields=fields, mom_table=mom_table)


def complex_product(left_side, right_side):
    highest = lax.Precision.HIGHEST
    real_part = jnp.matmul(left_side[..., 0, :, :], right_side[..., 0, :, :], precision=highest) - jnp.matmul(left_side[..., 1, :, :], right_side[..., 1, :, :], precision=highest)
    imag_part = jnp.matmul(left_side[..., 0, :, :], right_side[..., 1, :, :], precision=highest) + jnp.matmul(left_side[..., 1, :, :], right_side[..., 0, :, :], precision=highest)
    return jnp.stack([real_part, imag_part], axis=-3)


def reference(fields, mom_table):
    whole = fields.astype(jnp.float32)
    product_rounds = []
    correlator_rounds = []
    for round_number in range(ROUNDS):
        partner = jnp.roll(whole, -(round_number + 1), axis=1)
        product_list = []
        correlator_list = []
        for combination in range(NCOMB):
            picks = mom_table[round_number, combination]
            product = complex_product(whole[picks[0]], partner[picks[1]]).astype(jnp.bfloat16)
            crossed = complex_product(partner[picks[2]], whole[picks[3]]).astype(jnp.bfloat16)
            product_f = product.astype(jnp.float32)
            crossed_t = jnp.swapaxes(crossed.astype(jnp.float32), -1, -2)
            real_part = jnp.sum(product_f[:, 0] * crossed_t[:, 0] - product_f[:, 1] * crossed_t[:, 1], axis=(1, 2))
            imag_part = jnp.sum(product_f[:, 0] * crossed_t[:, 1] + product_f[:, 1] * crossed_t[:, 0], axis=(1, 2))
            product_list.append(product)
            correlator_list.append(jnp.stack([real_part, imag_part], axis=-1) / jnp.float32(NMODE))
        product_rounds.append(jnp.stack(product_list))
        correlator_rounds.append(jnp.stack(correlator_list))
    return jnp.stack(product_rounds), jnp.stack(correlator_rounds)
```

```python
import functools

import jax
import jax.numpy as jnp
from jax import lax
from jax.experimental import pallas as pl
from jax.experimental.pallas import tpu as pltpu
from jax.sharding import PartitionSpec as P

BOTH = ("tm", "row")
BF16 = jnp.bfloat16
F32 = jnp.float32


def index_of(m, c, z, h, ring):
    return ((m % 8) * 2 + c) * (2 * ring) + (z % ring) * 2 + h


def moved(block, route, ring):
    pairs = []
    for m in range(8):
        for c in range(2):
            for z in range(ring):
                for h in range(2):
                    pairs.append((index_of(m, c, z, h, ring), index_of(*route(m, c, z, h), ring)))
    return lax.ppermute(block, BOTH, pairs)


def along(step):
    return lambda m, c, z, h: (m, c, z + step, h)


def other_core(m, c, z, h):
    return (m, 1 - c, z, h)


def to_hub(turn):
    return lambda m, c, z, h: (m, h ^ turn, z, c)


def hub_ahead(step):
    def route(m, c, z, h):
        s = (2 * m + h + 1 + c) % 16
        return (s // 2, c, z + step, s % 2)

    return route


def from_hub(turn):
    def route(m, c, z, h):
        t = (2 * m + h - 1 - c) % 16
        return (t // 2, t % 2, z, c ^ turn)

    return route


VMEM = pl.BlockSpec(memory_space=pltpu.VMEM)
SMEM = pl.BlockSpec(memory_space=pltpu.SMEM)


def left_side(a_ref, place):
    columns = pl.ds(pl.multiple_of(place * 128, 128), 128)
    real, imag = a_ref[0, :, columns], a_ref[1, :, columns]
    return jnp.concatenate(
        [jnp.concatenate([real, -imag], axis=1), jnp.concatenate([imag, real], axis=1)], axis=0
    )


def add_products(info, a_ref, own, other, acc_in, acc_out):
    total = acc_in[...] if acc_in is not None else None
    for number in range(len(own)):
        block = jnp.where(info[8] == 1, own[number][...], other[number][...]).reshape(256, 1024)
        term = jnp.dot(left_side(a_ref, info[number]), block, preferred_element_type=F32)
        total = term if total is None else total + term
    acc_out[...] = total


def first_kernel(info, a_ref, own, other, acc_out):
    add_products(info, a_ref, [own], [other], None, acc_out)


def step_kernel(info, a_ref, own_u, own_d, other_u, other_d, acc_in, acc_out):
    add_products(info, a_ref, [own_u, own_d], [other_u, other_d], acc_in, acc_out)


def params(flops):
    return dict(
        compiler_params=pltpu.CompilerParams(vmem_limit_bytes=32 * 1024 * 1024),
        cost_estimate=pl.CostEstimate(flops=flops, bytes_accessed=4 << 20, transcendentals=0),
    )


def first_step(info, a, own, other):
    return pl.pallas_call(
        first_kernel,
        out_shape=jax.ShapeDtypeStruct((256, 1024), F32),
        in_specs=[SMEM] + [VMEM] * 3,
        out_specs=VMEM,
        **params(2 * 256 * 256 * 1024),
    )(info, a, own, other)


def next_step(info, a, own_u, own_d, other_u, other_d, acc):
    return pl.pallas_call(
        step_kernel,
        out_shape=jax.ShapeDtypeStruct((256, 1024), F32),
        in_specs=[SMEM] + [VMEM] * 6,
        out_specs=VMEM,
        input_output_aliases={6: 0},
        **params(4 * 256 * 256 * 1024),
    )(info, a, own_u, own_d, other_u, other_d, acc)


def crossed_block(real, imag, drhs):
    block = jnp.dot(real, drhs[0:1024, :], preferred_element_type=F32)
    block += jnp.dot(imag, drhs[1024:2048, :], preferred_element_type=F32)
    turned = jnp.concatenate([block[:, :128].T, block[:, 128:].T], axis=0)
    return turned.astype(BF16)


def crossed_kernel(info, *refs):
    slices, own, other = refs[0:8], refs[8:15], refs[15:22]
    drhs, crossed = refs[22], refs[23]
    for number in range(8):
        top = pl.multiple_of(info[number] * 128, 128)
        real, imag = slices[number][0], slices[number][1]
        drhs[pl.ds(top, 128), 0:128] = real
        drhs[pl.ds(top, 128), 128:256] = imag
        drhs[pl.ds(1024 + top, 128), 0:128] = -imag
        drhs[pl.ds(1024 + top, 128), 128:256] = real
    for number in range(7):
        real = jnp.where(info[9] == 1, own[number][0], other[number][0])
        imag = jnp.where(info[9] == 1, own[number][1], other[number][1])
        columns = pl.ds(pl.multiple_of(info[number] * 128, 128), 128)
        crossed[:, columns] = crossed_block(real, imag, drhs)


def crossed_most(info, slices, own, other):
    return pl.pallas_call(
        crossed_kernel,
        out_shape=(jax.ShapeDtypeStruct((2048, 256), BF16), jax.ShapeDtypeStruct((256, 1024), BF16)),
        in_specs=[SMEM] + [VMEM] * 22,
        out_specs=(VMEM, VMEM),
        **params(14 * 128 * 2048 * 256),
    )(info, *slices, *own, *other)


def last_kernel(info, a_ref, own_re, own_im, other_re, other_im, acc, drhs, crossed, keep, send, trace, turned):
    place = info[7]
    real = jnp.where(info[8] == 1, own_re[...], other_re[...])
    imag = jnp.where(info[8] == 1, own_im[...], other_im[...])
    block = jnp.concatenate([real, imag], axis=0)
    product = acc[...] + jnp.dot(left_side(a_ref, place), block, preferred_element_type=F32)
    rounded = product.astype(BF16)
    for part in range(2):
        low, high = rounded[part * 128 : part * 128 + 64], rounded[part * 128 + 64 : part * 128 + 128]
        keep[part] = jnp.where(info[10] == 0, low, high)
        send[part] = jnp.where(info[10] == 0, high, low)
    real = jnp.where(info[9] == 1, own_re[...], other_re[...])
    imag = jnp.where(info[9] == 1, own_im[...], other_im[...])
    turned[...] = crossed[...]
    turned[:, pl.ds(pl.multiple_of(place * 128, 128), 128)] = crossed_block(real, imag, drhs)
    p_re, p_im = rounded[:128].astype(F32), rounded[128:].astype(F32)
    c_re, c_im = turned[:128, :].astype(F32), turned[128:, :].astype(F32)
    re = jnp.sum(p_re * c_re - p_im * c_im, axis=0, keepdims=True)
    im = jnp.sum(p_re * c_im + p_im * c_re, axis=0, keepdims=True)
    re = jnp.sum(re, axis=1, keepdims=True)
    im = jnp.sum(im, axis=1, keepdims=True)
    lane = lax.broadcasted_iota(jnp.int32, (1, 128), 1)
    trace[...] = jnp.where(lane == 0, re, im)


def last_step(info, a, own_re, own_im, other_re, other_im, acc, drhs, crossed):
    half = jax.ShapeDtypeStruct((2, 64, 1024), BF16)
    return pl.pallas_call(
        last_kernel,
        out_shape=(half, half, jax.ShapeDtypeStruct((1, 128), F32)),
        in_specs=[SMEM] + [VMEM] * 8,
        out_specs=(VMEM, VMEM, VMEM),
        scratch_shapes=[pltpu.VMEM((256, 1024), BF16)],
        **params(2 * 256 * 256 * 1024 + 2 * 128 * 2048 * 256),
    )(info, a, own_re, own_im, other_re, other_im, acc, drhs, crossed)


def shards(fields, mom_table):
    rows = fields[:, 0]
    tm, row = lax.axis_index("tm"), lax.axis_index("row")
    core, place, half = tm % 2, row // 2, row % 2
    ring = lax.axis_size("row") // 2
    mom_a, mom_b, mom_c, mom_d = [mom_table[core, 0, k] for k in range(4)]

    def go(block, route):
        return moved(block, route, ring)

    first = go(jnp.where(half == 0, rows[0], rows[1]), to_hub(0))
    second = go(jnp.where(half == 0, rows[1], rows[0]), to_hub(1))
    own = jnp.where(core == 0, jnp.concatenate([first, second], 1), jnp.concatenate([second, first], 1))

    offsets = [0, -1, 1, -2, 2, -3, 3, 4]
    own_blocks, up, down = [own], own, own
    for _ in range(3):
        up, down = go(up, along(1)), go(down, along(-1))
        own_blocks += [up, down]
    far_re, far_im = go(up[0], along(1)), go(down[1], along(-1))
    other_blocks = [go(block, other_core) for block in own_blocks]
    other_re, other_im = go(far_re, other_core), go(far_im, other_core)

    places = [lax.rem(place + offset + ring, ring) for offset in offsets]

    def info_of(order):
        flags = [mom_b == core, mom_c == core, core]
        return jnp.stack([places[k] for k in order] + [jnp.int32(f) for f in flags] + [jnp.int32(0)])

    whole_info = info_of(range(8))

    a = go(jnp.where(mom_a == core, own_blocks[0], other_blocks[0]), hub_ahead(0))

    def columns(k, at):
        def cut(block):
            return lax.dynamic_slice(block, (0, 0, at * 128), (2, 128, 128))

        return jnp.where(mom_d == core, cut(own_blocks[k]), cut(other_blocks[k]))

    slices = [None] * 8
    for group in ([0, 1, 2], [3, 4], [5, 6]):
        got = go(jnp.stack([columns(k, place) for k in group]), hub_ahead(0))
        for position, k in enumerate(group):
            slices[k] = got[position]
    slices[7] = go(columns(0, lax.rem(place + 4, ring)), hub_ahead(4))

    acc = first_step(whole_info, a, own_blocks[0], other_blocks[0])
    for k in (1, 3, 5):
        step_info = info_of([k, k + 1] + [0] * 6)
        acc = next_step(step_info, a, own_blocks[k], own_blocks[k + 1], other_blocks[k], other_blocks[k + 1], acc)
    drhs, crossed = crossed_most(whole_info, slices, own_blocks, other_blocks)
    keep, send, trace = last_step(whole_info, a, far_re, far_im, other_re, other_im, acc, drhs, crossed)

    for distance in (1, 2, 4):
        trace = trace + go(trace, lambda m, c, z, h: (m, c, z ^ distance, h))
    trace = trace[0, :2] / F32(1024)
    kept, sent = go(trace, from_hub(0)), go(trace, from_hub(1))
    correlator = jnp.where(half == 0, jnp.stack([kept, sent]), jnp.stack([sent, kept]))[:, None, None, :]

    kept, sent = go(keep, from_hub(0)), go(send, from_hub(1))
    products = jnp.where(half == 0, jnp.stack([kept, sent]), jnp.stack([sent, kept]))[:, None, None]
    return products, correlator


def solution(mesh):
    return jax.shard_map(
        shards,
        mesh=mesh,
        in_specs=(P(None, "tm", None, "row", None), P()),
        out_specs=(P(None, None, "tm", None, "row", None), P(None, None, "tm", None)),
        check_vma=False,
    )
```

```python
import jax
import jax.numpy as jnp
from jax import lax
from jax.experimental import pallas as pl
from jax.experimental.pallas import tpu as pltpu
from jax.sharding import PartitionSpec as P

BOTH = ("tm", "row")
BF16 = jnp.bfloat16
F32 = jnp.float32


def hub_of(s):
    m, odd = divmod(s % 16, 2)
    low, x = divmod(m, 4)
    return (1 - low) * 4 + x, odd ^ low


SERVED = {hub_of(s): s for s in range(16)}


def moved(block, route):
    def index_of(m, c, z, h):
        return ((m % 8) * 2 + c) * 16 + (z % 8) * 2 + h

    places = [(m, c, z, h) for m in range(8) for c in range(2) for z in range(8) for h in range(2)]
    return lax.ppermute(block, BOTH, [(index_of(*at), index_of(*route(*at))) for at in places])


def along(step):
    return lambda m, c, z, h: (m, c, z + step, h)


def other_core(m, c, z, h):
    return (m, 1 - c, z, h)


def to_hub(step):
    def route(m, c, z, h):
        column, half = hub_of(2 * m + c)
        return (column, h, z + step, half)

    return route


def hub_ahead(step):
    def route(m, c, z, h):
        column, half = hub_of(SERVED[m, h] + 1 + c)
        return (column, c, z + step, half)

    return route


def from_hub(turn):
    def route(m, c, z, h):
        t = (SERVED[m, h] - 1 - c) % 16
        return (t // 2, t % 2, z, c ^ turn)

    return route


VMEM = pl.BlockSpec(memory_space=pltpu.VMEM)
SMEM = pl.BlockSpec(memory_space=pltpu.SMEM)
SLICES = jax.ShapeDtypeStruct((2, 128, 128), BF16)


def call(kernel, info, arrays, out_shape, flops, scratch=()):
    outs = jax.tree.map(lambda _: VMEM, out_shape)
    return pl.pallas_call(
        kernel,
        out_shape=out_shape,
        in_specs=[SMEM] + [VMEM] * len(arrays),
        out_specs=outs,
        scratch_shapes=scratch,
        compiler_params=pltpu.CompilerParams(vmem_limit_bytes=24 * 1024 * 1024),
        cost_estimate=pl.CostEstimate(flops=flops, bytes_accessed=1 << 20, transcendentals=0),
    )(info, *arrays)


def place_of(info, offset):
    return lax.rem(info[0] + (offset + 8), 8)


def columns_of(info, offset):
    return pl.ds(pl.multiple_of(place_of(info, offset) * 128, 128), 128)


def halves(info, own, other):
    first = jnp.where(info[1] == 0, own, other)
    second = jnp.where(info[1] == 0, other, own)
    return first, second


def whole(info, own_ref, other_ref, momentum, part):
    return jnp.concatenate(halves(info, own_ref[momentum, part], other_ref[momentum, part]), axis=0)


def cut(info, own_ref, other_ref, offset, out):
    columns = columns_of(info, offset)
    for part in range(2):
        first, second = halves(info, own_ref[info[5], part, :, columns], other_ref[info[5], part, :, columns])
        out[part, 0:64] = first
        out[part, 64:128] = second


def first_cut_kernel(info, own, other, a, across):
    for part in range(2):
        a[part] = whole(info, own, other, info[2], part)
    cut(info, own, other, 4, across)


def cut_kernel(info, *refs):
    count = len(refs) // 2
    for k in range(count):
        cut(info, refs[k], refs[count + k], 0, refs[-1].at[k])


def left_side(info, a_ref, offset):
    columns = columns_of(info, offset)
    real, imag = a_ref[0, :, columns], a_ref[1, :, columns]
    return jnp.concatenate(
        [jnp.concatenate([real, -imag], axis=1), jnp.concatenate([imag, real], axis=1)], axis=0
    )


def products_kernel(offsets, info, a_ref, *refs):
    count = len(offsets)
    own, other, out = refs[:count], refs[count : 2 * count], refs[-1]
    total = refs[2 * count][...] if len(refs) > 2 * count + 1 else None
    for offset, one, two in zip(offsets, own, other):
        block = jnp.concatenate([whole(info, one, two, info[3], part) for part in range(2)], axis=0)
        term = jnp.dot(left_side(info, a_ref, offset), block, preferred_element_type=F32)
        total = term if total is None else total + term
    out[...] = total


def crossed_block(real, imag, drhs):
    block = jnp.dot(real, drhs[0:1024, :], preferred_element_type=F32)
    block += jnp.dot(imag, drhs[1024:2048, :], preferred_element_type=F32)
    turned = jnp.concatenate([block[:, :128].T, block[:, 128:].T], axis=0)
    return turned.astype(BF16)


OFFSETS = (0, -1, 1, -2, 2, -3, 3, 4)


def crossed_kernel(info, near, late, across, *refs):
    own, other, drhs, crossed = refs[0:7], refs[7:14], refs[14], refs[15]
    slices = [near.at[k] for k in range(3)] + [late.at[k] for k in range(4)] + [across]
    for offset, piece in zip(OFFSETS, slices):
        top = pl.multiple_of(place_of(info, offset) * 128, 128)
        real, imag = piece[0], piece[1]
        drhs[pl.ds(top, 128), 0:128] = real
        drhs[pl.ds(top, 128), 128:256] = imag
        drhs[pl.ds(1024 + top, 128), 0:128] = -imag
        drhs[pl.ds(1024 + top, 128), 128:256] = real
    for offset, one, two in zip(OFFSETS, own, other):
        real, imag = (whole(info, one, two, info[4], part) for part in range(2))
        crossed[:, columns_of(info, offset)] = crossed_block(real, imag, drhs)


def last_kernel(info, a_ref, own_0, own_1, other_0, other_1, acc, drhs, crossed, keep, send, trace, turned):
    def parts(momentum):
        own = jnp.where(momentum == 0, own_0[...], own_1[...])
        other = jnp.where(momentum == 0, other_0[...], other_1[...])
        return [jnp.concatenate(halves(info, own[part], other[part]), axis=0) for part in range(2)]

    block = jnp.concatenate(parts(info[3]), axis=0)
    product = acc[...] + jnp.dot(left_side(info, a_ref, 4), block, preferred_element_type=F32)
    rounded = product.astype(BF16)
    for part in range(2):
        low, high = rounded[part * 128 : part * 128 + 64], rounded[part * 128 + 64 : part * 128 + 128]
        keep[part], send[part] = halves(info, low, high)
    real, imag = parts(info[4])
    turned[...] = crossed[...]
    turned[:, columns_of(info, 4)] = crossed_block(real, imag, drhs)
    p_re, p_im = rounded[:128].astype(F32), rounded[128:].astype(F32)
    c_re, c_im = turned[:128, :].astype(F32), turned[128:, :].astype(F32)
    re = jnp.sum(p_re * c_re - p_im * c_im, axis=0, keepdims=True)
    im = jnp.sum(p_re * c_im + p_im * c_re, axis=0, keepdims=True)
    re = jnp.sum(re, axis=1, keepdims=True)
    im = jnp.sum(im, axis=1, keepdims=True)
    lane = lax.broadcasted_iota(jnp.int32, (1, 128), 1)
    trace[...] = jnp.where(lane == 2 * info[0], re, jnp.where(lane == 2 * info[0] + 1, im, 0.0))


def shards(fields, mom_table):
    rows = fields[:, 0]
    tm, row = lax.axis_index("tm"), lax.axis_index("row")
    core, place, half = tm % 2, row // 2, row % 2
    momenta = lax.dynamic_index_in_dim(mom_table, core, 0, keepdims=False)[0]
    info = jnp.concatenate([jnp.stack([place, core]), momenta])
    wall = lax.optimization_barrier
    block_of_products = jax.ShapeDtypeStruct((256, 1024), F32)

    own = moved(rows, to_hub(0))

    u1, d1, ownx = moved(own, along(1)), moved(own, along(-1)), moved(own, other_core)
    u1, d1, ownx = wall((u1, d1, ownx))

    u2, d2 = moved(u1, along(1)), moved(d1, along(-1))
    u1x, d1x = moved(u1, other_core), moved(d1, other_core)
    a, across = call(first_cut_kernel, info, [own, ownx], (jax.ShapeDtypeStruct((2, 128, 1024), BF16), SLICES), 1)
    a = moved(a, hub_ahead(0))
    u2, d2, u1x, d1x, a, across = wall((u2, d2, u1x, d1x, a, across))

    u3, d3 = moved(u2, along(1)), moved(d2, along(-1))
    u2x, d2x = moved(u2, other_core), moved(d2, other_core)
    near = call(cut_kernel, info, [own, u1, d1, ownx, u1x, d1x], jax.ShapeDtypeStruct((3, 2, 128, 128), BF16), 1)
    near, across = moved(near, hub_ahead(0)), moved(across, hub_ahead(4))
    acc = call(
        lambda *refs: products_kernel(OFFSETS[:3], *refs),
        info,
        [a, own, u1, d1, ownx, u1x, d1x],
        block_of_products,
        1,
    )
    u3, d3, u2x, d2x, near, across, acc = wall((u3, d3, u2x, d2x, near, across, acc))

    far_0, far_1 = moved(u3[0], along(1)), moved(d3[1], along(-1))
    u3x, d3x = moved(u3, other_core), moved(d3, other_core)
    late = call(
        cut_kernel, info, [u2, d2, u3, d3, u2x, d2x, u3x, d3x], jax.ShapeDtypeStruct((4, 2, 128, 128), BF16), 1
    )
    late = moved(late, hub_ahead(0))
    acc = call(
        lambda *refs: products_kernel(OFFSETS[3:7], *refs),
        info,
        [a, u2, d2, u3, d3, u2x, d2x, u3x, d3x, acc],
        block_of_products,
        1,
    )
    far_0, far_1, late, acc = wall((far_0, far_1, late, acc))

    far_0x, far_1x = moved(far_0, other_core), moved(far_1, other_core)
    drhs, crossed = call(
        crossed_kernel,
        info,
        [near, late, across, own, u1, d1, u2, d2, u3, d3, ownx, u1x, d1x, u2x, d2x, u3x, d3x],
        (jax.ShapeDtypeStruct((2048, 256), BF16), jax.ShapeDtypeStruct((256, 1024), BF16)),
        1,
    )
    half_block = jax.ShapeDtypeStruct((2, 64, 1024), BF16)
    keep, send, trace = call(
        last_kernel,
        info,
        [a, far_0, far_1, far_0x, far_1x, acc, drhs, crossed],
        (half_block, half_block, jax.ShapeDtypeStruct((1, 128), F32)),
        1,
        [pltpu.VMEM((256, 1024), BF16)],
    )

    below, above = moved(trace, along(1)), moved(trace, along(-1))
    kept, sent = moved(keep, from_hub(0)), moved(send, from_hub(1))
    two, three = wall((trace + above, below + trace + above))
    below, above = moved(two, along(3)), moved(three, along(-3))
    trace, kept, sent = wall((below + three + above, kept, sent))
    first, second = moved(trace, from_hub(0)), moved(trace, from_hub(1))
    products = jnp.where(half == 0, jnp.stack([kept, sent]), jnp.stack([sent, kept]))[:, None, None]
    both = jnp.where(half == 0, jnp.concatenate([first, second]), jnp.concatenate([second, first]))
    correlator = jnp.sum(both[:, :16].reshape(2, 8, 2), axis=1)[:, None, None, :] / F32(1024)
    return products, correlator


def solution(mesh):
    return jax.shard_map(
        shards,
        mesh=mesh,
        in_specs=(P(None, "tm", None, "row", None), P()),
        out_specs=(P(None, None, "tm", None, "row", None), P(None, None, "tm", None)),
        check_vma=False,
    )
```

```python
import jax
import jax.numpy as jnp
from jax import lax
from jax.experimental import pallas as pl
from jax.experimental.pallas import tpu as pltpu
from jax.sharding import PartitionSpec as P

BOTH = ("tm", "row")
BF16 = jnp.bfloat16
F32 = jnp.float32


def hub_of(s):
    m, odd = divmod(s % 16, 2)
    low, x = divmod(m, 4)
    return (1 - low) * 4 + x, odd ^ low


SERVED = {hub_of(s): s for s in range(16)}


def moved(block, route):
    def index_of(m, c, z, h):
        return ((m % 8) * 2 + c) * 16 + (z % 8) * 2 + h

    places = [(m, c, z, h) for m in range(8) for c in range(2) for z in range(8) for h in range(2)]
    return lax.ppermute(block, BOTH, [(index_of(*at), index_of(*route(*at))) for at in places])


def along(step):
    return lambda m, c, z, h: (m, c, z + step, h)


def onward(m, c, z, h):
    return (m, c, z + (1 if c == 0 else -1), h)


def other_core(m, c, z, h):
    return (m, 1 - c, z, h)


def to_hub(step):
    def route(m, c, z, h):
        column, half = hub_of(2 * m + c)
        return (column, h, z + step, half)

    return route


def hub_ahead(step):
    def route(m, c, z, h):
        column, half = hub_of(SERVED[m, h] + 1 + c)
        return (column, c, z + (step if c == 0 else -step), half)

    return route


def from_hub(turn):
    def route(m, c, z, h):
        t = (SERVED[m, h] - 1 - c) % 16
        return (t // 2, t % 2, z, c ^ turn)

    return route


VMEM = pl.BlockSpec(memory_space=pltpu.VMEM)
SMEM = pl.BlockSpec(memory_space=pltpu.SMEM)
SLICES = jax.ShapeDtypeStruct((2, 128, 128), BF16)


def call(kernel, info, arrays, out_shape, flops, scratch=()):
    outs = jax.tree.map(lambda _: VMEM, out_shape)
    return pl.pallas_call(
        kernel,
        out_shape=out_shape,
        in_specs=[SMEM] + [VMEM] * len(arrays),
        out_specs=outs,
        scratch_shapes=scratch,
        compiler_params=pltpu.CompilerParams(vmem_limit_bytes=24 * 1024 * 1024),
        cost_estimate=pl.CostEstimate(flops=flops, bytes_accessed=1 << 20, transcendentals=0),
    )(info, *arrays)


def place_of(info, offset):
    return lax.rem(info[0] + jnp.where(info[1] == 0, 8 - offset, 8 + offset), 8)


def columns_of(info, offset):
    return pl.ds(pl.multiple_of(place_of(info, offset) * 128, 128), 128)


def halves(info, own, other):
    first = jnp.where(info[1] == 0, own, other)
    second = jnp.where(info[1] == 0, other, own)
    return first, second


def whole(info, own_ref, other_ref, momentum, part):
    return jnp.concatenate(halves(info, own_ref[momentum, part], other_ref[momentum, part]), axis=0)


def cut(info, own_ref, other_ref, offset, out):
    columns = columns_of(info, offset)
    for part in range(2):
        first, second = halves(info, own_ref[info[5], part, :, columns], other_ref[info[5], part, :, columns])
        out[part, 0:64] = first
        out[part, 64:128] = second


def first_cut_kernel(info, own, other, a):
    for part in range(2):
        a[part] = whole(info, own, other, info[2], part)


def cut_kernel(info, *refs):
    count = len(refs) // 2
    for k in range(count):
        cut(info, refs[k], refs[count + k], 0, refs[-1].at[k])


def across_kernel(info, own, other, out):
    cut(info, own, other, -2, out)


def left_side(info, a_ref, offset):
    columns = columns_of(info, offset)
    real, imag = a_ref[0, :, columns], a_ref[1, :, columns]
    return jnp.concatenate(
        [jnp.concatenate([real, -imag], axis=1), jnp.concatenate([imag, real], axis=1)], axis=0
    )


def products_kernel(offsets, info, a_ref, *refs):
    count = len(offsets)
    own, other, out = refs[:count], refs[count : 2 * count], refs[-1]
    total = refs[2 * count][...] if len(refs) > 2 * count + 1 else None
    for offset, one, two in zip(offsets, own, other):
        block = jnp.concatenate([whole(info, one, two, info[3], part) for part in range(2)], axis=0)
        term = jnp.dot(left_side(info, a_ref, offset), block, preferred_element_type=F32)
        total = term if total is None else total + term
    out[...] = total


def crossed_block(real, imag, drhs):
    block = jnp.dot(real, drhs[0:1024, :], preferred_element_type=F32)
    block += jnp.dot(imag, drhs[1024:2048, :], preferred_element_type=F32)
    turned = jnp.concatenate([block[:, :128].T, block[:, 128:].T], axis=0)
    return turned.astype(BF16)


OFFSETS = (0, 1, -1, 2, -2, 3, -3, 4)


def crossed_kernel(info, near, late, across, *refs):
    own, other, drhs, crossed = refs[0:7], refs[7:14], refs[14], refs[15]
    slices = [near.at[k] for k in range(3)] + [late.at[k] for k in range(4)] + [across]
    for offset, piece in zip(OFFSETS, slices):
        top = pl.multiple_of(place_of(info, offset) * 128, 128)
        real, imag = piece[0], piece[1]
        drhs[pl.ds(top, 128), 0:128] = real
        drhs[pl.ds(top, 128), 128:256] = imag
        drhs[pl.ds(1024 + top, 128), 0:128] = -imag
        drhs[pl.ds(1024 + top, 128), 128:256] = real
    for offset, one, two in zip(OFFSETS, own, other):
        real, imag = (whole(info, one, two, info[4], part) for part in range(2))
        crossed[:, columns_of(info, offset)] = crossed_block(real, imag, drhs)


def last_kernel(info, a_ref, own, other, acc, drhs, crossed, keep, send, trace, turned):
    def parts(momentum):
        return [whole(info, own, other, momentum, part) for part in range(2)]

    block = jnp.concatenate(parts(info[3]), axis=0)
    product = acc[...] + jnp.dot(left_side(info, a_ref, 4), block, preferred_element_type=F32)
    rounded = product.astype(BF16)
    for part in range(2):
        low, high = rounded[part * 128 : part * 128 + 64], rounded[part * 128 + 64 : part * 128 + 128]
        keep[part], send[part] = halves(info, low, high)
    real, imag = parts(info[4])
    turned[...] = crossed[...]
    turned[:, columns_of(info, 4)] = crossed_block(real, imag, drhs)
    p_re, p_im = rounded[:128].astype(F32), rounded[128:].astype(F32)
    c_re, c_im = turned[:128, :].astype(F32), turned[128:, :].astype(F32)
    re = jnp.sum(p_re * c_re - p_im * c_im, axis=0, keepdims=True)
    im = jnp.sum(p_re * c_im + p_im * c_re, axis=0, keepdims=True)
    re = jnp.sum(re, axis=1, keepdims=True)
    im = jnp.sum(im, axis=1, keepdims=True)
    lane = lax.broadcasted_iota(jnp.int32, (1, 128), 1)
    trace[...] = jnp.where(lane == 2 * info[0], re, jnp.where(lane == 2 * info[0] + 1, im, 0.0))


def shards(fields, mom_table):
    rows = fields[:, 0]
    tm, row = lax.axis_index("tm"), lax.axis_index("row")
    core, place, half = tm % 2, row // 2, row % 2
    momenta = lax.dynamic_index_in_dim(mom_table, core, 0, keepdims=False)[0]
    info = jnp.concatenate([jnp.stack([place, core]), momenta])
    wall = lax.optimization_barrier
    block_of_products = jax.ShapeDtypeStruct((256, 1024), F32)

    own = moved(rows, to_hub(0))
    ownx = moved(own, other_core)

    p1, q1 = moved(own, onward), moved(ownx, onward)
    a = moved(call(first_cut_kernel, info, [own, ownx], jax.ShapeDtypeStruct((2, 128, 1024), BF16), 1), hub_ahead(0))

    p2, p1x = moved(p1, onward), moved(p1, other_core)
    q2, q1x = moved(q1, onward), moved(q1, other_core)
    first_three = [own, p1, q1x, ownx, q1, p1x]
    near = call(cut_kernel, info, first_three, jax.ShapeDtypeStruct((3, 2, 128, 128), BF16), 1)
    near = moved(near, hub_ahead(0))
    p2, a = wall((p2, a))

    p3, p2x = moved(p2, onward), moved(p2, other_core)
    q3, q2x = moved(q2, onward), moved(q2, other_core)
    across = moved(call(across_kernel, info, [p2, q2], SLICES, 1), hub_ahead(2))
    acc = call(
        lambda *refs: products_kernel(OFFSETS[:3], *refs), info, [a] + first_three, block_of_products, 1
    )
    p3, near = wall((p3, near))

    p4, p3x = moved(p3, onward), moved(p3, other_core)
    q3x = moved(q3, other_core)
    next_four = [p2, q2x, p3, q3x, q2, p2x, q3, p3x]
    late = call(cut_kernel, info, next_four, jax.ShapeDtypeStruct((4, 2, 128, 128), BF16), 1)
    late = moved(late, hub_ahead(0))
    acc = call(
        lambda *refs: products_kernel(OFFSETS[3:7], *refs), info, [a] + next_four + [acc], block_of_products, 1
    )
    p4, across, acc, late = wall((p4, across, acc, late))

    p4x = moved(p4, other_core)
    drhs, crossed = call(
        crossed_kernel,
        info,
        [near, late, across] + first_three[:3] + next_four[:4] + first_three[3:] + next_four[4:],
        (jax.ShapeDtypeStruct((2048, 256), BF16), jax.ShapeDtypeStruct((256, 1024), BF16)),
        1,
    )
    half_block = jax.ShapeDtypeStruct((2, 64, 1024), BF16)
    keep, send, trace = call(
        last_kernel,
        info,
        [a, p4, p4x, acc, drhs, crossed],
        (half_block, half_block, jax.ShapeDtypeStruct((1, 128), F32)),
        1,
        [pltpu.VMEM((256, 1024), BF16)],
    )

    below, above = moved(trace, along(1)), moved(trace, along(-1))
    kept, sent = moved(keep, from_hub(0)), moved(send, from_hub(1))
    two, three = wall((trace + above, below + trace + above))
    below, above = moved(two, along(3)), moved(three, along(-3))
    trace, kept, sent = wall((below + three + above, kept, sent))
    first, second = moved(trace, from_hub(0)), moved(trace, from_hub(1))
    products = jnp.where(half == 0, jnp.stack([kept, sent]), jnp.stack([sent, kept]))[:, None, None]
    both = jnp.where(half == 0, jnp.concatenate([first, second]), jnp.concatenate([second, first]))
    correlator = jnp.sum(both[:, :16].reshape(2, 8, 2), axis=1)[:, None, None, :] / F32(1024)
    return products, correlator


def solution(mesh):
    return jax.shard_map(
        shards,
        mesh=mesh,
        in_specs=(P(None, "tm", None, "row", None), P()),
        out_specs=(P(None, None, "tm", None, "row", None), P(None, None, "tm", None)),
        check_vma=False,
    )
```

```python
import jax
import jax.numpy as jnp
from jax import lax
from jax.experimental import pallas as pl
from jax.experimental.pallas import tpu as pltpu
from jax.sharding import PartitionSpec as P

BOTH = ("tm", "row")
BF16 = jnp.bfloat16
F32 = jnp.float32


def hub_of(s):
    m, odd = divmod(s % 16, 2)
    low, x = divmod(m, 4)
    return (1 - low) * 4 + x, odd ^ low


SERVED = {hub_of(s): s for s in range(16)}


def moved(block, route):
    def index_of(m, c, z, h):
        return ((m % 8) * 2 + c) * 16 + (z % 8) * 2 + h

    places = [(m, c, z, h) for m in range(8) for c in range(2) for z in range(8) for h in range(2)]
    return lax.ppermute(block, BOTH, [(index_of(*at), index_of(*route(*at))) for at in places])


def along(step):
    return lambda m, c, z, h: (m, c, z + step, h)


def onward(m, c, z, h):
    return (m, c, z + (1 if c == 0 else -1), h)


def other_core(m, c, z, h):
    return (m, 1 - c, z, h)


def to_hub(turn, step):
    def route(m, c, z, h):
        column, half = hub_of(2 * m + c)
        core = h ^ turn
        return (column, core, z + (step if core == 0 else -step), half)

    return route


def hub_ahead(step):
    def route(m, c, z, h):
        column, half = hub_of(SERVED[m, h] + 1 + c)
        return (column, c, z + (step if c == 0 else -step), half)

    return route


def from_hub(turn):
    def route(m, c, z, h):
        t = (SERVED[m, h] - 1 - c) % 16
        return (t // 2, t % 2, z, c ^ turn)

    return route


VMEM = pl.BlockSpec(memory_space=pltpu.VMEM)
SMEM = pl.BlockSpec(memory_space=pltpu.SMEM)
SLICES = jax.ShapeDtypeStruct((2, 128, 128), BF16)


def call(kernel, info, arrays, out_shape, flops, scratch=()):
    outs = jax.tree.map(lambda _: VMEM, out_shape)
    return pl.pallas_call(
        kernel,
        out_shape=out_shape,
        in_specs=[SMEM] + [VMEM] * len(arrays),
        out_specs=outs,
        scratch_shapes=scratch,
        compiler_params=pltpu.CompilerParams(vmem_limit_bytes=24 * 1024 * 1024),
        cost_estimate=pl.CostEstimate(flops=flops, bytes_accessed=1 << 20, transcendentals=0),
    )(info, *arrays)


def place_of(info, offset):
    return lax.rem(info[0] + jnp.where(info[1] == 0, 8 - offset, 8 + offset), 8)


def columns_of(info, offset):
    return pl.ds(pl.multiple_of(place_of(info, offset) * 128, 128), 128)


def halves(info, own, other):
    first = jnp.where(info[1] == 0, own, other)
    second = jnp.where(info[1] == 0, other, own)
    return first, second


def whole(info, own_ref, other_ref, momentum, part):
    return jnp.concatenate(halves(info, own_ref[momentum, part], other_ref[momentum, part]), axis=0)


def cut(info, own_ref, other_ref, offset, out):
    columns = columns_of(info, offset)
    for part in range(2):
        first, second = halves(info, own_ref[info[5], part, :, columns], other_ref[info[5], part, :, columns])
        out[part, 0:64] = first
        out[part, 64:128] = second


def first_cut_kernel(info, own, other, a):
    for part in range(2):
        a[part] = whole(info, own, other, info[2], part)


def near_kernel(info, *refs):
    for k in range(3):
        cut(info, refs[k], refs[3 + k], 0, refs[-1].at[k])


def middle_kernel(info, own, own_x, other, other_x, middle, down, up, across):
    cut(info, own, other, 0, middle.at[0])
    cut(info, own_x, other_x, 0, middle.at[1])
    cut(info, own, other, -1, down)
    cut(info, own_x, other_x, 1, up)
    cut(info, own, other, -2, across)


def left_side(info, a_ref, offset):
    columns = columns_of(info, offset)
    real, imag = a_ref[0, :, columns], a_ref[1, :, columns]
    return jnp.concatenate(
        [jnp.concatenate([real, -imag], axis=1), jnp.concatenate([imag, real], axis=1)], axis=0
    )


def products_kernel(offsets, info, a_ref, *refs):
    count = len(offsets)
    own, other, out = refs[:count], refs[count : 2 * count], refs[-1]
    total = refs[2 * count][...] if len(refs) > 2 * count + 1 else None
    for offset, one, two in zip(offsets, own, other):
        block = jnp.concatenate([whole(info, one, two, info[3], part) for part in range(2)], axis=0)
        term = jnp.dot(left_side(info, a_ref, offset), block, preferred_element_type=F32)
        total = term if total is None else total + term
    out[...] = total


def crossed_block(real, imag, drhs):
    block = jnp.dot(real, drhs[0:1024, :], preferred_element_type=F32)
    block += jnp.dot(imag, drhs[1024:2048, :], preferred_element_type=F32)
    turned = jnp.concatenate([block[:, :128].T, block[:, 128:].T], axis=0)
    return turned.astype(BF16)


OFFSETS = (0, 1, -1, 2, -2, 3, -3, 4)


def crossed_kernel(info, near, middle, down, up, across, *refs):
    own, other, drhs, crossed = refs[0:7], refs[7:14], refs[14], refs[15]
    slices = [near.at[0], near.at[1], near.at[2], middle.at[0], middle.at[1], down, up, across]
    for offset, piece in zip(OFFSETS, slices):
        top = pl.multiple_of(place_of(info, offset) * 128, 128)
        real, imag = piece[0], piece[1]
        drhs[pl.ds(top, 128), 0:128] = real
        drhs[pl.ds(top, 128), 128:256] = imag
        drhs[pl.ds(1024 + top, 128), 0:128] = -imag
        drhs[pl.ds(1024 + top, 128), 128:256] = real
    for offset, one, two in zip(OFFSETS, own, other):
        real, imag = (whole(info, one, two, info[4], part) for part in range(2))
        crossed[:, columns_of(info, offset)] = crossed_block(real, imag, drhs)


def last_kernel(info, a_ref, own, other, acc, drhs, crossed, keep, send, trace, turned):
    def parts(momentum):
        return [whole(info, own, other, momentum, part) for part in range(2)]

    block = jnp.concatenate(parts(info[3]), axis=0)
    product = acc[...] + jnp.dot(left_side(info, a_ref, 4), block, preferred_element_type=F32)
    rounded = product.astype(BF16)
    for part in range(2):
        low, high = rounded[part * 128 : part * 128 + 64], rounded[part * 128 + 64 : part * 128 + 128]
        keep[part], send[part] = halves(info, low, high)
    real, imag = parts(info[4])
    turned[...] = crossed[...]
    turned[:, columns_of(info, 4)] = crossed_block(real, imag, drhs)
    p_re, p_im = rounded[:128].astype(F32), rounded[128:].astype(F32)
    c_re, c_im = turned[:128, :].astype(F32), turned[128:, :].astype(F32)
    re = jnp.sum(p_re * c_re - p_im * c_im, axis=0, keepdims=True)
    im = jnp.sum(p_re * c_im + p_im * c_re, axis=0, keepdims=True)
    re = jnp.sum(re, axis=1, keepdims=True)
    im = jnp.sum(im, axis=1, keepdims=True)
    lane = lax.broadcasted_iota(jnp.int32, (1, 128), 1)
    trace[...] = jnp.where(lane == 2 * info[0], re, jnp.where(lane == 2 * info[0] + 1, im, 0.0))


def shards(fields, mom_table):
    rows = fields[:, 0]
    tm, row = lax.axis_index("tm"), lax.axis_index("row")
    core, place, half = tm % 2, row // 2, row % 2
    momenta = lax.dynamic_index_in_dim(mom_table, core, 0, keepdims=False)[0]
    info = jnp.concatenate([jnp.stack([place, core]), momenta])
    wall = lax.optimization_barrier
    block_of_products = jax.ShapeDtypeStruct((256, 1024), F32)

    p1, q1, own = moved(rows, to_hub(0, 1)), moved(rows, to_hub(1, 1)), moved(rows, to_hub(0, 0))

    p2, p1x = moved(p1, onward), moved(p1, other_core)
    q2, q1x = moved(q1, onward), moved(q1, other_core)
    ownx = moved(own, other_core)
    first_three = [own, p1, q1x, ownx, q1, p1x]
    a = call(first_cut_kernel, info, [own, ownx], jax.ShapeDtypeStruct((2, 128, 1024), BF16), 1)
    near = call(near_kernel, info, first_three, jax.ShapeDtypeStruct((3, 2, 128, 128), BF16), 1)
    q2, near, a = wall((q2, near, a))

    a, near = moved(a, hub_ahead(0)), moved(near, hub_ahead(0))
    p3, p2x = moved(p2, onward), moved(p2, other_core)
    q3, q2x = moved(q2, onward), moved(q2, other_core)
    next_two = [p2, q2x, q2, p2x]
    middle, down, up, across = call(
        middle_kernel,
        info,
        next_two,
        (jax.ShapeDtypeStruct((2, 2, 128, 128), BF16), SLICES, SLICES, SLICES),
        1,
    )
    q3, near, a, middle, down, up, across = wall((q3, near, a, middle, down, up, across))

    middle, down = moved(middle, hub_ahead(0)), moved(down, hub_ahead(1))
    up, across = moved(up, hub_ahead(-1)), moved(across, hub_ahead(2))
    p4, p3x = moved(p3, onward), moved(p3, other_core)
    q3x = moved(q3, other_core)
    acc = call(
        lambda *refs: products_kernel(OFFSETS[:5], *refs),
        info,
        [a] + first_three[:3] + next_two[:2] + first_three[3:] + next_two[2:],
        block_of_products,
        1,
    )
    p4, acc, middle, down, up, across = wall((p4, acc, middle, down, up, across))

    p4x = moved(p4, other_core)
    last_two = [p3, q3x, q3, p3x]
    acc = call(
        lambda *refs: products_kernel(OFFSETS[5:7], *refs), info, [a] + last_two + [acc], block_of_products, 1
    )
    drhs, crossed = call(
        crossed_kernel,
        info,
        [near, middle, down, up, across]
        + first_three[:3]
        + next_two[:2]
        + last_two[:2]
        + first_three[3:]
        + next_two[2:]
        + last_two[2:],
        (jax.ShapeDtypeStruct((2048, 256), BF16), jax.ShapeDtypeStruct((256, 1024), BF16)),
        1,
    )
    half_block = jax.ShapeDtypeStruct((2, 64, 1024), BF16)
    keep, send, trace = call(
        last_kernel,
        info,
        [a, p4, p4x, acc, drhs, crossed],
        (half_block, half_block, jax.ShapeDtypeStruct((1, 128), F32)),
        1,
        [pltpu.VMEM((256, 1024), BF16)],
    )

    below, above = moved(trace, along(1)), moved(trace, along(-1))
    kept, sent = moved(keep, from_hub(0)), moved(send, from_hub(1))
    two, three = wall((trace + above, below + trace + above))
    below, above = moved(two, along(3)), moved(three, along(-3))
    trace, kept, sent = wall((below + three + above, kept, sent))
    first, second = moved(trace, from_hub(0)), moved(trace, from_hub(1))
    products = jnp.where(half == 0, jnp.stack([kept, sent]), jnp.stack([sent, kept]))[:, None, None]
    both = jnp.where(half == 0, jnp.concatenate([first, second]), jnp.concatenate([second, first]))
    correlator = jnp.sum(both[:, :16].reshape(2, 8, 2), axis=1)[:, None, None, :] / F32(1024)
    return products, correlator


def solution(mesh):
    return jax.shard_map(
        shards,
        mesh=mesh,
        in_specs=(P(None, "tm", None, "row", None), P()),
        out_specs=(P(None, None, "tm", None, "row", None), P(None, None, "tm", None)),
        check_vma=False,
    )
```

```python
import jax
import jax.numpy as jnp
from jax import lax
from jax.experimental import pallas as pl
from jax.experimental.pallas import tpu as pltpu
from jax.sharding import PartitionSpec as P

BOTH = ("tm", "row")
BF16 = jnp.bfloat16
F32 = jnp.float32


def hub_of(s):
    m, odd = divmod(s % 16, 2)
    low, x = divmod(m, 4)
    return (1 - low) * 4 + x, odd ^ low


SERVED = {hub_of(s): s for s in range(16)}


def moved(block, route):
    def index_of(m, c, z, h):
        return ((m % 8) * 2 + c) * 16 + (z % 8) * 2 + h

    places = [(m, c, z, h) for m in range(8) for c in range(2) for z in range(8) for h in range(2)]
    return lax.ppermute(block, BOTH, [(index_of(*at), index_of(*route(*at))) for at in places])


def along(step):
    return lambda m, c, z, h: (m, c, z + step, h)


def onward(m, c, z, h):
    return (m, c, z + (1 if c == 0 else -1), h)


def other_core(m, c, z, h):
    return (m, 1 - c, z, h)


def to_hub(m, c, z, h):
    column, half = hub_of(2 * m + c)
    return (column, h, z, half)


def hub_ahead(turn, step):
    def route(m, c, z, h):
        r = c ^ turn
        column, half = hub_of(SERVED[m, h] + 1 + r)
        return (column, r, z + (step if r == 0 else -step), half)

    return route


def from_hub(turn):
    def route(m, c, z, h):
        t = (SERVED[m, h] - 1 - c) % 16
        return (t // 2, t % 2, z, c ^ turn)

    return route


VMEM = pl.BlockSpec(memory_space=pltpu.VMEM)
SMEM = pl.BlockSpec(memory_space=pltpu.SMEM)
SLICES = jax.ShapeDtypeStruct((2, 128, 128), BF16)


def call(kernel, info, arrays, out_shape, flops, scratch=()):
    outs = jax.tree.map(lambda _: VMEM, out_shape)
    return pl.pallas_call(
        kernel,
        out_shape=out_shape,
        in_specs=[SMEM] + [VMEM] * len(arrays),
        out_specs=outs,
        scratch_shapes=scratch,
        compiler_params=pltpu.CompilerParams(vmem_limit_bytes=24 * 1024 * 1024),
        cost_estimate=pl.CostEstimate(flops=flops, bytes_accessed=1 << 20, transcendentals=0),
    )(info, *arrays)


def place_of(info, offset):
    return lax.rem(info[0] + jnp.where(info[1] == 0, 8 - offset, 8 + offset), 8)


def columns_of(info, offset):
    return pl.ds(pl.multiple_of(place_of(info, offset) * 128, 128), 128)


def halves(info, own, other):
    first = jnp.where(info[1] == 0, own, other)
    second = jnp.where(info[1] == 0, other, own)
    return first, second


def whole(info, own_ref, other_ref, momentum, part):
    return jnp.concatenate(halves(info, own_ref[momentum, part], other_ref[momentum, part]), axis=0)


def cut(info, own_ref, other_ref, offset, out, momentum=5):
    columns = columns_of(info, offset)
    for part in range(2):
        first, second = halves(
            info, own_ref[info[momentum], part, :, columns], other_ref[info[momentum], part, :, columns]
        )
        out[part, 0:64] = first
        out[part, 64:128] = second


def first_cut_kernel(info, own, other, a):
    for part in range(2):
        a[part] = whole(info, own, other, info[2], part)


def near_kernel(info, *refs):
    for k in range(3):
        cut(info, refs[k], refs[3 + k], 0, refs[-1].at[k])


def across_kernel(info, own, other, out):
    cut(info, own, other, -2, out)


def late_kernel(info, own_2, own_3, other_2, other_3, here, there):
    for k, (own, other) in enumerate([(own_2, other_2), (own_3, other_3)]):
        cut(info, own, other, 0, here.at[k])
        cut(info, own, other, 0, there.at[k], momentum=6)


def left_side(info, a_ref, offset):
    columns = columns_of(info, offset)
    real, imag = a_ref[0, :, columns], a_ref[1, :, columns]
    return jnp.concatenate(
        [jnp.concatenate([real, -imag], axis=1), jnp.concatenate([imag, real], axis=1)], axis=0
    )


def products_kernel(offsets, info, a_ref, *refs):
    count = len(offsets)
    own, other, out = refs[:count], refs[count : 2 * count], refs[-1]
    total = refs[2 * count][...] if len(refs) > 2 * count + 1 else None
    for offset, one, two in zip(offsets, own, other):
        block = jnp.concatenate([whole(info, one, two, info[3], part) for part in range(2)], axis=0)
        term = jnp.dot(left_side(info, a_ref, offset), block, preferred_element_type=F32)
        total = term if total is None else total + term
    out[...] = total


OFFSETS = (0, 1, -1, 2, -2, 3, -3, 4)


def crossed_sum(info, own, other, slices):
    total = None
    for offset, piece in slices:
        columns = columns_of(info, offset)
        left = []
        for one, two in zip(own, other):
            parts = [halves(info, one[info[4], part, :, columns], two[info[4], part, :, columns]) for part in range(2)]
            left += [jnp.concatenate([parts[0][k], parts[1][k]], axis=1) for k in range(2)]
        real, imag = piece[0], piece[1]
        right = jnp.concatenate(
            [jnp.concatenate([real, imag], axis=1), jnp.concatenate([-imag, real], axis=1)], axis=0
        )
        term = jnp.dot(jnp.concatenate(left, axis=0), right, preferred_element_type=F32)
        total = term if total is None else total + term
    return total


def crossed_kernel(info, near, across, here, there, *refs):
    slices = [(0, near.at[0]), (1, near.at[1]), (-1, near.at[2]), (4, across)]
    slices += [(2, here.at[0]), (-2, there.at[0]), (3, here.at[1]), (-3, there.at[1])]
    total = crossed_sum(info, refs[0:7], refs[7:14], slices)
    for k, offset in enumerate(OFFSETS[:7]):
        refs[14][columns_of(info, offset), :] = total[128 * k : 128 * k + 128].astype(BF16)
    refs[14][columns_of(info, 4), :] = jnp.zeros((128, 256), BF16)


def last_kernel(info, a_ref, acc, near, across, here, there, early, own, other, keep, send, trace, crossed):
    block = jnp.concatenate([whole(info, own, other, info[3], part) for part in range(2)], axis=0)
    product = acc[...] + jnp.dot(left_side(info, a_ref, 4), block, preferred_element_type=F32)
    rounded = product.astype(BF16)
    for part in range(2):
        low, high = rounded[part * 128 : part * 128 + 64], rounded[part * 128 + 64 : part * 128 + 128]
        keep[part], send[part] = halves(info, low, high)
    slices = [(0, near.at[0]), (1, near.at[1]), (-1, near.at[2]), (4, across)]
    slices += [(2, here.at[0]), (-2, there.at[0]), (3, here.at[1]), (-3, there.at[1])]
    crossed[...] = early[...]
    crossed[columns_of(info, 4), :] = crossed_sum(info, [own], [other], slices).astype(BF16)
    square = jnp.dot(rounded, crossed[...], preferred_element_type=F32)
    row = lax.broadcasted_iota(jnp.int32, (128, 128), 0)
    column = lax.broadcasted_iota(jnp.int32, (128, 128), 1)
    re = jnp.where(row == column, square[:128, :128] - square[128:, 128:], 0.0)
    im = jnp.where(row == column, square[:128, 128:] + square[128:, :128], 0.0)
    re = jnp.sum(jnp.sum(re, axis=0, keepdims=True), axis=1, keepdims=True)
    im = jnp.sum(jnp.sum(im, axis=0, keepdims=True), axis=1, keepdims=True)
    lane = lax.broadcasted_iota(jnp.int32, (1, 128), 1)
    trace[...] = jnp.where(lane == 2 * info[0], re, jnp.where(lane == 2 * info[0] + 1, im, 0.0))


def shards(fields, mom_table):
    rows = fields[:, 0]
    tm, row = lax.axis_index("tm"), lax.axis_index("row")
    core, place, half = tm % 2, row // 2, row % 2
    momenta = lax.dynamic_index_in_dim(mom_table, core, 0, keepdims=False)[0]
    others = lax.dynamic_index_in_dim(mom_table, 1 - core, 0, keepdims=False)[0]
    info = jnp.concatenate([jnp.stack([place, core]), momenta, others[3:]])
    wall = lax.optimization_barrier
    block_of_products = jax.ShapeDtypeStruct((256, 1024), F32)

    own = moved(rows, to_hub)

    ownx, p1 = moved(own, other_core), moved(own, onward)
    q1 = moved(ownx, onward)
    a = call(first_cut_kernel, info, [own, ownx], jax.ShapeDtypeStruct((2, 128, 1024), BF16), 1)
    a = moved(a, hub_ahead(0, 0))

    p2, p1x = moved(p1, onward), moved(p1, other_core)
    q2, q1x = moved(q1, onward), moved(q1, other_core)
    three, three_x = [own, p1, q1x], [ownx, q1, p1x]
    near = call(near_kernel, info, three + three_x, jax.ShapeDtypeStruct((3, 2, 128, 128), BF16), 1)
    p2, a = wall((p2, a))
    q2, near = wall((q2, near))

    p3, p2x = moved(p2, onward), moved(p2, other_core)
    q3, q2x = moved(q2, onward), moved(q2, other_core)
    across = call(across_kernel, info, [p2, q2], SLICES, 1)
    five, five_x = three + [p2, q2x], three_x + [q2, p2x]
    acc = call(lambda *refs: products_kernel(OFFSETS[:5], *refs), info, [a] + five + five_x, block_of_products, 1)
    p3, near = wall((p3, near))

    near = moved(near, hub_ahead(0, 0))
    p4, p3x = moved(p3, onward), moved(p3, other_core)
    q3, across, acc = wall((q3, across, acc))

    pair = jax.ShapeDtypeStruct((2, 2, 128, 128), BF16)
    here, there = call(late_kernel, info, [p2, p3, q2, q3], (pair, pair), 1)
    here, there, across = moved(here, hub_ahead(0, 0)), moved(there, hub_ahead(1, 0)), moved(across, hub_ahead(0, 2))
    p4, near, across, here, there = wall((p4, near, across, here, there))

    p4x, q3x = moved(p4, other_core), moved(q3, other_core)
    two, two_x = [p3, q3x], [q3, p3x]
    acc = call(
        lambda *refs: products_kernel(OFFSETS[5:7], *refs), info, [a] + two + two_x + [acc], block_of_products, 1
    )
    slices = [near, across, here, there]
    early = call(
        crossed_kernel, info, slices + five + two + five_x + two_x, jax.ShapeDtypeStruct((1024, 256), BF16), 1
    )
    half_block = jax.ShapeDtypeStruct((2, 64, 1024), BF16)
    keep, send, trace = call(
        last_kernel,
        info,
        [a, acc] + slices + [early, p4, p4x],
        (half_block, half_block, jax.ShapeDtypeStruct((1, 128), F32)),
        1,
        [pltpu.VMEM((1024, 256), BF16)],
    )

    below, above = moved(trace, along(1)), moved(trace, along(-1))
    kept, sent = moved(keep, from_hub(0)), moved(send, from_hub(1))
    two, three = wall((trace + above, below + trace + above))
    below, above = moved(two, along(3)), moved(three, along(-3))
    trace, kept, sent = wall((below + three + above, kept, sent))
    first, second = moved(trace, from_hub(0)), moved(trace, from_hub(1))
    products = jnp.where(half == 0, jnp.stack([kept, sent]), jnp.stack([sent, kept]))[:, None, None]
    both = jnp.where(half == 0, jnp.concatenate([first, second]), jnp.concatenate([second, first]))
    correlator = jnp.sum(both[:, :16].reshape(2, 8, 2), axis=1)[:, None, None, :] / F32(1024)
    return products, correlator


def solution(mesh):
    return jax.shard_map(
        shards,
        mesh=mesh,
        in_specs=(P(None, "tm", None, "row", None), P()),
        out_specs=(P(None, None, "tm", None, "row", None), P(None, None, "tm", None)),
        check_vma=False,
    )
```

```python
import jax
import jax.numpy as jnp
from jax import lax
from jax.experimental import pallas as pl
from jax.experimental.pallas import tpu as pltpu
from jax.sharding import PartitionSpec as P

BOTH = ("tm", "row")
BF16 = jnp.bfloat16
F32 = jnp.float32


def hub_of(s):
    m, odd = divmod(s % 16, 2)
    low, x = divmod(m, 4)
    return (1 - low) * 4 + x, odd ^ low


SERVED = {hub_of(s): s for s in range(16)}


def moved(block, route):
    def index_of(m, c, z, h):
        return ((m % 8) * 2 + c) * 16 + (z % 8) * 2 + h

    places = [(m, c, z, h) for m in range(8) for c in range(2) for z in range(8) for h in range(2)]
    return lax.ppermute(block, BOTH, [(index_of(*at), index_of(*route(*at))) for at in places])


def along(step):
    return lambda m, c, z, h: (m, c, z + step, h)


def onward(m, c, z, h):
    return (m, c, z + (1 if c == 0 else -1), h)


def other_core(m, c, z, h):
    return (m, 1 - c, z, h)


def to_hub(m, c, z, h):
    column, half = hub_of(2 * m + c)
    return (column, h, z, half)


def hub_ahead(turn, step):
    def route(m, c, z, h):
        r = c ^ turn
        column, half = hub_of(SERVED[m, h] + 1 + r)
        return (column, r, z + (step if r == 0 else -step), half)

    return route


def from_hub(turn):
    def route(m, c, z, h):
        t = (SERVED[m, h] - 1 - c) % 16
        return (t // 2, t % 2, z, c ^ turn)

    return route


WEIGHT = 3_000_000_000
SMALL = 1_000_000_000

VMEM = pl.BlockSpec(memory_space=pltpu.VMEM)
SMEM = pl.BlockSpec(memory_space=pltpu.SMEM)
SLICES = jax.ShapeDtypeStruct((2, 128, 128), BF16)


def call(kernel, info, arrays, out_shape, flops, scratch=()):
    outs = jax.tree.map(lambda _: VMEM, out_shape)
    return pl.pallas_call(
        kernel,
        out_shape=out_shape,
        in_specs=[SMEM] + [VMEM] * len(arrays),
        out_specs=outs,
        scratch_shapes=scratch,
        compiler_params=pltpu.CompilerParams(vmem_limit_bytes=24 * 1024 * 1024),
        cost_estimate=pl.CostEstimate(flops=flops, bytes_accessed=1 << 20, transcendentals=0),
    )(info, *arrays)


def place_of(info, offset):
    return lax.rem(info[0] + jnp.where(info[1] == 0, 8 - offset, 8 + offset), 8)


def columns_of(info, offset):
    return pl.ds(pl.multiple_of(place_of(info, offset) * 128, 128), 128)


def halves(info, own, other):
    first = jnp.where(info[1] == 0, own, other)
    second = jnp.where(info[1] == 0, other, own)
    return first, second


def whole(info, own_ref, other_ref, momentum, part):
    return jnp.concatenate(halves(info, own_ref[momentum, part], other_ref[momentum, part]), axis=0)


def cut(info, own_ref, other_ref, offset, out, momentum=5):
    columns = columns_of(info, offset)
    for part in range(2):
        first, second = halves(
            info, own_ref[info[momentum], part, :, columns], other_ref[info[momentum], part, :, columns]
        )
        out[part, 0:64] = first
        out[part, 64:128] = second


def first_cut_kernel(info, own, other, a):
    for part in range(2):
        a[part] = whole(info, own, other, info[2], part)


def near_kernel(info, *refs):
    for k in range(3):
        cut(info, refs[k], refs[3 + k], 0, refs[-1].at[k])


def across_kernel(info, own, other, out):
    cut(info, own, other, -2, out)


def late_kernel(info, own_2, own_3, other_2, other_3, here, there):
    for k, (own, other) in enumerate([(own_2, other_2), (own_3, other_3)]):
        cut(info, own, other, 0, here.at[k])
        cut(info, own, other, 0, there.at[k], momentum=6)


def left_side(info, a_ref, offset):
    columns = columns_of(info, offset)
    real, imag = a_ref[0, :, columns], a_ref[1, :, columns]
    return jnp.concatenate(
        [jnp.concatenate([real, -imag], axis=1), jnp.concatenate([imag, real], axis=1)], axis=0
    )


def products_kernel(offsets, info, a_ref, *refs):
    count = len(offsets)
    own, other, out = refs[:count], refs[count : 2 * count], refs[-1]
    total = refs[2 * count][...] if len(refs) > 2 * count + 1 else None
    for offset, one, two in zip(offsets, own, other):
        block = jnp.concatenate([whole(info, one, two, info[3], part) for part in range(2)], axis=0)
        term = jnp.dot(left_side(info, a_ref, offset), block, preferred_element_type=F32)
        total = term if total is None else total + term
    out[...] = total


OFFSETS = (0, 1, -1, 2, -2, 3, -3, 4)


def crossed_sum(info, own, other, slices):
    total = None
    for offset, piece in slices:
        columns = columns_of(info, offset)
        left = []
        for one, two in zip(own, other):
            parts = [halves(info, one[info[4], part, :, columns], two[info[4], part, :, columns]) for part in range(2)]
            left += [jnp.concatenate([parts[0][k], parts[1][k]], axis=1) for k in range(2)]
        real, imag = piece[0], piece[1]
        right = jnp.concatenate(
            [jnp.concatenate([real, imag], axis=1), jnp.concatenate([-imag, real], axis=1)], axis=0
        )
        term = jnp.dot(jnp.concatenate(left, axis=0), right, preferred_element_type=F32)
        total = term if total is None else total + term
    return total


def first_slices(near, across):
    return [(0, near.at[0]), (1, near.at[1]), (-1, near.at[2]), (4, across)]


def last_slices(here, there):
    return [(2, here.at[0]), (-2, there.at[0]), (3, here.at[1]), (-3, there.at[1])]


def early_kernel(info, near, across, *refs):
    refs[10][...] = crossed_sum(info, refs[0:5], refs[5:10], first_slices(near, across))


def crossed_kernel(info, near, across, here, there, early, *refs):
    own, other, out = refs[0:7], refs[7:14], refs[14]
    later = crossed_sum(info, own[5:], other[5:], first_slices(near, across))
    total = jnp.concatenate([early[...], later], axis=0) + crossed_sum(info, own, other, last_slices(here, there))
    for k, offset in enumerate(OFFSETS[:7]):
        out[columns_of(info, offset), :] = total[128 * k : 128 * k + 128].astype(BF16)
    out[columns_of(info, 4), :] = jnp.zeros((128, 256), BF16)


def last_kernel(info, a_ref, acc, near, across, here, there, early, own, other, keep, send, trace, crossed):
    block = jnp.concatenate([whole(info, own, other, info[3], part) for part in range(2)], axis=0)
    product = acc[...] + jnp.dot(left_side(info, a_ref, 4), block, preferred_element_type=F32)
    rounded = product.astype(BF16)
    for part in range(2):
        low, high = rounded[part * 128 : part * 128 + 64], rounded[part * 128 + 64 : part * 128 + 128]
        keep[part], send[part] = halves(info, low, high)
    slices = first_slices(near, across) + last_slices(here, there)
    crossed[...] = early[...]
    crossed[columns_of(info, 4), :] = crossed_sum(info, [own], [other], slices).astype(BF16)
    square = jnp.dot(rounded, crossed[...], preferred_element_type=F32)
    row = lax.broadcasted_iota(jnp.int32, (128, 128), 0)
    column = lax.broadcasted_iota(jnp.int32, (128, 128), 1)
    re = jnp.where(row == column, square[:128, :128] - square[128:, 128:], 0.0)
    im = jnp.where(row == column, square[:128, 128:] + square[128:, :128], 0.0)
    re = jnp.sum(jnp.sum(re, axis=0, keepdims=True), axis=1, keepdims=True)
    im = jnp.sum(jnp.sum(im, axis=0, keepdims=True), axis=1, keepdims=True)
    lane = lax.broadcasted_iota(jnp.int32, (1, 128), 1)
    trace[...] = jnp.where(lane == 2 * info[0], re, jnp.where(lane == 2 * info[0] + 1, im, 0.0))


def shards(fields, mom_table):
    rows = fields[:, 0]
    tm, row = lax.axis_index("tm"), lax.axis_index("row")
    core, place, half = tm % 2, row // 2, row % 2
    momenta = lax.dynamic_index_in_dim(mom_table, core, 0, keepdims=False)[0]
    others = lax.dynamic_index_in_dim(mom_table, 1 - core, 0, keepdims=False)[0]
    info = jnp.concatenate([jnp.stack([place, core]), momenta, others[3:]])
    wall = lax.optimization_barrier
    block_of_products = jax.ShapeDtypeStruct((256, 1024), F32)

    own = moved(rows, to_hub)

    ownx, p1 = moved(own, other_core), moved(own, onward)
    q1 = moved(ownx, onward)
    a = call(first_cut_kernel, info, [own, ownx], jax.ShapeDtypeStruct((2, 128, 1024), BF16), 1)
    a = moved(a, hub_ahead(0, 0))

    p2, p1x = moved(p1, onward), moved(p1, other_core)
    q2, q1x = moved(q1, onward), moved(q1, other_core)
    three, three_x = [own, p1, q1x], [ownx, q1, p1x]
    near = call(near_kernel, info, three + three_x, jax.ShapeDtypeStruct((3, 2, 128, 128), BF16), 1)
    acc = call(lambda *refs: products_kernel(OFFSETS[:1], *refs), info, [a, own, ownx], block_of_products, WEIGHT)
    p2, a, acc = wall((p2, a, acc))
    q2, near = wall((q2, near))

    p3, p2x = moved(p2, onward), moved(p2, other_core)
    q3, q2x = moved(q2, onward), moved(q2, other_core)
    across = call(across_kernel, info, [p2, q2], SLICES, 1)
    five, five_x = three + [p2, q2x], three_x + [q2, p2x]
    acc = call(
        lambda *refs: products_kernel(OFFSETS[1:5], *refs), info, [a] + five[1:] + five_x[1:] + [acc], block_of_products, 1
    )
    p3, near = wall((p3, near))

    near = moved(near, hub_ahead(0, 0))
    p4, p3x = moved(p3, onward), moved(p3, other_core)
    q3, acc = wall((q3, acc))

    pair = jax.ShapeDtypeStruct((2, 2, 128, 128), BF16)
    here, there = call(late_kernel, info, [p2, p3, q2, q3], (pair, pair), 1)
    here, there, across = moved(here, hub_ahead(0, 0)), moved(there, hub_ahead(1, 0)), moved(across, hub_ahead(0, 2))
    early = call(early_kernel, info, [near, across] + five + five_x, jax.ShapeDtypeStruct((640, 256), F32), SMALL)
    p4, near, across, here, there, early = wall((p4, near, across, here, there, early))

    p4x, q3x = moved(p4, other_core), moved(q3, other_core)
    two, two_x = [p3, q3x], [q3, p3x]
    acc = call(
        lambda *refs: products_kernel(OFFSETS[5:7], *refs), info, [a] + two + two_x + [acc], block_of_products, 1
    )
    slices = [near, across, here, there]
    early = call(
        crossed_kernel, info, slices + [early] + five + two + five_x + two_x, jax.ShapeDtypeStruct((1024, 256), BF16), 1
    )
    half_block = jax.ShapeDtypeStruct((2, 64, 1024), BF16)
    keep, send, trace = call(
        last_kernel,
        info,
        [a, acc] + slices + [early, p4, p4x],
        (half_block, half_block, jax.ShapeDtypeStruct((1, 128), F32)),
        1,
        [pltpu.VMEM((1024, 256), BF16)],
    )

    below, above = moved(trace, along(1)), moved(trace, along(-1))
    kept, sent = moved(keep, from_hub(0)), moved(send, from_hub(1))
    two, three = wall((trace + above, below + trace + above))
    below, above = moved(two, along(3)), moved(three, along(-3))
    trace, kept, sent = wall((below + three + above, kept, sent))
    first, second = moved(trace, from_hub(0)), moved(trace, from_hub(1))
    products = jnp.where(half == 0, jnp.stack([kept, sent]), jnp.stack([sent, kept]))[:, None, None]
    both = jnp.where(half == 0, jnp.concatenate([first, second]), jnp.concatenate([second, first]))
    correlator = jnp.sum(both[:, :16].reshape(2, 8, 2), axis=1)[:, None, None, :] / F32(1024)
    return products, correlator


def solution(mesh):
    return jax.shard_map(
        shards,
        mesh=mesh,
        in_specs=(P(None, "tm", None, "row", None), P()),
        out_specs=(P(None, None, "tm", None, "row", None), P(None, None, "tm", None)),
        check_vma=False,
    )
```

```python
import jax
import jax.numpy as jnp
from jax import lax
from jax.experimental import pallas as pl
from jax.experimental.pallas import tpu as pltpu
from jax.sharding import PartitionSpec as P

BOTH = ("tm", "row")
BF16 = jnp.bfloat16
F32 = jnp.float32


def hub_of(s):
    m, odd = divmod(s % 16, 2)
    low, x = divmod(m, 4)
    return (1 - low) * 4 + x, odd ^ low


SERVED = {hub_of(s): s for s in range(16)}


def moved(block, route):
    def index_of(m, c, z, h):
        return ((m % 8) * 2 + c) * 16 + (z % 8) * 2 + h

    places = [(m, c, z, h) for m in range(8) for c in range(2) for z in range(8) for h in range(2)]
    return lax.ppermute(block, BOTH, [(index_of(*at), index_of(*route(*at))) for at in places])


def along(step):
    return lambda m, c, z, h: (m, c, z + step, h)


def onward(m, c, z, h):
    return (m, c, z + (1 if c == 0 else -1), h)


def other_core(m, c, z, h):
    return (m, 1 - c, z, h)


def to_hub(m, c, z, h):
    column, half = hub_of(2 * m + c)
    return (column, h, z, half)


def hub_ahead(step):
    def route(m, c, z, h):
        column, half = hub_of(SERVED[m, h] + 1 + c)
        return (column, c, z + (step if c == 0 else -step), half)

    return route


def from_hub(turn):
    def route(m, c, z, h):
        t = (SERVED[m, h] - 1 - c) % 16
        return (t // 2, t % 2, z, c ^ turn)

    return route


WEIGHT = 3_000_000_000

VMEM = pl.BlockSpec(memory_space=pltpu.VMEM)
SMEM = pl.BlockSpec(memory_space=pltpu.SMEM)
SLICES = jax.ShapeDtypeStruct((2, 128, 128), BF16)


def call(kernel, info, arrays, out_shape, flops, scratch=()):
    outs = jax.tree.map(lambda _: VMEM, out_shape)
    return pl.pallas_call(
        kernel,
        out_shape=out_shape,
        in_specs=[SMEM] + [VMEM] * len(arrays),
        out_specs=outs,
        scratch_shapes=scratch,
        compiler_params=pltpu.CompilerParams(vmem_limit_bytes=24 * 1024 * 1024),
        cost_estimate=pl.CostEstimate(flops=flops, bytes_accessed=1 << 20, transcendentals=0),
    )(info, *arrays)


def place_of(info, offset):
    return lax.rem(info[0] + jnp.where(info[1] == 0, 8 - offset, 8 + offset), 8)


def columns_of(info, offset):
    return pl.ds(pl.multiple_of(place_of(info, offset) * 128, 128), 128)


def halves(info, own, other):
    first = jnp.where(info[1] == 0, own, other)
    second = jnp.where(info[1] == 0, other, own)
    return first, second


def whole(info, own_ref, other_ref, momentum, part):
    return jnp.concatenate(halves(info, own_ref[momentum, part], other_ref[momentum, part]), axis=0)


def cut(info, own_ref, other_ref, offset, out):
    columns = columns_of(info, offset)
    for part in range(2):
        first, second = halves(info, own_ref[info[5], part, :, columns], other_ref[info[5], part, :, columns])
        out[part] = jnp.concatenate([first, second], axis=0).T


def first_cut_kernel(info, own, other, a):
    for part in range(2):
        a[part] = whole(info, own, other, info[2], part)


def cut_kernel(info, *refs):
    count = len(refs) // 2
    for k in range(count):
        cut(info, refs[k], refs[count + k], 0, refs[-1].at[k])


def across_kernel(info, own, other, out):
    cut(info, own, other, -2, out)


def left_side(info, a_ref, offset):
    columns = columns_of(info, offset)
    real, imag = a_ref[0, :, columns], a_ref[1, :, columns]
    return jnp.concatenate(
        [jnp.concatenate([real, -imag], axis=1), jnp.concatenate([imag, real], axis=1)], axis=0
    )


def products_kernel(offsets, info, a_ref, *refs):
    count = len(offsets)
    own, other, out = refs[:count], refs[count : 2 * count], refs[-1]
    total = refs[2 * count][...] if len(refs) > 2 * count + 1 else None
    for offset, one, two in zip(offsets, own, other):
        block = jnp.concatenate([whole(info, one, two, info[3], part) for part in range(2)], axis=0)
        term = jnp.dot(left_side(info, a_ref, offset), block, preferred_element_type=F32)
        total = term if total is None else total + term
    out[...] = total


OFFSETS = (0, 1, -1, 2, -2, 3, -3, 4)


def last_kernel(info, a_ref, acc, *refs):
    own, other = refs[0:8], refs[8:16]
    keep, send, out, rounded_ref = refs[16:20]
    block = jnp.concatenate([whole(info, own[7], other[7], info[3], part) for part in range(2)], axis=0)
    product = acc[...] + jnp.dot(left_side(info, a_ref, 4), block, preferred_element_type=F32)
    rounded = product.astype(BF16)
    for part in range(2):
        rounded_ref[part] = rounded[part * 128 : part * 128 + 128]
        low, high = rounded[part * 128 : part * 128 + 64], rounded[part * 128 + 64 : part * 128 + 128]
        keep[part], send[part] = halves(info, low, high)
    total = None
    for offset, one, two in zip(OFFSETS, own, other):
        block = jnp.concatenate([whole(info, one, two, info[4], part) for part in range(2)], axis=0)
        term = jnp.dot(left_side(info, rounded_ref, offset), block, preferred_element_type=F32)
        total = term if total is None else total + term
    out[...] = total


def trace_kernel(info, product, near, late, across, trace):
    slices = [near.at[0], near.at[1], near.at[2], late.at[0], late.at[1], late.at[2], late.at[3], across]
    re = im = None
    for offset, piece in zip(OFFSETS, slices):
        columns = columns_of(info, offset)
        q_re, q_im = product[0:128, columns], product[128:256, columns]
        d_re, d_im = piece[0].astype(F32), piece[1].astype(F32)
        more_re, more_im = q_re * d_re - q_im * d_im, q_re * d_im + q_im * d_re
        re = more_re if re is None else re + more_re
        im = more_im if im is None else im + more_im
    re = jnp.sum(jnp.sum(re, axis=0, keepdims=True), axis=1, keepdims=True)
    im = jnp.sum(jnp.sum(im, axis=0, keepdims=True), axis=1, keepdims=True)
    lane = lax.broadcasted_iota(jnp.int32, (1, 128), 1)
    trace[...] = jnp.where(lane == 2 * info[0], re, jnp.where(lane == 2 * info[0] + 1, im, 0.0))


def shards(fields, mom_table):
    rows = fields[:, 0]
    tm, row = lax.axis_index("tm"), lax.axis_index("row")
    core, place, half = tm % 2, row // 2, row % 2
    momenta = lax.dynamic_index_in_dim(mom_table, core, 0, keepdims=False)[0]
    info = jnp.concatenate([jnp.stack([place, core]), momenta])
    wall = lax.optimization_barrier
    block_of_products = jax.ShapeDtypeStruct((256, 1024), F32)

    own = moved(rows, to_hub)

    ownx, p1 = moved(own, other_core), moved(own, onward)
    q1 = moved(ownx, onward)
    a = call(first_cut_kernel, info, [own, ownx], jax.ShapeDtypeStruct((2, 128, 1024), BF16), 1)
    a = moved(a, hub_ahead(0))

    p2, p1x = moved(p1, onward), moved(p1, other_core)
    q2, q1x = moved(q1, onward), moved(q1, other_core)
    three, three_x = [own, p1, q1x], [ownx, q1, p1x]
    near = call(cut_kernel, info, three + three_x, jax.ShapeDtypeStruct((3, 2, 128, 128), BF16), 1)
    acc = call(lambda *refs: products_kernel(OFFSETS[:1], *refs), info, [a, own, ownx], block_of_products, WEIGHT)
    p2, a, acc = wall((p2, a, acc))
    q2, near = wall((q2, near))

    p3, p2x = moved(p2, onward), moved(p2, other_core)
    q3, q2x = moved(q2, onward), moved(q2, other_core)
    across = call(across_kernel, info, [p2, q2], SLICES, 1)
    five, five_x = three + [p2, q2x], three_x + [q2, p2x]
    acc = call(
        lambda *refs: products_kernel(OFFSETS[1:5], *refs), info, [a] + five[1:] + five_x[1:] + [acc], block_of_products, 1
    )
    p3, near = wall((p3, near))

    near = moved(near, hub_ahead(0))
    p4, p3x = moved(p3, onward), moved(p3, other_core)
    q3, acc = wall((q3, acc))

    q3x = moved(q3, other_core)
    p4, near, across = wall((p4, near, across))

    p4x = moved(p4, other_core)
    across = moved(across, hub_ahead(2))
    two, two_x = [p3, q3x], [q3, p3x]
    four, four_x = five[3:] + two, five_x[3:] + two_x
    late = call(cut_kernel, info, four + four_x, jax.ShapeDtypeStruct((4, 2, 128, 128), BF16), 1)
    late = moved(late, hub_ahead(0))
    acc = call(
        lambda *refs: products_kernel(OFFSETS[5:7], *refs), info, [a] + two + two_x + [acc], block_of_products, 1
    )
    half_block = jax.ShapeDtypeStruct((2, 64, 1024), BF16)
    keep, send, product = call(
        last_kernel,
        info,
        [a, acc] + five + two + [p4] + five_x + two_x + [p4x],
        (half_block, half_block, block_of_products),
        WEIGHT,
        [pltpu.VMEM((2, 128, 1024), BF16)],
    )
    trace = call(trace_kernel, info, [product, near, late, across], jax.ShapeDtypeStruct((1, 128), F32), 1)

    below, above = moved(trace, along(1)), moved(trace, along(-1))
    kept, sent = moved(keep, from_hub(0)), moved(send, from_hub(1))
    two, three = wall((trace + above, below + trace + above))
    below, above = moved(two, along(3)), moved(three, along(-3))
    trace, kept, sent = wall((below + three + above, kept, sent))
    first, second = moved(trace, from_hub(0)), moved(trace, from_hub(1))
    products = jnp.where(half == 0, jnp.stack([kept, sent]), jnp.stack([sent, kept]))[:, None, None]
    both = jnp.where(half == 0, jnp.concatenate([first, second]), jnp.concatenate([second, first]))
    correlator = jnp.sum(both[:, :16].reshape(2, 8, 2), axis=1)[:, None, None, :] / F32(1024)
    return products, correlator


def solution(mesh):
    return jax.shard_map(
        shards,
        mesh=mesh,
        in_specs=(P(None, "tm", None, "row", None), P()),
        out_specs=(P(None, None, "tm", None, "row", None), P(None, None, "tm", None)),
        check_vma=False,
    )
```

```python
import jax
import jax.numpy as jnp
from jax import lax
from jax.experimental import pallas as pl
from jax.experimental.pallas import tpu as pltpu
from jax.sharding import PartitionSpec as P

BOTH = ("tm", "row")
BF16 = jnp.bfloat16
F32 = jnp.float32


def hub_of(s):
    m, odd = divmod(s % 16, 2)
    low, x = divmod(m, 4)
    return (1 - low) * 4 + x, odd ^ low


SERVED = {hub_of(s): s for s in range(16)}


def moved(block, route):
    def index_of(m, c, z, h):
        return ((m % 8) * 2 + c) * 16 + (z % 8) * 2 + h

    places = [(m, c, z, h) for m in range(8) for c in range(2) for z in range(8) for h in range(2)]
    return lax.ppermute(block, BOTH, [(index_of(*at), index_of(*route(*at))) for at in places])


def along(step):
    return lambda m, c, z, h: (m, c, z + step, h)


def onward(m, c, z, h):
    return (m, c, z + (1 if c == 0 else -1), h)


def other_core(m, c, z, h):
    return (m, 1 - c, z, h)


def to_hub(m, c, z, h):
    column, half = hub_of(2 * m + c)
    return (column, h, z, half)


def hub_ahead(step):
    def route(m, c, z, h):
        column, half = hub_of(SERVED[m, h] + 1 + c)
        return (column, c, z + (step if c == 0 else -step), half)

    return route


def from_hub(turn):
    def route(m, c, z, h):
        t = (SERVED[m, h] - 1 - c) % 16
        return (t // 2, t % 2, z, c ^ turn)

    return route


WEIGHT = 3_000_000_000

VMEM = pl.BlockSpec(memory_space=pltpu.VMEM)
SMEM = pl.BlockSpec(memory_space=pltpu.SMEM)


def slices_of(count):
    return jax.ShapeDtypeStruct((count, 2, 128, 128), BF16)


def call(kernel, info, arrays, out_shape, flops, scratch=()):
    outs = jax.tree.map(lambda _: VMEM, out_shape)
    return pl.pallas_call(
        kernel,
        out_shape=out_shape,
        in_specs=[SMEM] + [VMEM] * len(arrays),
        out_specs=outs,
        scratch_shapes=scratch,
        compiler_params=pltpu.CompilerParams(vmem_limit_bytes=24 * 1024 * 1024),
        cost_estimate=pl.CostEstimate(flops=flops, bytes_accessed=1 << 20, transcendentals=0),
    )(info, *arrays)


def place_of(info, offset):
    return lax.rem(info[0] + jnp.where(info[1] == 0, 8 - offset, 8 + offset), 8)


def columns_of(info, offset):
    return pl.ds(pl.multiple_of(place_of(info, offset) * 128, 128), 128)


def halves(info, own, other):
    first = jnp.where(info[1] == 0, own, other)
    second = jnp.where(info[1] == 0, other, own)
    return first, second


def whole(info, own_ref, other_ref, momentum, part):
    return jnp.concatenate(halves(info, own_ref[momentum, part], other_ref[momentum, part]), axis=0)


def cut(info, own_ref, other_ref, offset, out):
    columns = columns_of(info, offset)
    for part in range(2):
        first, second = halves(info, own_ref[info[5], part, :, columns], other_ref[info[5], part, :, columns])
        out[part] = jnp.concatenate([first, second], axis=0).T


def first_cut_kernel(info, own, other, a):
    for part in range(2):
        a[part] = whole(info, own, other, info[2], part)


def cut_kernel(info, *refs):
    count = len(refs) // 2
    for k in range(count):
        cut(info, refs[k], refs[count + k], 0, refs[-1].at[k])


def left_side(info, a_ref, offset):
    columns = columns_of(info, offset)
    real, imag = a_ref[0, :, columns], a_ref[1, :, columns]
    return jnp.concatenate(
        [jnp.concatenate([real, -imag], axis=1), jnp.concatenate([imag, real], axis=1)], axis=0
    )


def products_kernel(offsets, info, a_ref, *refs):
    count = len(offsets)
    own, other, out = refs[:count], refs[count : 2 * count], refs[-1]
    total = refs[2 * count][...] if len(refs) > 2 * count + 1 else None
    for offset, one, two in zip(offsets, own, other):
        block = jnp.concatenate([whole(info, one, two, info[3], part) for part in range(2)], axis=0)
        term = jnp.dot(left_side(info, a_ref, offset), block, preferred_element_type=F32)
        total = term if total is None else total + term
    out[...] = total


OFFSETS = (0, 1, -1, 2, -2, 3, -3, 4)


def last_kernel(info, a_ref, acc, *refs):
    own, other = refs[0:8], refs[8:16]
    keep, send, out, rounded_ref = refs[16:20]
    block = jnp.concatenate([whole(info, own[7], other[7], info[3], part) for part in range(2)], axis=0)
    product = acc[...] + jnp.dot(left_side(info, a_ref, 4), block, preferred_element_type=F32)
    rounded = product.astype(BF16)
    for part in range(2):
        rounded_ref[part] = rounded[part * 128 : part * 128 + 128]
        low, high = rounded[part * 128 : part * 128 + 64], rounded[part * 128 + 64 : part * 128 + 128]
        keep[part], send[part] = halves(info, low, high)
    total = None
    for offset, one, two in zip(OFFSETS, own, other):
        block = jnp.concatenate([whole(info, one, two, info[4], part) for part in range(2)], axis=0)
        term = jnp.dot(left_side(info, rounded_ref, offset), block, preferred_element_type=F32)
        total = term if total is None else total + term
    out[...] = total


def trace_kernel(info, product, near, middle, late, trace):
    slices = [near.at[0], near.at[1], near.at[2], middle.at[0], middle.at[1], late.at[0], late.at[1], late.at[2]]
    re = im = None
    for offset, piece in zip(OFFSETS, slices):
        columns = columns_of(info, offset)
        q_re, q_im = product[0:128, columns], product[128:256, columns]
        d_re, d_im = piece[0].astype(F32), piece[1].astype(F32)
        more_re, more_im = q_re * d_re - q_im * d_im, q_re * d_im + q_im * d_re
        re = more_re if re is None else re + more_re
        im = more_im if im is None else im + more_im
    re = jnp.sum(jnp.sum(re, axis=0, keepdims=True), axis=1, keepdims=True)
    im = jnp.sum(jnp.sum(im, axis=0, keepdims=True), axis=1, keepdims=True)
    lane = lax.broadcasted_iota(jnp.int32, (1, 128), 1)
    trace[...] = jnp.where(lane == 2 * info[0], re, jnp.where(lane == 2 * info[0] + 1, im, 0.0))


def add_kernel(info, below, own, above, two, three):
    two[...] = own[...] + above[...]
    three[...] = below[...] + own[...] + above[...]


def shards(fields, mom_table):
    rows = fields[:, 0]
    tm, row = lax.axis_index("tm"), lax.axis_index("row")
    core, place, half = tm % 2, row // 2, row % 2
    momenta = lax.dynamic_index_in_dim(mom_table, core, 0, keepdims=False)[0]
    info = jnp.concatenate([jnp.stack([place, core]), momenta])
    wall = lax.optimization_barrier
    block_of_products = jax.ShapeDtypeStruct((256, 1024), F32)

    own = moved(rows, to_hub)

    ownx, p1 = moved(own, other_core), moved(own, onward)
    q1 = moved(ownx, onward)
    a = call(first_cut_kernel, info, [own, ownx], jax.ShapeDtypeStruct((2, 128, 1024), BF16), 1)
    a = moved(a, hub_ahead(0))

    p2, p1x = moved(p1, onward), moved(p1, other_core)
    q2, q1x = moved(q1, onward), moved(q1, other_core)
    three, three_x = [own, p1, q1x], [ownx, q1, p1x]
    near = call(cut_kernel, info, three + three_x, slices_of(3), 1)
    acc = call(lambda *refs: products_kernel(OFFSETS[:1], *refs), info, [a, own, ownx], block_of_products, WEIGHT)
    p2, a, acc = wall((p2, a, acc))

    near = moved(near, hub_ahead(0))
    p3, p2x = moved(p2, onward), moved(p2, other_core)
    q3, q2x = moved(q2, onward), moved(q2, other_core)
    p3, near = wall((p3, near))

    p4, p3x = moved(p3, onward), moved(p3, other_core)
    five, five_x = three + [p2, q2x], three_x + [q2, p2x]
    middle = moved(call(cut_kernel, info, five[3:] + five_x[3:], slices_of(2), 1), hub_ahead(0))
    acc = call(
        lambda *refs: products_kernel(OFFSETS[1:5], *refs), info, [a] + five[1:] + five_x[1:] + [acc], block_of_products, 1
    )
    q3, acc = wall((q3, acc))

    q3x = moved(q3, other_core)
    p4, middle = wall((p4, middle))

    p4x = moved(p4, other_core)
    two, two_x = [p3, q3x], [q3, p3x]
    acc = call(
        lambda *refs: products_kernel(OFFSETS[5:7], *refs), info, [a] + two + two_x + [acc], block_of_products, 1
    )
    late = moved(call(cut_kernel, info, two + [p4] + two_x + [p4x], slices_of(3), 1), hub_ahead(0))
    half_block = jax.ShapeDtypeStruct((2, 64, 1024), BF16)
    keep, send, product = call(
        last_kernel,
        info,
        [a, acc] + five + two + [p4] + five_x + two_x + [p4x],
        (half_block, half_block, block_of_products),
        WEIGHT,
        [pltpu.VMEM((2, 128, 1024), BF16)],
    )
    share = jax.ShapeDtypeStruct((1, 128), F32)
    trace = call(trace_kernel, info, [product, near, middle, late], share, 1)

    below, above = moved(trace, along(1)), moved(trace, along(-1))
    kept, sent = moved(keep, from_hub(0)), moved(send, from_hub(1))
    two, three = call(add_kernel, info, [below, trace, above], (share, share), WEIGHT)
    below, above = moved(two, along(3)), moved(three, along(-3))
    trace, kept, sent = wall((below + three + above, kept, sent))
    first, second = moved(trace, from_hub(0)), moved(trace, from_hub(1))
    products = jnp.where(half == 0, jnp.stack([kept, sent]), jnp.stack([sent, kept]))[:, None, None]
    both = jnp.where(half == 0, jnp.concatenate([first, second]), jnp.concatenate([second, first]))
    correlator = jnp.sum(both[:, :16].reshape(2, 8, 2), axis=1)[:, None, None, :] / F32(1024)
    return products, correlator


def solution(mesh):
    return jax.shard_map(
        shards,
        mesh=mesh,
        in_specs=(P(None, "tm", None, "row", None), P()),
        out_specs=(P(None, None, "tm", None, "row", None), P(None, None, "tm", None)),
        check_vma=False,
    )
```

```python
import jax
import jax.numpy as jnp
from jax import lax
from jax.experimental import pallas as pl
from jax.experimental.pallas import tpu as pltpu
from jax.sharding import PartitionSpec as P

BOTH = ("tm", "row")
BF16 = jnp.bfloat16
F32 = jnp.float32


def hub_of(s):
    m, odd = divmod(s % 16, 2)
    low, x = divmod(m, 4)
    return (1 - low) * 4 + x, odd ^ low


SERVED = {hub_of(s): s for s in range(16)}


def moved(block, route):
    def index_of(m, c, z, h):
        return ((m % 8) * 2 + c) * 16 + (z % 8) * 2 + h

    places = [(m, c, z, h) for m in range(8) for c in range(2) for z in range(8) for h in range(2)]
    return lax.ppermute(block, BOTH, [(index_of(*at), index_of(*route(*at))) for at in places])


def along(step):
    return lambda m, c, z, h: (m, c, z + step, h)


def onward(m, c, z, h):
    return (m, c, z + (1 if c == 0 else -1), h)


def other_core(m, c, z, h):
    return (m, 1 - c, z, h)


def to_hub(m, c, z, h):
    column, half = hub_of(2 * m + c)
    return (column, h, z, half)


def hub_ahead(step):
    def route(m, c, z, h):
        column, half = hub_of(SERVED[m, h] + 1 + c)
        return (column, c, z + (step if c == 0 else -step), half)

    return route


def from_hub(turn):
    def route(m, c, z, h):
        t = (SERVED[m, h] - 1 - c) % 16
        return (t // 2, t % 2, z, c ^ turn)

    return route


WEIGHT = 3_000_000_000

VMEM = pl.BlockSpec(memory_space=pltpu.VMEM)
SMEM = pl.BlockSpec(memory_space=pltpu.SMEM)


def slices_of(count):
    return jax.ShapeDtypeStruct((count, 2, 128, 128), BF16)


def call(kernel, info, arrays, out_shape, flops, scratch=()):
    outs = jax.tree.map(lambda _: VMEM, out_shape)
    return pl.pallas_call(
        kernel,
        out_shape=out_shape,
        in_specs=[SMEM] + [VMEM] * len(arrays),
        out_specs=outs,
        scratch_shapes=scratch,
        compiler_params=pltpu.CompilerParams(vmem_limit_bytes=24 * 1024 * 1024),
        cost_estimate=pl.CostEstimate(flops=flops, bytes_accessed=1 << 20, transcendentals=0),
    )(info, *arrays)


def place_of(info, offset):
    return lax.rem(info[0] + jnp.where(info[1] == 0, 8 - offset, 8 + offset), 8)


def columns_of(info, offset):
    return pl.ds(pl.multiple_of(place_of(info, offset) * 128, 128), 128)


def halves(info, own, other):
    first = jnp.where(info[1] == 0, own, other)
    second = jnp.where(info[1] == 0, other, own)
    return first, second


def whole(info, own_ref, other_ref, momentum, part):
    return jnp.concatenate(halves(info, own_ref[momentum, part], other_ref[momentum, part]), axis=0)


def cut(info, own_ref, other_ref, offset, out):
    columns = columns_of(info, offset)
    for part in range(2):
        first, second = halves(info, own_ref[info[5], part, :, columns], other_ref[info[5], part, :, columns])
        out[part] = jnp.concatenate([first, second], axis=0).T


def first_cut_kernel(info, own, other, a):
    for part in range(2):
        a[part] = whole(info, own, other, info[2], part)


def cut_kernel(info, *refs):
    count = len(refs) // 2
    for k in range(count):
        cut(info, refs[k], refs[count + k], 0, refs[-1].at[k])


def left_side(info, a_ref, offset):
    columns = columns_of(info, offset)
    real, imag = a_ref[0, :, columns], a_ref[1, :, columns]
    return jnp.concatenate(
        [jnp.concatenate([real, -imag], axis=1), jnp.concatenate([imag, real], axis=1)], axis=0
    )


def products_kernel(offsets, info, a_ref, *refs):
    count = len(offsets)
    own, other, out = refs[:count], refs[count : 2 * count], refs[-1]
    total = refs[2 * count][...] if len(refs) > 2 * count + 1 else None
    for offset, one, two in zip(offsets, own, other):
        block = jnp.concatenate([whole(info, one, two, info[3], part) for part in range(2)], axis=0)
        term = jnp.dot(left_side(info, a_ref, offset), block, preferred_element_type=F32)
        total = term if total is None else total + term
    out[...] = total


OFFSETS = (0, 1, -1, 2, -2, 3, -3, 4)


def last_kernel(info, a_ref, acc, *refs):
    own, other = refs[0:8], refs[8:16]
    keep, send, out, rounded_ref = refs[16:20]
    block = jnp.concatenate([whole(info, own[7], other[7], info[3], part) for part in range(2)], axis=0)
    product = acc[...] + jnp.dot(left_side(info, a_ref, 4), block, preferred_element_type=F32)
    rounded = product.astype(BF16)
    for part in range(2):
        rounded_ref[part] = rounded[part * 128 : part * 128 + 128]
        low, high = rounded[part * 128 : part * 128 + 64], rounded[part * 128 + 64 : part * 128 + 128]
        keep[part], send[part] = halves(info, low, high)
    total = None
    for offset, one, two in zip(OFFSETS, own, other):
        block = jnp.concatenate([whole(info, one, two, info[4], part) for part in range(2)], axis=0)
        term = jnp.dot(left_side(info, rounded_ref, offset), block, preferred_element_type=F32)
        total = term if total is None else total + term
    out[...] = total


def trace_kernel(info, product, near, middle, late, trace):
    slices = [near.at[0], near.at[1], near.at[2], middle.at[0], middle.at[1], late.at[0], late.at[1], late.at[2]]
    re = im = None
    for offset, piece in zip(OFFSETS, slices):
        columns = columns_of(info, offset)
        q_re, q_im = product[0:128, columns], product[128:256, columns]
        d_re, d_im = piece[0].astype(F32), piece[1].astype(F32)
        more_re, more_im = q_re * d_re - q_im * d_im, q_re * d_im + q_im * d_re
        re = more_re if re is None else re + more_re
        im = more_im if im is None else im + more_im
    re = jnp.sum(jnp.sum(re, axis=0, keepdims=True), axis=1, keepdims=True)
    im = jnp.sum(jnp.sum(im, axis=0, keepdims=True), axis=1, keepdims=True)
    lane = lax.broadcasted_iota(jnp.int32, (1, 128), 1)
    trace[...] = jnp.where(lane == 2 * info[0], re, jnp.where(lane == 2 * info[0] + 1, im, 0.0))


def shards(fields, mom_table):
    rows = fields[:, 0]
    tm, row = lax.axis_index("tm"), lax.axis_index("row")
    core, place, half = tm % 2, row // 2, row % 2
    momenta = lax.dynamic_index_in_dim(mom_table, core, 0, keepdims=False)[0]
    info = jnp.concatenate([jnp.stack([place, core]), momenta])
    wall = lax.optimization_barrier
    block_of_products = jax.ShapeDtypeStruct((256, 1024), F32)

    own = moved(rows, to_hub)

    ownx, p1 = moved(own, other_core), moved(own, onward)
    q1 = moved(ownx, onward)
    a = call(first_cut_kernel, info, [own, ownx], jax.ShapeDtypeStruct((2, 128, 1024), BF16), 1)
    a = moved(a, hub_ahead(0))

    p2, p1x = moved(p1, onward), moved(p1, other_core)
    q2, q1x = moved(q1, onward), moved(q1, other_core)
    three, three_x = [own, p1, q1x], [ownx, q1, p1x]
    near = call(cut_kernel, info, three + three_x, slices_of(3), 1)
    acc = call(lambda *refs: products_kernel(OFFSETS[:1], *refs), info, [a, own, ownx], block_of_products, WEIGHT)
    p2, a, acc = wall((p2, a, acc))

    near = moved(near, hub_ahead(0))
    p3, p2x = moved(p2, onward), moved(p2, other_core)
    q3, q2x = moved(q2, onward), moved(q2, other_core)
    p3, near = wall((p3, near))

    p4, p3x = moved(p3, onward), moved(p3, other_core)
    five, five_x = three + [p2, q2x], three_x + [q2, p2x]
    middle = moved(call(cut_kernel, info, five[3:] + five_x[3:], slices_of(2), 1), hub_ahead(0))
    acc = call(
        lambda *refs: products_kernel(OFFSETS[1:5], *refs), info, [a] + five[1:] + five_x[1:] + [acc], block_of_products, 1
    )
    q3, acc = wall((q3, acc))

    q3x = moved(q3, other_core)
    p4, middle = wall((p4, middle))

    p4x = moved(p4, other_core)
    two, two_x = [p3, q3x], [q3, p3x]
    acc = call(
        lambda *refs: products_kernel(OFFSETS[5:7], *refs), info, [a] + two + two_x + [acc], block_of_products, 1
    )
    late = moved(call(cut_kernel, info, two + [p4] + two_x + [p4x], slices_of(3), 1), hub_ahead(0))
    half_block = jax.ShapeDtypeStruct((2, 64, 1024), BF16)
    keep, send, product = call(
        last_kernel,
        info,
        [a, acc] + five + two + [p4] + five_x + two_x + [p4x],
        (half_block, half_block, block_of_products),
        WEIGHT,
        [pltpu.VMEM((2, 128, 1024), BF16)],
    )
    share = jax.ShapeDtypeStruct((1, 128), F32)
    trace = call(trace_kernel, info, [product, near, middle, late], share, 1)

    below, above = moved(trace, along(1)), moved(trace, along(-1))
    kept, sent = moved(keep, from_hub(0)), moved(send, from_hub(1))
    two, three, kept = wall((trace + above, below + trace + above, kept))
    below, above = moved(two, along(3)), moved(three, along(-3))
    trace, kept, sent = wall((below + three + above, kept, sent))
    first, second = moved(trace, from_hub(0)), moved(trace, from_hub(1))
    products = jnp.where(half == 0, jnp.stack([kept, sent]), jnp.stack([sent, kept]))[:, None, None]
    both = jnp.where(half == 0, jnp.concatenate([first, second]), jnp.concatenate([second, first]))
    correlator = jnp.sum(both[:, :16].reshape(2, 8, 2), axis=1)[:, None, None, :] / F32(1024)
    return products, correlator


def solution(mesh):
    return jax.shard_map(
        shards,
        mesh=mesh,
        in_specs=(P(None, "tm", None, "row", None), P()),
        out_specs=(P(None, None, "tm", None, "row", None), P(None, None, "tm", None)),
        check_vma=False,
    )
```

```python
import jax
import jax.numpy as jnp
from jax import lax
from jax.experimental import pallas as pl
from jax.experimental.pallas import tpu as pltpu
from jax.sharding import PartitionSpec as P

BOTH = ("tm", "row")
BF16 = jnp.bfloat16
F32 = jnp.float32


def hub_of(s):
    m, odd = divmod(s % 16, 2)
    low, x = divmod(m, 4)
    return (1 - low) * 4 + x, odd ^ low


SERVED = {hub_of(s): s for s in range(16)}


def moved(block, route):
    def index_of(m, c, z, h):
        return ((m % 8) * 2 + c) * 16 + (z % 8) * 2 + h

    places = [(m, c, z, h) for m in range(8) for c in range(2) for z in range(8) for h in range(2)]
    return lax.ppermute(block, BOTH, [(index_of(*at), index_of(*route(*at))) for at in places])


def along(step):
    return lambda m, c, z, h: (m, c, z + step, h)


def onward(m, c, z, h):
    return (m, c, z + (1 if c == 0 else -1), h)


def other_core(m, c, z, h):
    return (m, 1 - c, z, h)


def to_hub(m, c, z, h):
    column, half = hub_of(2 * m + c)
    return (column, h, z, half)


def hub_ahead(step):
    def route(m, c, z, h):
        column, half = hub_of(SERVED[m, h] + 1 + c)
        return (column, c, z + (step if c == 0 else -step), half)

    return route


def from_hub(turn):
    def route(m, c, z, h):
        t = (SERVED[m, h] - 1 - c) % 16
        return (t // 2, t % 2, z, c ^ turn)

    return route


WEIGHT = 3_000_000_000

VMEM = pl.BlockSpec(memory_space=pltpu.VMEM)
SMEM = pl.BlockSpec(memory_space=pltpu.SMEM)


def slices_of(count):
    return jax.ShapeDtypeStruct((count, 2, 128, 128), BF16)


def call(kernel, info, arrays, out_shape, flops, scratch=()):
    outs = jax.tree.map(lambda _: VMEM, out_shape)
    return pl.pallas_call(
        kernel,
        out_shape=out_shape,
        in_specs=[SMEM] + [VMEM] * len(arrays),
        out_specs=outs,
        scratch_shapes=scratch,
        compiler_params=pltpu.CompilerParams(vmem_limit_bytes=24 * 1024 * 1024),
        cost_estimate=pl.CostEstimate(flops=flops, bytes_accessed=1 << 20, transcendentals=0),
    )(info, *arrays)


def place_of(info, offset):
    return lax.rem(info[0] + jnp.where(info[1] == 0, 8 - offset, 8 + offset), 8)


def columns_of(info, offset):
    return pl.ds(pl.multiple_of(place_of(info, offset) * 128, 128), 128)


def halves(info, own, other):
    first = jnp.where(info[1] == 0, own, other)
    second = jnp.where(info[1] == 0, other, own)
    return first, second


def whole(info, own_ref, other_ref, momentum, part):
    return jnp.concatenate(halves(info, own_ref[momentum, part], other_ref[momentum, part]), axis=0)


def cut(info, own_ref, other_ref, offset, out):
    columns = columns_of(info, offset)
    for part in range(2):
        first, second = halves(info, own_ref[info[5], part, :, columns], other_ref[info[5], part, :, columns])
        out[part] = jnp.concatenate([first, second], axis=0).T


def first_cut_kernel(info, own, other, a):
    for part in range(2):
        a[part] = whole(info, own, other, info[2], part)


def cut_kernel(info, *refs):
    count = len(refs) // 2
    for k in range(count):
        cut(info, refs[k], refs[count + k], 0, refs[-1].at[k])


def late_kernel(info, own_u, own_d, other_u, other_d, out, across):
    cut(info, own_u, other_u, 0, out.at[0])
    cut(info, own_d, other_d, 0, out.at[1])
    cut(info, own_u, other_u, -1, across)


def left_side(info, a_ref, offset):
    columns = columns_of(info, offset)
    real, imag = a_ref[0, :, columns], a_ref[1, :, columns]
    return jnp.concatenate(
        [jnp.concatenate([real, -imag], axis=1), jnp.concatenate([imag, real], axis=1)], axis=0
    )


def products_kernel(offsets, info, a_ref, *refs):
    count = len(offsets)
    own, other, out = refs[:count], refs[count : 2 * count], refs[-1]
    total = refs[2 * count][...] if len(refs) > 2 * count + 1 else None
    for offset, one, two in zip(offsets, own, other):
        block = jnp.concatenate([whole(info, one, two, info[3], part) for part in range(2)], axis=0)
        term = jnp.dot(left_side(info, a_ref, offset), block, preferred_element_type=F32)
        total = term if total is None else total + term
    out[...] = total


OFFSETS = (0, 1, -1, 2, -2, 3, -3, 4)


def last_kernel(info, a_ref, acc, near, middle, *refs):
    own, other = refs[0:8], refs[8:16]
    keep, send, out, early, rounded_ref = refs[16:21]
    block = jnp.concatenate([whole(info, own[7], other[7], info[3], part) for part in range(2)], axis=0)
    product = acc[...] + jnp.dot(left_side(info, a_ref, 4), block, preferred_element_type=F32)
    rounded = product.astype(BF16)
    for part in range(2):
        rounded_ref[part] = rounded[part * 128 : part * 128 + 128]
        low, high = rounded[part * 128 : part * 128 + 64], rounded[part * 128 + 64 : part * 128 + 128]
        keep[part], send[part] = halves(info, low, high)
    total = None
    for offset, one, two in zip(OFFSETS, own, other):
        block = jnp.concatenate([whole(info, one, two, info[4], part) for part in range(2)], axis=0)
        term = jnp.dot(left_side(info, rounded_ref, offset), block, preferred_element_type=F32)
        total = term if total is None else total + term
    out[...] = total
    slices = [near.at[0], near.at[1], near.at[2], middle.at[0], middle.at[1]]
    early[0:1, :], early[1:2, :] = trace_sum(info, out, list(zip(OFFSETS, slices)))


def trace_sum(info, product, slices):
    re = im = None
    for offset, piece in slices:
        columns = columns_of(info, offset)
        q_re, q_im = product[0:128, columns], product[128:256, columns]
        d_re, d_im = piece[0].astype(F32), piece[1].astype(F32)
        more_re, more_im = q_re * d_re - q_im * d_im, q_re * d_im + q_im * d_re
        re = more_re if re is None else re + more_re
        im = more_im if im is None else im + more_im
    return [jnp.sum(part, axis=0, keepdims=True) for part in (re, im)]


def trace_kernel(info, product, early, late, across, trace):
    re, im = trace_sum(info, product, [(3, late.at[0]), (-3, late.at[1]), (4, across)])
    re = jnp.sum(re + early[0:1, :], axis=1, keepdims=True)
    im = jnp.sum(im + early[1:2, :], axis=1, keepdims=True)
    lane = lax.broadcasted_iota(jnp.int32, (1, 128), 1)
    trace[...] = jnp.where(lane == 2 * info[0], re, jnp.where(lane == 2 * info[0] + 1, im, 0.0))


def shards(fields, mom_table):
    rows = fields[:, 0]
    tm, row = lax.axis_index("tm"), lax.axis_index("row")
    core, place, half = tm % 2, row // 2, row % 2
    momenta = lax.dynamic_index_in_dim(mom_table, core, 0, keepdims=False)[0]
    info = jnp.concatenate([jnp.stack([place, core]), momenta])
    wall = lax.optimization_barrier
    block_of_products = jax.ShapeDtypeStruct((256, 1024), F32)

    own = moved(rows, to_hub)

    ownx, p1 = moved(own, other_core), moved(own, onward)
    q1 = moved(ownx, onward)
    a = call(first_cut_kernel, info, [own, ownx], jax.ShapeDtypeStruct((2, 128, 1024), BF16), 1)
    a = moved(a, hub_ahead(0))

    p2, p1x = moved(p1, onward), moved(p1, other_core)
    q2, q1x = moved(q1, onward), moved(q1, other_core)
    three, three_x = [own, p1, q1x], [ownx, q1, p1x]
    near = call(cut_kernel, info, three + three_x, slices_of(3), 1)
    acc = call(lambda *refs: products_kernel(OFFSETS[:1], *refs), info, [a, own, ownx], block_of_products, WEIGHT)
    p2, a, acc = wall((p2, a, acc))

    near = moved(near, hub_ahead(0))
    p3, p2x = moved(p2, onward), moved(p2, other_core)
    q3, q2x = moved(q2, onward), moved(q2, other_core)
    p3, near = wall((p3, near))

    p4, p3x = moved(p3, onward), moved(p3, other_core)
    five, five_x = three + [p2, q2x], three_x + [q2, p2x]
    middle = moved(call(cut_kernel, info, five[3:] + five_x[3:], slices_of(2), 1), hub_ahead(0))
    acc = call(
        lambda *refs: products_kernel(OFFSETS[1:5], *refs), info, [a] + five[1:] + five_x[1:] + [acc], block_of_products, 1
    )
    q3, acc = wall((q3, acc))

    q3x = moved(q3, other_core)
    two, two_x = [p3, q3x], [q3, p3x]
    late, across = call(late_kernel, info, two + two_x, (slices_of(2), jax.ShapeDtypeStruct((2, 128, 128), BF16)), 1)
    p4, middle = wall((p4, middle))

    p4x = moved(p4, other_core)
    late, across = moved(late, hub_ahead(0)), moved(across, hub_ahead(1))
    acc = call(
        lambda *refs: products_kernel(OFFSETS[5:7], *refs), info, [a] + two + two_x + [acc], block_of_products, 1
    )
    half_block = jax.ShapeDtypeStruct((2, 64, 1024), BF16)
    keep, send, product, early = call(
        last_kernel,
        info,
        [a, acc, near, middle] + five + two + [p4] + five_x + two_x + [p4x],
        (half_block, half_block, block_of_products, jax.ShapeDtypeStruct((8, 128), F32)),
        1,
        [pltpu.VMEM((2, 128, 1024), BF16)],
    )
    trace = call(trace_kernel, info, [product, early, late, across], jax.ShapeDtypeStruct((1, 128), F32), 1)

    below, above = moved(trace, along(1)), moved(trace, along(-1))
    kept, sent = moved(keep, from_hub(0)), moved(send, from_hub(1))
    two, three, kept = wall((trace + above, below + trace + above, kept))
    below, above = moved(two, along(3)), moved(three, along(-3))
    trace, kept, sent = wall((below + three + above, kept, sent))
    first, second = moved(trace, from_hub(0)), moved(trace, from_hub(1))
    products = jnp.where(half == 0, jnp.stack([kept, sent]), jnp.stack([sent, kept]))[:, None, None]
    both = jnp.where(half == 0, jnp.concatenate([first, second]), jnp.concatenate([second, first]))
    correlator = jnp.sum(both[:, :16].reshape(2, 8, 2), axis=1)[:, None, None, :] / F32(1024)
    return products, correlator


def solution(mesh):
    return jax.shard_map(
        shards,
        mesh=mesh,
        in_specs=(P(None, "tm", None, "row", None), P()),
        out_specs=(P(None, None, "tm", None, "row", None), P(None, None, "tm", None)),
        check_vma=False,
    )
```

```python
import jax
import jax.numpy as jnp
from jax import lax
from jax.experimental import pallas as pl
from jax.experimental.pallas import tpu as pltpu
from jax.sharding import PartitionSpec as P

BOTH = ("tm", "row")
BF16 = jnp.bfloat16
F32 = jnp.float32


def hub_of(s):
    m, odd = divmod(s % 16, 2)
    low, x = divmod(m, 4)
    return (1 - low) * 4 + x, odd ^ low


SERVED = {hub_of(s): s for s in range(16)}


def moved(block, route):
    def index_of(m, c, z, h):
        return ((m % 8) * 2 + c) * 16 + (z % 8) * 2 + h

    places = [(m, c, z, h) for m in range(8) for c in range(2) for z in range(8) for h in range(2)]
    return lax.ppermute(block, BOTH, [(index_of(*at), index_of(*route(*at))) for at in places])


def along(step):
    return lambda m, c, z, h: (m, c, z + step, h)


def onward(m, c, z, h):
    return (m, c, z + (1 if c == 0 else -1), h)


def other_core(m, c, z, h):
    return (m, 1 - c, z, h)


def to_hub(m, c, z, h):
    column, half = hub_of(2 * m + c)
    return (column, h, z, half)


def hub_ahead(step, turn=0):
    def route(m, c, z, h):
        r = c ^ turn
        column, half = hub_of(SERVED[m, h] + 1 + r)
        return (column, r, z + (step if r == 0 else -step), half)

    return route


def from_hub(turn):
    def route(m, c, z, h):
        t = (SERVED[m, h] - 1 - c) % 16
        return (t // 2, t % 2, z, c ^ turn)

    return route


WEIGHT = 3_000_000_000
ROOM = 5_000_000_000

VMEM = pl.BlockSpec(memory_space=pltpu.VMEM)
SMEM = pl.BlockSpec(memory_space=pltpu.SMEM)


def slices_of(count):
    return jax.ShapeDtypeStruct((count, 2, 128, 128), BF16)


def call(kernel, info, arrays, out_shape, flops, scratch=()):
    outs = jax.tree.map(lambda _: VMEM, out_shape)
    return pl.pallas_call(
        kernel,
        out_shape=out_shape,
        in_specs=[SMEM] + [VMEM] * len(arrays),
        out_specs=outs,
        scratch_shapes=scratch,
        compiler_params=pltpu.CompilerParams(vmem_limit_bytes=24 * 1024 * 1024),
        cost_estimate=pl.CostEstimate(flops=flops, bytes_accessed=1 << 20, transcendentals=0),
    )(info, *arrays)


def place_of(info, offset):
    return lax.rem(info[0] + jnp.where(info[1] == 0, 8 - offset, 8 + offset), 8)


def columns_of(info, offset):
    return pl.ds(pl.multiple_of(place_of(info, offset) * 128, 128), 128)


def halves(info, own, other):
    first = jnp.where(info[1] == 0, own, other)
    second = jnp.where(info[1] == 0, other, own)
    return first, second


def whole(info, own_ref, other_ref, momentum, part):
    return jnp.concatenate(halves(info, own_ref[momentum, part], other_ref[momentum, part]), axis=0)


def cut(info, own_ref, other_ref, offset, out, momentum=5):
    columns = columns_of(info, offset)
    for part in range(2):
        first, second = halves(
            info, own_ref[info[momentum], part, :, columns], other_ref[info[momentum], part, :, columns]
        )
        out[part] = jnp.concatenate([first, second], axis=0).T


def first_cut_kernel(info, own, other, a):
    for part in range(2):
        a[part] = whole(info, own, other, info[2], part)


def cut_kernel(info, *refs):
    count = len(refs) // 2
    for k in range(count):
        cut(info, refs[k], refs[count + k], 0, refs[-1].at[k])


def late_kernel(info, own, other, here, there, across):
    cut(info, own, other, 0, here)
    cut(info, own, other, 0, there, momentum=6)
    cut(info, own, other, -1, across)


def left_side(info, a_ref, offset):
    columns = columns_of(info, offset)
    real, imag = a_ref[0, :, columns], a_ref[1, :, columns]
    return jnp.concatenate(
        [jnp.concatenate([real, -imag], axis=1), jnp.concatenate([imag, real], axis=1)], axis=0
    )


def products_kernel(offsets, info, a_ref, *refs):
    count = len(offsets)
    own, other, out = refs[:count], refs[count : 2 * count], refs[-1]
    total = refs[2 * count][...] if len(refs) > 2 * count + 1 else None
    for offset, one, two in zip(offsets, own, other):
        block = jnp.concatenate([whole(info, one, two, info[3], part) for part in range(2)], axis=0)
        term = jnp.dot(left_side(info, a_ref, offset), block, preferred_element_type=F32)
        total = term if total is None else total + term
    out[...] = total


OFFSETS = (0, 1, -1, 2, -2, 3, -3, 4)


def last_kernel(info, a_ref, acc, near, middle, *refs):
    own, other = refs[0:8], refs[8:16]
    keep, send, out, early, rounded_ref = refs[16:21]
    block = jnp.concatenate([whole(info, own[7], other[7], info[3], part) for part in range(2)], axis=0)
    product = acc[...] + jnp.dot(left_side(info, a_ref, 4), block, preferred_element_type=F32)
    rounded = product.astype(BF16)
    for part in range(2):
        rounded_ref[part] = rounded[part * 128 : part * 128 + 128]
        low, high = rounded[part * 128 : part * 128 + 64], rounded[part * 128 + 64 : part * 128 + 128]
        keep[part], send[part] = halves(info, low, high)
    total = None
    for offset, one, two in zip(OFFSETS, own, other):
        block = jnp.concatenate([whole(info, one, two, info[4], part) for part in range(2)], axis=0)
        term = jnp.dot(left_side(info, rounded_ref, offset), block, preferred_element_type=F32)
        total = term if total is None else total + term
    out[...] = total
    slices = [near.at[0], near.at[1], near.at[2], middle.at[0], middle.at[1]]
    early[0:1, :], early[1:2, :] = trace_sum(info, out, list(zip(OFFSETS, slices)))


def trace_sum(info, product, slices):
    re = im = None
    for offset, piece in slices:
        columns = columns_of(info, offset)
        q_re, q_im = product[0:128, columns], product[128:256, columns]
        d_re, d_im = piece[0].astype(F32), piece[1].astype(F32)
        more_re, more_im = q_re * d_re - q_im * d_im, q_re * d_im + q_im * d_re
        re = more_re if re is None else re + more_re
        im = more_im if im is None else im + more_im
    return [jnp.sum(part, axis=0, keepdims=True) for part in (re, im)]


def collect_kernel(info, here, there, across, out):
    out[0], out[1], out[2] = here[...], there[...], across[...]


def trace_kernel(info, product, early, late, trace):
    re, im = trace_sum(info, product, [(3, late.at[0]), (-3, late.at[1]), (4, late.at[2])])
    re = jnp.sum(re + early[0:1, :], axis=1, keepdims=True)
    im = jnp.sum(im + early[1:2, :], axis=1, keepdims=True)
    lane = lax.broadcasted_iota(jnp.int32, (1, 128), 1)
    trace[...] = jnp.where(lane == 2 * info[0], re, jnp.where(lane == 2 * info[0] + 1, im, 0.0))


def shards(fields, mom_table):
    rows = fields[:, 0]
    tm, row = lax.axis_index("tm"), lax.axis_index("row")
    core, place, half = tm % 2, row // 2, row % 2
    momenta = lax.dynamic_index_in_dim(mom_table, core, 0, keepdims=False)[0]
    others = lax.dynamic_index_in_dim(mom_table, 1 - core, 0, keepdims=False)[0]
    info = jnp.concatenate([jnp.stack([place, core]), momenta, others[3:]])
    wall = lax.optimization_barrier
    block_of_products = jax.ShapeDtypeStruct((256, 1024), F32)

    own = moved(rows, to_hub)

    ownx, p1 = moved(own, other_core), moved(own, onward)
    q1 = moved(ownx, onward)
    a = call(first_cut_kernel, info, [own, ownx], jax.ShapeDtypeStruct((2, 128, 1024), BF16), 1)
    a = moved(a, hub_ahead(0))

    p2, p1x = moved(p1, onward), moved(p1, other_core)
    q2, q1x = moved(q1, onward), moved(q1, other_core)
    three, three_x = [own, p1, q1x], [ownx, q1, p1x]
    near = call(cut_kernel, info, three + three_x, slices_of(3), 1)
    acc = call(lambda *refs: products_kernel(OFFSETS[:1], *refs), info, [a, own, ownx], block_of_products, WEIGHT)
    p2, a, acc = wall((p2, a, acc))

    near = moved(near, hub_ahead(0))
    p3, p2x = moved(p2, onward), moved(p2, other_core)
    q3, q2x = moved(q2, onward), moved(q2, other_core)
    p3, near = wall((p3, near))

    p4, p3x = moved(p3, onward), moved(p3, other_core)
    five, five_x = three + [p2, q2x], three_x + [q2, p2x]
    middle = moved(call(cut_kernel, info, five[3:] + five_x[3:], slices_of(2), 1), hub_ahead(0))
    acc = call(
        lambda *refs: products_kernel(OFFSETS[1:5], *refs), info, [a] + five[1:] + five_x[1:] + [acc], block_of_products, 1
    )
    q3, acc = wall((q3, acc))

    piece = jax.ShapeDtypeStruct((2, 128, 128), BF16)
    here, there, across = call(late_kernel, info, [p3, q3], (piece, piece, piece), 1)
    here, there, across = moved(here, hub_ahead(0)), moved(there, hub_ahead(0, 1)), moved(across, hub_ahead(1))
    late = call(collect_kernel, info, [here, there, across], slices_of(3), ROOM)
    p4, middle = wall((p4, middle))

    p4x, q3x = moved(p4, other_core), moved(q3, other_core)
    two, two_x = [p3, q3x], [q3, p3x]
    acc = call(
        lambda *refs: products_kernel(OFFSETS[5:7], *refs), info, [a] + two + two_x + [acc], block_of_products, 1
    )
    p4x, late = wall((p4x, late))
    half_block = jax.ShapeDtypeStruct((2, 64, 1024), BF16)
    keep, send, product, early = call(
        last_kernel,
        info,
        [a, acc, near, middle] + five + two + [p4] + five_x + two_x + [p4x],
        (half_block, half_block, block_of_products, jax.ShapeDtypeStruct((8, 128), F32)),
        1,
        [pltpu.VMEM((2, 128, 1024), BF16)],
    )
    trace = call(trace_kernel, info, [product, early, late], jax.ShapeDtypeStruct((1, 128), F32), 1)

    below, above = moved(trace, along(1)), moved(trace, along(-1))
    kept, sent = moved(keep, from_hub(0)), moved(send, from_hub(1))
    two, three, kept = wall((trace + above, below + trace + above, kept))
    below, above = moved(two, along(3)), moved(three, along(-3))
    trace, kept, sent = wall((below + three + above, kept, sent))
    first, second = moved(trace, from_hub(0)), moved(trace, from_hub(1))
    products = jnp.where(half == 0, jnp.stack([kept, sent]), jnp.stack([sent, kept]))[:, None, None]
    both = jnp.where(half == 0, jnp.concatenate([first, second]), jnp.concatenate([second, first]))
    correlator = jnp.sum(both[:, :16].reshape(2, 8, 2), axis=1)[:, None, None, :] / F32(1024)
    return products, correlator


def solution(mesh):
    return jax.shard_map(
        shards,
        mesh=mesh,
        in_specs=(P(None, "tm", None, "row", None), P()),
        out_specs=(P(None, None, "tm", None, "row", None), P(None, None, "tm", None)),
        check_vma=False,
    )
```

```python
import jax
import jax.numpy as jnp
from jax import lax
from jax.experimental import pallas as pl
from jax.experimental.pallas import tpu as pltpu
from jax.sharding import PartitionSpec as P

BOTH = ("tm", "row")
BF16 = jnp.bfloat16
F32 = jnp.float32


def hub_of(s):
    m, odd = divmod(s % 16, 2)
    low, x = divmod(m, 4)
    return (1 - low) * 4 + x, odd ^ low


SERVED = {hub_of(s): s for s in range(16)}


def moved(block, route):
    def index_of(m, c, z, h):
        return ((m % 8) * 2 + c) * 16 + (z % 8) * 2 + h

    places = [(m, c, z, h) for m in range(8) for c in range(2) for z in range(8) for h in range(2)]
    return lax.ppermute(block, BOTH, [(index_of(*at), index_of(*route(*at))) for at in places])


def along(step):
    return lambda m, c, z, h: (m, c, z + step, h)


def onward(m, c, z, h):
    return (m, c, z + (1 if c == 0 else -1), h)


def other_core(m, c, z, h):
    return (m, 1 - c, z, h)


def to_hub(step, turn=0):
    def route(m, c, z, h):
        column, half = hub_of(2 * m + c)
        core = h ^ turn
        return (column, core, z + (step if core == 0 else -step), half)

    return route


def hub_ahead(step):
    def route(m, c, z, h):
        column, half = hub_of(SERVED[m, h] + 1 + c)
        return (column, c, z + (step if c == 0 else -step), half)

    return route


def from_hub(turn):
    def route(m, c, z, h):
        t = (SERVED[m, h] - 1 - c) % 16
        return (t // 2, t % 2, z, c ^ turn)

    return route


WEIGHT = 3_000_000_000
WEIGHT0 = 1
ROOM = 1_000_000_000

VMEM = pl.BlockSpec(memory_space=pltpu.VMEM)
SMEM = pl.BlockSpec(memory_space=pltpu.SMEM)


def slices_of(count):
    return jax.ShapeDtypeStruct((count, 2, 128, 128), BF16)


def call(kernel, info, arrays, out_shape, flops, scratch=()):
    outs = jax.tree.map(lambda _: VMEM, out_shape)
    return pl.pallas_call(
        kernel,
        out_shape=out_shape,
        in_specs=[SMEM] + [VMEM] * len(arrays),
        out_specs=outs,
        scratch_shapes=scratch,
        compiler_params=pltpu.CompilerParams(vmem_limit_bytes=24 * 1024 * 1024),
        cost_estimate=pl.CostEstimate(flops=flops, bytes_accessed=1 << 20, transcendentals=0),
    )(info, *arrays)


def place_of(info, offset):
    return lax.rem(info[0] + jnp.where(info[1] == 0, 8 - offset, 8 + offset), 8)


def columns_of(info, offset):
    return pl.ds(pl.multiple_of(place_of(info, offset) * 128, 128), 128)


def halves(info, own, other):
    first = jnp.where(info[1] == 0, own, other)
    second = jnp.where(info[1] == 0, other, own)
    return first, second


def whole(info, own_ref, other_ref, momentum, part):
    return jnp.concatenate(halves(info, own_ref[momentum, part], other_ref[momentum, part]), axis=0)


def cut(info, own_ref, other_ref, offset, out):
    columns = columns_of(info, offset)
    for part in range(2):
        first, second = halves(info, own_ref[info[5], part, :, columns], other_ref[info[5], part, :, columns])
        out[part] = jnp.concatenate([first, second], axis=0).T


def first_cut_kernel(info, own, other, a):
    for part in range(2):
        a[part] = whole(info, own, other, info[2], part)


def cut_kernel(info, *refs):
    count = len(refs) // 2
    for k in range(count):
        cut(info, refs[k], refs[count + k], 0, refs[-1].at[k])


def left_side(info, a_ref, offset):
    columns = columns_of(info, offset)
    real, imag = a_ref[0, :, columns], a_ref[1, :, columns]
    return jnp.concatenate(
        [jnp.concatenate([real, -imag], axis=1), jnp.concatenate([imag, real], axis=1)], axis=0
    )


def products_kernel(offsets, info, a_ref, *refs):
    count = len(offsets)
    own, other, out = refs[:count], refs[count : 2 * count], refs[-1]
    total = refs[2 * count][...] if len(refs) > 2 * count + 1 else None
    for offset, one, two in zip(offsets, own, other):
        block = jnp.concatenate([whole(info, one, two, info[3], part) for part in range(2)], axis=0)
        term = jnp.dot(left_side(info, a_ref, offset), block, preferred_element_type=F32)
        total = term if total is None else total + term
    out[...] = total


OFFSETS = (0, 1, -1, 2, -2, 3, -3, 4)


def last_kernel(info, a_ref, acc, *refs):
    own, other = refs[0:8], refs[8:16]
    keep, send, out, rounded_ref = refs[16:20]
    block = jnp.concatenate([whole(info, own[7], other[7], info[3], part) for part in range(2)], axis=0)
    product = acc[...] + jnp.dot(left_side(info, a_ref, 4), block, preferred_element_type=F32)
    rounded = product.astype(BF16)
    rounded_ref[0] = rounded
    rounded_ref[1, 0:128], rounded_ref[1, 128:256] = -rounded[128:256], rounded[0:128]
    for part in range(2):
        low, high = rounded[part * 128 : part * 128 + 64], rounded[part * 128 + 64 : part * 128 + 128]
        keep[part], send[part] = halves(info, low, high)
    for tile in range(4):
        columns = pl.ds(tile * 256, 256)
        total = None
        for offset, one, two in zip(OFFSETS, own, other):
            parts = [halves(info, one[info[4], part, :, columns], two[info[4], part, :, columns]) for part in range(2)]
            block = jnp.concatenate([parts[0][0], parts[0][1], parts[1][0], parts[1][1]], axis=0)
            place = columns_of(info, offset)
            left = jnp.concatenate([rounded_ref[0, :, place], rounded_ref[1, :, place]], axis=1)
            term = jnp.dot(left, block, preferred_element_type=F32)
            total = term if total is None else total + term
        out[:, columns] = total


def trace_kernel(info, product, near, middle, late, trace):
    slices = [near.at[0], near.at[1], near.at[2], middle.at[0], middle.at[1], late.at[0], late.at[1], late.at[2]]
    re = im = None
    for offset, piece in zip(OFFSETS, slices):
        columns = columns_of(info, offset)
        q_re, q_im = product[0:128, columns], product[128:256, columns]
        d_re, d_im = piece[0].astype(F32), piece[1].astype(F32)
        more_re, more_im = q_re * d_re - q_im * d_im, q_re * d_im + q_im * d_re
        re = more_re if re is None else re + more_re
        im = more_im if im is None else im + more_im
    re = jnp.sum(jnp.sum(re, axis=0, keepdims=True), axis=1, keepdims=True)
    im = jnp.sum(jnp.sum(im, axis=0, keepdims=True), axis=1, keepdims=True)
    re, im = re * (1.0 / 1024), im * (1.0 / 1024)
    lane = lax.broadcasted_iota(jnp.int32, (1, 128), 1)
    trace[...] = jnp.where(lane == 2 * info[0], re, jnp.where(lane == 2 * info[0] + 1, im, 0.0))


def hold_kernel(info, block, out):
    pass


def hold(info, block, flops):
    anywhere = pl.BlockSpec(memory_space=pl.ANY)
    return pl.pallas_call(
        hold_kernel,
        out_shape=jax.ShapeDtypeStruct(block.shape, block.dtype),
        in_specs=[SMEM, anywhere],
        out_specs=anywhere,
        input_output_aliases={1: 0},
        cost_estimate=pl.CostEstimate(flops=flops, bytes_accessed=1 << 10, transcendentals=0),
    )(info, block)


def shards(fields, mom_table):
    rows = fields[:, 0]
    tm, row = lax.axis_index("tm"), lax.axis_index("row")
    core, place, half = tm % 2, row // 2, row % 2
    momenta = lax.dynamic_index_in_dim(mom_table, core, 0, keepdims=False)[0]
    info = jnp.concatenate([jnp.stack([place, core]), momenta])
    wall = lax.optimization_barrier
    block_of_products = jax.ShapeDtypeStruct((256, 1024), F32)

    p1, q1, rows = wall((moved(rows, to_hub(1)), moved(rows, to_hub(1, 1)), rows))

    p2, p1x = moved(p1, onward), moved(p1, other_core)
    q2, q1x = moved(q1, onward), moved(q1, other_core)
    own = moved(rows, to_hub(0))
    ownx = moved(own, other_core)
    a = call(first_cut_kernel, info, [own, ownx], jax.ShapeDtypeStruct((2, 128, 1024), BF16), 1)
    a = moved(a, hub_ahead(0))
    three, three_x = [own, p1, q1x], [ownx, q1, p1x]
    near = moved(call(cut_kernel, info, three + three_x, slices_of(3), 1), hub_ahead(0))
    p3, p2x = moved(p2, onward), moved(p2, other_core)
    q3, q2x = moved(q2, onward), moved(q2, other_core)

    p4, p3x = moved(p3, onward), moved(p3, other_core)
    q3x = moved(q3, other_core)
    five, five_x = three + [p2, q2x], three_x + [q2, p2x]
    two, two_x = [p3, q3x], [q3, p3x]
    middle = moved(call(cut_kernel, info, five[3:] + five_x[3:], slices_of(2), 1), hub_ahead(0))
    acc = call(
        lambda *refs: products_kernel(OFFSETS[:5], *refs), info, [a] + five + five_x, block_of_products, WEIGHT0
    )
    acc = call(
        lambda *refs: products_kernel(OFFSETS[5:7], *refs), info, [a] + two + two_x + [acc], block_of_products, 1
    )
    p4, near, middle, acc = wall((hold(info, p4, ROOM), near, middle, acc))

    p4x = moved(p4, other_core)
    late = moved(call(cut_kernel, info, two + [p4] + two_x + [p4x], slices_of(3), 1), hub_ahead(0))
    half_block = jax.ShapeDtypeStruct((2, 64, 1024), BF16)
    keep, send, product = call(
        last_kernel,
        info,
        [a, acc] + five + two + [p4] + five_x + two_x + [p4x],
        (half_block, half_block, block_of_products),
        WEIGHT,
        [pltpu.VMEM((2, 256, 1024), BF16)],
    )
    share = jax.ShapeDtypeStruct((1, 128), F32)
    trace = call(trace_kernel, info, [product, near, middle, late], share, 1)

    below, above = moved(trace, along(1)), moved(trace, along(-1))
    kept, sent = moved(keep, from_hub(0)), moved(send, from_hub(1))
    two, three, kept = wall((trace + above, below + trace + above, kept))
    below, above = moved(two, along(3)), moved(three, along(-3))
    trace, kept, sent = wall((below + three + above, kept, sent))
    first, second = moved(trace, from_hub(0)), moved(trace, from_hub(1))
    products = jnp.where(half == 0, jnp.stack([kept, sent]), jnp.stack([sent, kept]))[:, None, None]
    both = jnp.where(half == 0, jnp.concatenate([first, second]), jnp.concatenate([second, first]))
    correlator = jnp.sum(both[:, :16].reshape(2, 8, 2), axis=1)[:, None, None, :]
    return products, correlator


def solution(mesh):
    return jax.shard_map(
        shards,
        mesh=mesh,
        in_specs=(P(None, "tm", None, "row", None), P()),
        out_specs=(P(None, None, "tm", None, "row", None), P(None, None, "tm", None)),
        check_vma=False,
    )
```

```python
import jax
import jax.numpy as jnp
from jax import lax
from jax.experimental import pallas as pl
from jax.experimental.pallas import tpu as pltpu
from jax.sharding import PartitionSpec as P

BOTH = ("tm", "row")
BF16 = jnp.bfloat16
F32 = jnp.float32


def hub_of(s):
    m, odd = divmod(s % 16, 2)
    low, x = divmod(m, 4)
    return (1 - low) * 4 + x, odd ^ low


SERVED = {hub_of(s): s for s in range(16)}


def moved(block, route):
    def index_of(m, c, z, h):
        return ((m % 8) * 2 + c) * 16 + (z % 8) * 2 + h

    places = [(m, c, z, h) for m in range(8) for c in range(2) for z in range(8) for h in range(2)]
    return lax.ppermute(block, BOTH, [(index_of(*at), index_of(*route(*at))) for at in places])


def onward(m, c, z, h):
    return (m, c, z + (1 if c == 0 else -1), h)


def across(distance):
    return lambda m, c, z, h: (m, c, z ^ distance, h)


def other_core(m, c, z, h):
    return (m, 1 - c, z, h)


def to_hub(m, c, z, h):
    column, half = hub_of(2 * m + c)
    return (column, h, z, half)


def hub_ahead(step):
    def route(m, c, z, h):
        column, half = hub_of(SERVED[m, h] + 1 + c)
        return (column, c, z + (step if c == 0 else -step), half)

    return route


def from_hub(turn):
    def route(m, c, z, h):
        t = (SERVED[m, h] - 1 - c) % 16
        return (t // 2, t % 2, z, c ^ turn)

    return route


WEIGHT = 3_000_000_000

VMEM = pl.BlockSpec(memory_space=pltpu.VMEM)
SMEM = pl.BlockSpec(memory_space=pltpu.SMEM)


def slices_of(count):
    return jax.ShapeDtypeStruct((count, 2, 128, 128), BF16)


def call(kernel, info, arrays, out_shape, flops, scratch=()):
    outs = jax.tree.map(lambda _: VMEM, out_shape)
    return pl.pallas_call(
        kernel,
        out_shape=out_shape,
        in_specs=[SMEM] + [VMEM] * len(arrays),
        out_specs=outs,
        scratch_shapes=scratch,
        compiler_params=pltpu.CompilerParams(vmem_limit_bytes=24 * 1024 * 1024),
        cost_estimate=pl.CostEstimate(flops=flops, bytes_accessed=1 << 20, transcendentals=0),
    )(info, *arrays)


def place_of(info, offset):
    return lax.rem(info[0] + jnp.where(info[1] == 0, 8 - offset, 8 + offset), 8)


def columns_of(info, offset):
    return pl.ds(pl.multiple_of(place_of(info, offset) * 128, 128), 128)


def halves(info, own, other):
    first = jnp.where(info[1] == 0, own, other)
    second = jnp.where(info[1] == 0, other, own)
    return first, second


def whole(info, own_ref, other_ref, momentum, part):
    return jnp.concatenate(halves(info, own_ref[momentum, part], other_ref[momentum, part]), axis=0)


def cut(info, own_ref, other_ref, offset, out):
    columns = columns_of(info, offset)
    for part in range(2):
        first, second = halves(info, own_ref[info[5], part, :, columns], other_ref[info[5], part, :, columns])
        out[part] = jnp.concatenate([first, second], axis=0).T


def first_cut_kernel(info, own, other, a):
    for part in range(2):
        a[part] = whole(info, own, other, info[2], part)


def cut_kernel(info, *refs):
    count = len(refs) // 2
    for k in range(count):
        cut(info, refs[k], refs[count + k], 0, refs[-1].at[k])


def left_side(info, a_ref, offset):
    columns = columns_of(info, offset)
    real, imag = a_ref[0, :, columns], a_ref[1, :, columns]
    return jnp.concatenate(
        [jnp.concatenate([real, -imag], axis=1), jnp.concatenate([imag, real], axis=1)], axis=0
    )


def products_kernel(offsets, info, a_ref, *refs):
    count = len(offsets)
    own, other, out = refs[:count], refs[count : 2 * count], refs[-1]
    total = refs[2 * count][...] if len(refs) > 2 * count + 1 else None
    for offset, one, two in zip(offsets, own, other):
        block = jnp.concatenate([whole(info, one, two, info[3], part) for part in range(2)], axis=0)
        term = jnp.dot(left_side(info, a_ref, offset), block, preferred_element_type=F32)
        total = term if total is None else total + term
    out[...] = total


OFFSETS = (0, 1, -1, 2, -2, 3, -3, 4)


def last_kernel(info, a_ref, acc, near, middle, *refs):
    own, other = refs[0:8], refs[8:16]
    keep, send, out, early, rounded_ref = refs[16:21]
    block = jnp.concatenate([whole(info, own[7], other[7], info[3], part) for part in range(2)], axis=0)
    product = acc[...] + jnp.dot(left_side(info, a_ref, 4), block, preferred_element_type=F32)
    rounded = product.astype(BF16)
    for part in range(2):
        rounded_ref[part] = rounded[part * 128 : part * 128 + 128]
        low, high = rounded[part * 128 : part * 128 + 64], rounded[part * 128 + 64 : part * 128 + 128]
        keep[part], send[part] = halves(info, low, high)
    total = None
    for offset, one, two in zip(OFFSETS, own, other):
        block = jnp.concatenate([whole(info, one, two, info[4], part) for part in range(2)], axis=0)
        term = jnp.dot(left_side(info, rounded_ref, offset), block, preferred_element_type=F32)
        total = term if total is None else total + term
    out[...] = total
    slices = [near.at[0], near.at[1], near.at[2], middle.at[0], middle.at[1]]
    early[0:1, :], early[1:2, :] = trace_sum(info, out, list(zip(OFFSETS, slices)))


def trace_sum(info, product, slices):
    re = im = None
    for offset, piece in slices:
        columns = columns_of(info, offset)
        q_re, q_im = product[0:128, columns], product[128:256, columns]
        d_re, d_im = piece[0].astype(F32), piece[1].astype(F32)
        more_re, more_im = q_re * d_re - q_im * d_im, q_re * d_im + q_im * d_re
        re = more_re if re is None else re + more_re
        im = more_im if im is None else im + more_im
    return [jnp.sum(part, axis=0, keepdims=True) for part in (re, im)]


def trace_kernel(info, product, early, late, trace):
    re, im = trace_sum(info, product, [(3, late.at[0]), (-3, late.at[1]), (4, late.at[2])])
    re = jnp.sum(re + early[0:1, :], axis=1, keepdims=True)
    im = jnp.sum(im + early[1:2, :], axis=1, keepdims=True)
    lane = lax.broadcasted_iota(jnp.int32, (1, 128), 1)
    trace[...] = jnp.where(lane == 2 * info[0], re, jnp.where(lane == 2 * info[0] + 1, im, 0.0))


def shards(fields, mom_table):
    rows = fields[:, 0]
    tm, row = lax.axis_index("tm"), lax.axis_index("row")
    core, place, half = tm % 2, row // 2, row % 2
    momenta = lax.dynamic_index_in_dim(mom_table, core, 0, keepdims=False)[0]
    info = jnp.concatenate([jnp.stack([place, core]), momenta])
    wall = lax.optimization_barrier
    block_of_products = jax.ShapeDtypeStruct((256, 1024), F32)

    own = moved(rows, to_hub)

    ownx, p1 = moved(own, other_core), moved(own, onward)
    q1 = moved(ownx, onward)
    a = call(first_cut_kernel, info, [own, ownx], jax.ShapeDtypeStruct((2, 128, 1024), BF16), 1)
    a = moved(a, hub_ahead(0))

    p2, p1x = moved(p1, onward), moved(p1, other_core)
    q2, q1x = moved(q1, onward), moved(q1, other_core)
    three, three_x = [own, p1, q1x], [ownx, q1, p1x]
    near = call(cut_kernel, info, three + three_x, slices_of(3), 1)
    acc = call(lambda *refs: products_kernel(OFFSETS[:1], *refs), info, [a, own, ownx], block_of_products, WEIGHT)
    p2, a, acc = wall((p2, a, acc))

    near = moved(near, hub_ahead(0))
    p3, p2x = moved(p2, onward), moved(p2, other_core)
    q3, q2x = moved(q2, onward), moved(q2, other_core)
    p3, near = wall((p3, near))

    p4, p3x = moved(p3, onward), moved(p3, other_core)
    five, five_x = three + [p2, q2x], three_x + [q2, p2x]
    middle = moved(call(cut_kernel, info, five[3:] + five_x[3:], slices_of(2), 1), hub_ahead(0))
    acc = call(
        lambda *refs: products_kernel(OFFSETS[1:5], *refs), info, [a] + five[1:] + five_x[1:] + [acc], block_of_products, 1
    )
    q3, acc = wall((q3, acc))

    q3x = moved(q3, other_core)
    p4, middle = wall((p4, middle))

    p4x = moved(p4, other_core)
    two, two_x = [p3, q3x], [q3, p3x]
    acc = call(
        lambda *refs: products_kernel(OFFSETS[5:7], *refs), info, [a] + two + two_x + [acc], block_of_products, 1
    )
    late = moved(call(cut_kernel, info, two + [p4] + two_x + [p4x], slices_of(3), 1), hub_ahead(0))
    half_block = jax.ShapeDtypeStruct((2, 64, 1024), BF16)
    keep, send, product, early = call(
        last_kernel,
        info,
        [a, acc, near, middle] + five + two + [p4] + five_x + two_x + [p4x],
        (half_block, half_block, block_of_products, jax.ShapeDtypeStruct((8, 128), F32)),
        WEIGHT,
        [pltpu.VMEM((2, 128, 1024), BF16)],
    )
    trace = call(trace_kernel, info, [product, early, late], jax.ShapeDtypeStruct((1, 128), F32), WEIGHT)

    kept, sent = moved(keep, from_hub(0)), moved(send, from_hub(1))
    trace = trace + moved(trace, across(1))
    trace = trace + moved(trace, across(2))
    trace, kept = wall((trace, kept))
    trace = trace + moved(trace, across(4))
    trace, sent = wall((trace, sent))
    first, second = moved(trace, from_hub(0)), moved(trace, from_hub(1))
    products = jnp.where(half == 0, jnp.stack([kept, sent]), jnp.stack([sent, kept]))[:, None, None]
    both = jnp.where(half == 0, jnp.concatenate([first, second]), jnp.concatenate([second, first]))
    correlator = jnp.sum(both[:, :16].reshape(2, 8, 2), axis=1)[:, None, None, :] / F32(1024)
    return products, correlator


def solution(mesh):
    return jax.shard_map(
        shards,
        mesh=mesh,
        in_specs=(P(None, "tm", None, "row", None), P()),
        out_specs=(P(None, None, "tm", None, "row", None), P(None, None, "tm", None)),
        check_vma=False,
    )
```

```python
import jax
import jax.numpy as jnp
from jax import lax
from jax.experimental import pallas as pl
from jax.experimental.pallas import tpu as pltpu
from jax.sharding import PartitionSpec as P

BOTH = ("tm", "row")
BF16 = jnp.bfloat16
F32 = jnp.float32


def hub_of(s):
    m, odd = divmod(s % 16, 2)
    low, x = divmod(m, 4)
    return (1 - low) * 4 + x, odd ^ low


SERVED = {hub_of(s): s for s in range(16)}


def moved(block, route):
    def index_of(m, c, z, h):
        return ((m % 8) * 2 + c) * 16 + (z % 8) * 2 + h

    places = [(m, c, z, h) for m in range(8) for c in range(2) for z in range(8) for h in range(2)]
    return lax.ppermute(block, BOTH, [(index_of(*at), index_of(*route(*at))) for at in places])


def onward(m, c, z, h):
    return (m, c, z + (1 if c == 0 else -1), h)


def along(step):
    return lambda m, c, z, h: (m, c, z + step, h)


def other_core(m, c, z, h):
    return (m, 1 - c, z, h)


def to_hub(m, c, z, h):
    column, half = hub_of(2 * m + c)
    return (column, h, z, half)


def hub_ahead(step):
    def route(m, c, z, h):
        column, half = hub_of(SERVED[m, h] + 1 + c)
        return (column, c, z + (step if c == 0 else -step), half)

    return route


def from_hub(turn):
    def route(m, c, z, h):
        t = (SERVED[m, h] - 1 - c) % 16
        return (t // 2, t % 2, z, c ^ turn)

    return route


WEIGHT = 3_000_000_000

VMEM = pl.BlockSpec(memory_space=pltpu.VMEM)
SMEM = pl.BlockSpec(memory_space=pltpu.SMEM)


def slices_of(count):
    return jax.ShapeDtypeStruct((count, 2, 128, 128), BF16)


def call(kernel, info, arrays, out_shape, flops, scratch=()):
    outs = jax.tree.map(lambda _: VMEM, out_shape)
    return pl.pallas_call(
        kernel,
        out_shape=out_shape,
        in_specs=[SMEM] + [VMEM] * len(arrays),
        out_specs=outs,
        scratch_shapes=scratch,
        compiler_params=pltpu.CompilerParams(vmem_limit_bytes=24 * 1024 * 1024),
        cost_estimate=pl.CostEstimate(flops=flops, bytes_accessed=1 << 20, transcendentals=0),
    )(info, *arrays)


def place_of(info, offset):
    return lax.rem(info[0] + jnp.where(info[1] == 0, 8 - offset, 8 + offset), 8)


def columns_of(info, offset):
    return pl.ds(pl.multiple_of(place_of(info, offset) * 128, 128), 128)


def halves(info, own, other):
    first = jnp.where(info[1] == 0, own, other)
    second = jnp.where(info[1] == 0, other, own)
    return first, second


def whole(info, own_ref, other_ref, momentum, part):
    return jnp.concatenate(halves(info, own_ref[momentum, part], other_ref[momentum, part]), axis=0)


def cut(info, own_ref, other_ref, offset, out):
    columns = columns_of(info, offset)
    for part in range(2):
        first, second = halves(info, own_ref[info[5], part, :, columns], other_ref[info[5], part, :, columns])
        out[part] = jnp.concatenate([first, second], axis=0).T


def first_cut_kernel(info, own, other, a):
    for part in range(2):
        a[part] = whole(info, own, other, info[2], part)


def cut_kernel(info, *refs):
    count = len(refs) // 2
    for k in range(count):
        cut(info, refs[k], refs[count + k], 0, refs[-1].at[k])


def left_side(info, a_ref, offset):
    columns = columns_of(info, offset)
    real, imag = a_ref[0, :, columns], a_ref[1, :, columns]
    return jnp.concatenate(
        [jnp.concatenate([real, -imag], axis=1), jnp.concatenate([imag, real], axis=1)], axis=0
    )


def products_kernel(offsets, info, a_ref, *refs):
    count = len(offsets)
    own, other, out = refs[:count], refs[count : 2 * count], refs[-1]
    total = refs[2 * count][...] if len(refs) > 2 * count + 1 else None
    for offset, one, two in zip(offsets, own, other):
        block = jnp.concatenate([whole(info, one, two, info[3], part) for part in range(2)], axis=0)
        term = jnp.dot(left_side(info, a_ref, offset), block, preferred_element_type=F32)
        total = term if total is None else total + term
    out[...] = total


OFFSETS = (0, 1, -1, 2, -2, 3, -3, 4)


def last_kernel(info, a_ref, acc, near, middle, *refs):
    own, other = refs[0:8], refs[8:16]
    keep, send, out, early, rounded_ref = refs[16:21]
    block = jnp.concatenate([whole(info, own[7], other[7], info[3], part) for part in range(2)], axis=0)
    product = acc[...] + jnp.dot(left_side(info, a_ref, 4), block, preferred_element_type=F32)
    rounded = product.astype(BF16)
    for part in range(2):
        rounded_ref[part] = rounded[part * 128 : part * 128 + 128]
        low, high = rounded[part * 128 : part * 128 + 64], rounded[part * 128 + 64 : part * 128 + 128]
        keep[part], send[part] = halves(info, low, high)
    total = None
    for offset, one, two in zip(OFFSETS, own, other):
        block = jnp.concatenate([whole(info, one, two, info[4], part) for part in range(2)], axis=0)
        term = jnp.dot(left_side(info, rounded_ref, offset), block, preferred_element_type=F32)
        total = term if total is None else total + term
    out[...] = total
    slices = [near.at[0], near.at[1], near.at[2], middle.at[0], middle.at[1]]
    early[0:1, :], early[1:2, :] = trace_sum(info, out, list(zip(OFFSETS, slices)))


def trace_sum(info, product, slices):
    re = im = None
    for offset, piece in slices:
        columns = columns_of(info, offset)
        q_re, q_im = product[0:128, columns], product[128:256, columns]
        d_re, d_im = piece[0].astype(F32), piece[1].astype(F32)
        more_re, more_im = q_re * d_re - q_im * d_im, q_re * d_im + q_im * d_re
        re = more_re if re is None else re + more_re
        im = more_im if im is None else im + more_im
    return [jnp.sum(part, axis=0, keepdims=True) for part in (re, im)]


def trace_kernel(info, product, early, late, trace):
    re, im = trace_sum(info, product, [(3, late.at[0]), (-3, late.at[1]), (4, late.at[2])])
    re = jnp.sum(re + early[0:1, :], axis=1, keepdims=True)
    im = jnp.sum(im + early[1:2, :], axis=1, keepdims=True)
    lane = lax.broadcasted_iota(jnp.int32, (1, 128), 1)
    trace[...] = jnp.where(lane == 2 * info[0], re, jnp.where(lane == 2 * info[0] + 1, im, 0.0))


def shards(fields, mom_table):
    rows = fields[:, 0]
    tm, row = lax.axis_index("tm"), lax.axis_index("row")
    core, place, half = tm % 2, row // 2, row % 2
    momenta = lax.dynamic_index_in_dim(mom_table, core, 0, keepdims=False)[0]
    info = jnp.concatenate([jnp.stack([place, core]), momenta])
    wall = lax.optimization_barrier
    block_of_products = jax.ShapeDtypeStruct((256, 1024), F32)

    own = moved(rows, to_hub)

    ownx, p1 = moved(own, other_core), moved(own, onward)
    q1 = moved(ownx, onward)
    a = call(first_cut_kernel, info, [own, ownx], jax.ShapeDtypeStruct((2, 128, 1024), BF16), 1)
    a = moved(a, hub_ahead(0))

    p2, p1x = moved(p1, onward), moved(p1, other_core)
    q2, q1x = moved(q1, onward), moved(q1, other_core)
    three, three_x = [own, p1, q1x], [ownx, q1, p1x]
    near = call(cut_kernel, info, three + three_x, slices_of(3), 1)
    acc = call(lambda *refs: products_kernel(OFFSETS[:1], *refs), info, [a, own, ownx], block_of_products, WEIGHT)
    p2, a, acc = wall((p2, a, acc))

    near = moved(near, hub_ahead(0))
    p3, p2x = moved(p2, onward), moved(p2, other_core)
    q3, q2x = moved(q2, onward), moved(q2, other_core)
    p3, near = wall((p3, near))

    p4, p3x = moved(p3, onward), moved(p3, other_core)
    five, five_x = three + [p2, q2x], three_x + [q2, p2x]
    middle = moved(call(cut_kernel, info, five[3:] + five_x[3:], slices_of(2), 1), hub_ahead(0))
    acc = call(
        lambda *refs: products_kernel(OFFSETS[1:5], *refs), info, [a] + five[1:] + five_x[1:] + [acc], block_of_products, 1
    )
    q3, acc = wall((q3, acc))

    q3x = moved(q3, other_core)
    p4, middle = wall((p4, middle))

    p4x = moved(p4, other_core)
    two, two_x = [p3, q3x], [q3, p3x]
    acc = call(
        lambda *refs: products_kernel(OFFSETS[5:7], *refs), info, [a] + two + two_x + [acc], block_of_products, 1
    )
    late = moved(call(cut_kernel, info, two + [p4] + two_x + [p4x], slices_of(3), 1), hub_ahead(0))
    half_block = jax.ShapeDtypeStruct((2, 64, 1024), BF16)
    keep, send, product, early = call(
        last_kernel,
        info,
        [a, acc, near, middle] + five + two + [p4] + five_x + two_x + [p4x],
        (half_block, half_block, block_of_products, jax.ShapeDtypeStruct((8, 128), F32)),
        WEIGHT,
        [pltpu.VMEM((2, 128, 1024), BF16)],
    )
    trace = call(trace_kernel, info, [product, early, late], jax.ShapeDtypeStruct((1, 128), F32), WEIGHT)

    kept, sent = moved(keep, from_hub(0)), moved(send, from_hub(1))
    first, second = moved(trace, from_hub(0)), moved(trace, from_hub(1))
    both = jnp.where(half == 0, jnp.concatenate([first, second]), jnp.concatenate([second, first]))
    below, above = moved(both, along(1)), moved(both, along(-1))
    two, three, kept = wall((both + above, below + both + above, kept))
    below, above = moved(two, along(3)), moved(three, along(-3))
    both = below + three + above
    products = jnp.where(half == 0, jnp.stack([kept, sent]), jnp.stack([sent, kept]))[:, None, None]
    correlator = jnp.sum(both[:, :16].reshape(2, 8, 2), axis=1)[:, None, None, :] / F32(1024)
    return products, correlator


def solution(mesh):
    return jax.shard_map(
        shards,
        mesh=mesh,
        in_specs=(P(None, "tm", None, "row", None), P()),
        out_specs=(P(None, None, "tm", None, "row", None), P(None, None, "tm", None)),
        check_vma=False,
    )
```

```python
import jax
import jax.numpy as jnp
from jax import lax
from jax.experimental import pallas as pl
from jax.experimental.pallas import tpu as pltpu
from jax.sharding import PartitionSpec as P

BOTH = ("tm", "row")
BF16 = jnp.bfloat16
F32 = jnp.float32


def hub_of(s):
    m, odd = divmod(s % 16, 2)
    low, x = divmod(m, 4)
    return (1 - low) * 4 + x, odd ^ low


SERVED = {hub_of(s): s for s in range(16)}


def moved(block, route):
    def index_of(m, c, z, h):
        return ((m % 8) * 2 + c) * 16 + (z % 8) * 2 + h

    places = [(m, c, z, h) for m in range(8) for c in range(2) for z in range(8) for h in range(2)]
    return lax.ppermute(block, BOTH, [(index_of(*at), index_of(*route(*at))) for at in places])


def onward(m, c, z, h):
    return (m, c, z + (1 if c == 0 else -1), h)


def along(step):
    return lambda m, c, z, h: (m, c, z + step, h)


def other_core(m, c, z, h):
    return (m, 1 - c, z, h)


def to_hub(m, c, z, h):
    column, half = hub_of(2 * m + c)
    return (column, h, z, half)


def hub_ahead(step):
    def route(m, c, z, h):
        column, half = hub_of(SERVED[m, h] + 1 + c)
        return (column, c, z + (step if c == 0 else -step), half)

    return route


def from_hub(turn):
    def route(m, c, z, h):
        t = (SERVED[m, h] - 1 - c) % 16
        return (t // 2, t % 2, z, c ^ turn)

    return route


WEIGHT = 3_000_000_000

VMEM = pl.BlockSpec(memory_space=pltpu.VMEM)
SMEM = pl.BlockSpec(memory_space=pltpu.SMEM)


def slices_of(count):
    return jax.ShapeDtypeStruct((count, 2, 128, 128), BF16)


def call(kernel, info, arrays, out_shape, flops, scratch=()):
    outs = jax.tree.map(lambda _: VMEM, out_shape)
    return pl.pallas_call(
        kernel,
        out_shape=out_shape,
        in_specs=[SMEM] + [VMEM] * len(arrays),
        out_specs=outs,
        scratch_shapes=scratch,
        compiler_params=pltpu.CompilerParams(vmem_limit_bytes=24 * 1024 * 1024),
        cost_estimate=pl.CostEstimate(flops=flops, bytes_accessed=1 << 20, transcendentals=0),
    )(info, *arrays)


def place_of(info, offset):
    return lax.rem(info[0] + jnp.where(info[1] == 0, 8 - offset, 8 + offset), 8)


def columns_of(info, offset):
    return pl.ds(pl.multiple_of(place_of(info, offset) * 128, 128), 128)


def halves(info, own, other):
    first = jnp.where(info[1] == 0, own, other)
    second = jnp.where(info[1] == 0, other, own)
    return first, second


def whole(info, own_ref, other_ref, momentum, part):
    return jnp.concatenate(halves(info, own_ref[momentum, part], other_ref[momentum, part]), axis=0)


def cut(info, own_ref, other_ref, offset, out):
    columns = columns_of(info, offset)
    for part in range(2):
        first, second = halves(info, own_ref[info[5], part, :, columns], other_ref[info[5], part, :, columns])
        out[part] = jnp.concatenate([first, second], axis=0).T


def first_cut_kernel(info, own, other, a):
    for part in range(2):
        a[part] = whole(info, own, other, info[2], part)


def cut_kernel(info, *refs):
    count = len(refs) // 2
    for k in range(count):
        cut(info, refs[k], refs[count + k], 0, refs[-1].at[k])


def left_side(info, a_ref, offset):
    columns = columns_of(info, offset)
    real, imag = a_ref[0, :, columns], a_ref[1, :, columns]
    return jnp.concatenate(
        [jnp.concatenate([real, -imag], axis=1), jnp.concatenate([imag, real], axis=1)], axis=0
    )


def products_kernel(offsets, info, a_ref, *refs):
    count = len(offsets)
    own, other, out = refs[:count], refs[count : 2 * count], refs[-1]
    total = refs[2 * count][...] if len(refs) > 2 * count + 1 else None
    for offset, one, two in zip(offsets, own, other):
        block = jnp.concatenate([whole(info, one, two, info[3], part) for part in range(2)], axis=0)
        term = jnp.dot(left_side(info, a_ref, offset), block, preferred_element_type=F32)
        total = term if total is None else total + term
    out[...] = total


OFFSETS = (0, 1, -1, 2, -2, 3, -3, 4)


def last_kernel(info, a_ref, acc, near, middle, *refs):
    own, other = refs[0:8], refs[8:16]
    keep, send, out, early, rounded_ref = refs[16:21]
    block = jnp.concatenate([whole(info, own[7], other[7], info[3], part) for part in range(2)], axis=0)
    product = acc[...] + jnp.dot(left_side(info, a_ref, 4), block, preferred_element_type=F32)
    rounded = product.astype(BF16)
    for part in range(2):
        rounded_ref[part] = rounded[part * 128 : part * 128 + 128]
        low, high = rounded[part * 128 : part * 128 + 64], rounded[part * 128 + 64 : part * 128 + 128]
        keep[part], send[part] = halves(info, low, high)
    total = None
    for offset, one, two in zip(OFFSETS, own, other):
        block = jnp.concatenate([whole(info, one, two, info[4], part) for part in range(2)], axis=0)
        term = jnp.dot(left_side(info, rounded_ref, offset), block, preferred_element_type=F32)
        total = term if total is None else total + term
    out[...] = total
    slices = [near.at[0], near.at[1], near.at[2], middle.at[0], middle.at[1]]
    early[0:1, :], early[1:2, :] = trace_sum(info, out, list(zip(OFFSETS, slices)))


def trace_sum(info, product, slices):
    re = im = None
    for offset, piece in slices:
        columns = columns_of(info, offset)
        q_re, q_im = product[0:128, columns], product[128:256, columns]
        d_re, d_im = piece[0].astype(F32), piece[1].astype(F32)
        more_re, more_im = q_re * d_re - q_im * d_im, q_re * d_im + q_im * d_re
        re = more_re if re is None else re + more_re
        im = more_im if im is None else im + more_im
    return [jnp.sum(part, axis=0, keepdims=True) for part in (re, im)]


def trace_kernel(info, product, early, late, trace):
    re, im = trace_sum(info, product, [(3, late.at[0]), (-3, late.at[1]), (4, late.at[2])])
    re = jnp.sum(re + early[0:1, :], axis=1, keepdims=True)
    im = jnp.sum(im + early[1:2, :], axis=1, keepdims=True)
    lane = lax.broadcasted_iota(jnp.int32, (1, 128), 1)
    trace[...] = jnp.where(lane == 2 * info[0], re, jnp.where(lane == 2 * info[0] + 1, im, 0.0))


def shards(fields, mom_table):
    rows = fields[:, 0]
    tm, row = lax.axis_index("tm"), lax.axis_index("row")
    core, place, half = tm % 2, row // 2, row % 2
    momenta = lax.dynamic_index_in_dim(mom_table, core, 0, keepdims=False)[0]
    info = jnp.concatenate([jnp.stack([place, core]), momenta])
    wall = lax.optimization_barrier
    block_of_products = jax.ShapeDtypeStruct((256, 1024), F32)

    own = moved(rows, to_hub)

    ownx, p1 = moved(own, other_core), moved(own, onward)
    q1 = moved(ownx, onward)
    a = call(first_cut_kernel, info, [own, ownx], jax.ShapeDtypeStruct((2, 128, 1024), BF16), 1)
    a = moved(a, hub_ahead(0))

    p2, p1x = moved(p1, onward), moved(p1, other_core)
    q2, q1x = moved(q1, onward), moved(q1, other_core)
    three, three_x = [own, p1, q1x], [ownx, q1, p1x]
    near = call(cut_kernel, info, three + three_x, slices_of(3), 1)
    acc = call(lambda *refs: products_kernel(OFFSETS[:1], *refs), info, [a, own, ownx], block_of_products, WEIGHT)
    p2, a, acc = wall((p2, a, acc))

    near = moved(near, hub_ahead(0))
    p3, p2x = moved(p2, onward), moved(p2, other_core)
    q3, q2x = moved(q2, onward), moved(q2, other_core)
    p3, near = wall((p3, near))

    p4, p3x = moved(p3, onward), moved(p3, other_core)
    five, five_x = three + [p2, q2x], three_x + [q2, p2x]
    middle = moved(call(cut_kernel, info, five[3:] + five_x[3:], slices_of(2), 1), hub_ahead(0))
    acc = call(
        lambda *refs: products_kernel(OFFSETS[1:5], *refs), info, [a] + five[1:] + five_x[1:] + [acc], block_of_products, 1
    )
    q3, acc = wall((q3, acc))

    q3x = moved(q3, other_core)
    p4, middle = wall((p4, middle))

    p4x = moved(p4, other_core)
    two, two_x = [p3, q3x], [q3, p3x]
    acc = call(
        lambda *refs: products_kernel(OFFSETS[5:7], *refs), info, [a] + two + two_x + [acc], block_of_products, 1
    )
    late = moved(call(cut_kernel, info, two + [p4] + two_x + [p4x], slices_of(3), 1), hub_ahead(0))
    half_block = jax.ShapeDtypeStruct((2, 64, 1024), BF16)
    keep, send, product, early = call(
        last_kernel,
        info,
        [a, acc, near, middle] + five + two + [p4] + five_x + two_x + [p4x],
        (half_block, half_block, block_of_products, jax.ShapeDtypeStruct((8, 128), F32)),
        WEIGHT,
        [pltpu.VMEM((2, 128, 1024), BF16)],
    )
    trace = call(trace_kernel, info, [product, early, late], jax.ShapeDtypeStruct((1, 128), F32), WEIGHT)

    kept, sent = moved(keep, from_hub(0)), moved(send, from_hub(1))
    first, second = moved(trace, from_hub(0)), moved(trace, from_hub(1))
    both = jnp.where(half == 0, jnp.concatenate([first, second]), jnp.concatenate([second, first]))
    both, kept = wall((both, kept))
    below, above = moved(both, along(1)), moved(both, along(-1))
    two, three = both + above, below + both + above
    below, above = moved(two, along(3)), moved(three, along(-3))
    both = below + three + above
    products = jnp.where(half == 0, jnp.stack([kept, sent]), jnp.stack([sent, kept]))[:, None, None]
    correlator = jnp.sum(both[:, :16].reshape(2, 8, 2), axis=1)[:, None, None, :] / F32(1024)
    return products, correlator


def solution(mesh):
    return jax.shard_map(
        shards,
        mesh=mesh,
        in_specs=(P(None, "tm", None, "row", None), P()),
        out_specs=(P(None, None, "tm", None, "row", None), P(None, None, "tm", None)),
        check_vma=False,
    )
```

```python
import jax
import jax.numpy as jnp
from jax import lax
from jax.experimental import pallas as pl
from jax.experimental.pallas import tpu as pltpu
from jax.sharding import PartitionSpec as P

BOTH = ("tm", "row")
BF16 = jnp.bfloat16
F32 = jnp.float32


def hub_of(s):
    m, odd = divmod(s % 16, 2)
    low, x = divmod(m, 4)
    return (1 - low) * 4 + x, odd ^ low


SERVED = {hub_of(s): s for s in range(16)}


def moved(block, route):
    def index_of(m, c, z, h):
        return ((m % 8) * 2 + c) * 16 + (z % 8) * 2 + h

    places = [(m, c, z, h) for m in range(8) for c in range(2) for z in range(8) for h in range(2)]
    return lax.ppermute(block, BOTH, [(index_of(*at), index_of(*route(*at))) for at in places])


def onward(m, c, z, h):
    return (m, c, z + (1 if c == 0 else -1), h)


def across(distance):
    return lambda m, c, z, h: (m, c, z ^ distance, h)


def other_core(m, c, z, h):
    return (m, 1 - c, z, h)


def to_hub(m, c, z, h):
    column, half = hub_of(2 * m + c)
    return (column, h, z, half)


def hub_ahead(step):
    def route(m, c, z, h):
        column, half = hub_of(SERVED[m, h] + 1 + c)
        return (column, c, z + (step if c == 0 else -step), half)

    return route


def from_hub(turn):
    def route(m, c, z, h):
        t = (SERVED[m, h] - 1 - c) % 16
        return (t // 2, t % 2, z, c ^ turn)

    return route


WEIGHT = 3_000_000_000

VMEM = pl.BlockSpec(memory_space=pltpu.VMEM)
SMEM = pl.BlockSpec(memory_space=pltpu.SMEM)


def slices_of(count):
    return jax.ShapeDtypeStruct((count, 2, 128, 128), BF16)


def call(kernel, info, arrays, out_shape, flops, scratch=()):
    outs = jax.tree.map(lambda _: VMEM, out_shape)
    return pl.pallas_call(
        kernel,
        out_shape=out_shape,
        in_specs=[SMEM] + [VMEM] * len(arrays),
        out_specs=outs,
        scratch_shapes=scratch,
        compiler_params=pltpu.CompilerParams(vmem_limit_bytes=24 * 1024 * 1024),
        cost_estimate=pl.CostEstimate(flops=flops, bytes_accessed=1 << 20, transcendentals=0),
    )(info, *arrays)


def place_of(info, offset):
    return lax.rem(info[0] + jnp.where(info[1] == 0, 8 - offset, 8 + offset), 8)


def columns_of(info, offset):
    return pl.ds(pl.multiple_of(place_of(info, offset) * 128, 128), 128)


def halves(info, own, other):
    first = jnp.where(info[1] == 0, own, other)
    second = jnp.where(info[1] == 0, other, own)
    return first, second


def whole(info, own_ref, other_ref, momentum, part):
    return jnp.concatenate(halves(info, own_ref[momentum, part], other_ref[momentum, part]), axis=0)


def cut(info, own_ref, other_ref, offset, out):
    columns = columns_of(info, offset)
    for part in range(2):
        first, second = halves(info, own_ref[info[5], part, :, columns], other_ref[info[5], part, :, columns])
        out[part] = jnp.concatenate([first, second], axis=0).T


def first_cut_kernel(info, own, other, a):
    for part in range(2):
        a[part] = whole(info, own, other, info[2], part)


def cut_kernel(info, *refs):
    count = len(refs) // 2
    for k in range(count):
        cut(info, refs[k], refs[count + k], 0, refs[-1].at[k])


def left_side(info, a_ref, offset):
    columns = columns_of(info, offset)
    real, imag = a_ref[0, :, columns], a_ref[1, :, columns]
    return jnp.concatenate(
        [jnp.concatenate([real, -imag], axis=1), jnp.concatenate([imag, real], axis=1)], axis=0
    )


def products_kernel(offsets, info, a_ref, *refs):
    count = len(offsets)
    own, other, out = refs[:count], refs[count : 2 * count], refs[-1]
    total = refs[2 * count][...] if len(refs) > 2 * count + 1 else None
    for offset, one, two in zip(offsets, own, other):
        block = jnp.concatenate([whole(info, one, two, info[3], part) for part in range(2)], axis=0)
        term = jnp.dot(left_side(info, a_ref, offset), block, preferred_element_type=F32)
        total = term if total is None else total + term
    out[...] = total


OFFSETS = (0, 1, -1, 2, -2, 3, -3, 4)


def last_kernel(info, a_ref, acc, near, middle, *refs):
    own, other = refs[0:8], refs[8:16]
    keep, send, out, early, rounded_ref = refs[16:21]
    block = jnp.concatenate([whole(info, own[7], other[7], info[3], part) for part in range(2)], axis=0)
    product = acc[...] + jnp.dot(left_side(info, a_ref, 4), block, preferred_element_type=F32)
    rounded = product.astype(BF16)
    for part in range(2):
        rounded_ref[part] = rounded[part * 128 : part * 128 + 128]
        low, high = rounded[part * 128 : part * 128 + 64], rounded[part * 128 + 64 : part * 128 + 128]
        keep[part], send[part] = halves(info, low, high)
    total = None
    for offset, one, two in zip(OFFSETS, own, other):
        block = jnp.concatenate([whole(info, one, two, info[4], part) for part in range(2)], axis=0)
        term = jnp.dot(left_side(info, rounded_ref, offset), block, preferred_element_type=F32)
        total = term if total is None else total + term
    out[...] = total
    slices = [near.at[0], near.at[1], near.at[2], middle.at[0], middle.at[1]]
    early[0:1, :], early[1:2, :] = trace_sum(info, out, list(zip(OFFSETS, slices)))


def trace_sum(info, product, slices):
    re = im = None
    for offset, piece in slices:
        columns = columns_of(info, offset)
        q_re, q_im = product[0:128, columns], product[128:256, columns]
        d_re, d_im = piece[0].astype(F32), piece[1].astype(F32)
        more_re, more_im = q_re * d_re - q_im * d_im, q_re * d_im + q_im * d_re
        re = more_re if re is None else re + more_re
        im = more_im if im is None else im + more_im
    return [jnp.sum(part, axis=0, keepdims=True) for part in (re, im)]


def trace_kernel(info, product, early, late, trace):
    re, im = trace_sum(info, product, [(3, late.at[0]), (-3, late.at[1]), (4, late.at[2])])
    re = jnp.sum(re + early[0:1, :], axis=1, keepdims=True)
    im = jnp.sum(im + early[1:2, :], axis=1, keepdims=True)
    lane = lax.broadcasted_iota(jnp.int32, (1, 128), 1)
    trace[...] = jnp.where(lane == 2 * info[0], re, jnp.where(lane == 2 * info[0] + 1, im, 0.0))


def shards(fields, mom_table):
    rows = fields[:, 0]
    tm, row = lax.axis_index("tm"), lax.axis_index("row")
    core, place, half = tm % 2, row // 2, row % 2
    momenta = lax.dynamic_index_in_dim(mom_table, core, 0, keepdims=False)[0]
    info = jnp.concatenate([jnp.stack([place, core]), momenta])
    wall = lax.optimization_barrier
    block_of_products = jax.ShapeDtypeStruct((256, 1024), F32)

    own = moved(rows, to_hub)

    ownx, p1 = moved(own, other_core), moved(own, onward)
    q1 = moved(ownx, onward)
    a = call(first_cut_kernel, info, [own, ownx], jax.ShapeDtypeStruct((2, 128, 1024), BF16), 1)
    a = moved(a, hub_ahead(0))

    p2, p1x = moved(p1, onward), moved(p1, other_core)
    q2, q1x = moved(q1, onward), moved(q1, other_core)
    three, three_x = [own, p1, q1x], [ownx, q1, p1x]
    near = call(cut_kernel, info, three + three_x, slices_of(3), 1)
    acc = call(lambda *refs: products_kernel(OFFSETS[:1], *refs), info, [a, own, ownx], block_of_products, WEIGHT)
    p2, a, acc = wall((p2, a, acc))

    near = moved(near, hub_ahead(0))
    p3, p2x = moved(p2, onward), moved(p2, other_core)
    q3, q2x = moved(q2, onward), moved(q2, other_core)
    p3, near = wall((p3, near))

    p4, p3x = moved(p3, onward), moved(p3, other_core)
    five, five_x = three + [p2, q2x], three_x + [q2, p2x]
    middle = moved(call(cut_kernel, info, five[3:] + five_x[3:], slices_of(2), 1), hub_ahead(0))
    acc = call(
        lambda *refs: products_kernel(OFFSETS[1:5], *refs), info, [a] + five[1:] + five_x[1:] + [acc], block_of_products, 1
    )
    q3, acc = wall((q3, acc))

    q3x = moved(q3, other_core)
    p4, middle = wall((p4, middle))

    p4x = moved(p4, other_core)
    two, two_x = [p3, q3x], [q3, p3x]
    acc = call(
        lambda *refs: products_kernel(OFFSETS[5:7], *refs), info, [a] + two + two_x + [acc], block_of_products, 1
    )
    late = moved(call(cut_kernel, info, two + [p4] + two_x + [p4x], slices_of(3), 1), hub_ahead(0))
    half_block = jax.ShapeDtypeStruct((2, 64, 1024), BF16)
    keep, send, product, early = call(
        last_kernel,
        info,
        [a, acc, near, middle] + five + two + [p4] + five_x + two_x + [p4x],
        (half_block, half_block, block_of_products, jax.ShapeDtypeStruct((8, 128), F32)),
        WEIGHT,
        [pltpu.VMEM((2, 128, 1024), BF16)],
    )
    trace = call(trace_kernel, info, [product, early, late], jax.ShapeDtypeStruct((1, 128), F32), WEIGHT)

    kept, sent = moved(keep, from_hub(0)), moved(send, from_hub(1))
    first, second = moved(trace, from_hub(0)), moved(trace, from_hub(1))
    both = jnp.where(half == 0, jnp.concatenate([first, second]), jnp.concatenate([second, first]))
    both, kept = wall((both, kept))
    both, sent = wall((both + moved(both, across(1)), sent))
    both = both + moved(both, across(2))
    both = both + moved(both, across(4))
    products = jnp.where(half == 0, jnp.stack([kept, sent]), jnp.stack([sent, kept]))[:, None, None]
    correlator = jnp.sum(both[:, :16].reshape(2, 8, 2), axis=1)[:, None, None, :] / F32(1024)
    return products, correlator


def solution(mesh):
    return jax.shard_map(
        shards,
        mesh=mesh,
        in_specs=(P(None, "tm", None, "row", None), P()),
        out_specs=(P(None, None, "tm", None, "row", None), P(None, None, "tm", None)),
        check_vma=False,
    )
```

```python
import jax
import jax.numpy as jnp
from jax import lax
from jax.experimental import pallas as pl
from jax.experimental.pallas import tpu as pltpu
from jax.sharding import PartitionSpec as P

BOTH = ("tm", "row")
BF16 = jnp.bfloat16
F32 = jnp.float32


def hub_of(s):
    m, odd = divmod(s % 16, 2)
    low, x = divmod(m, 4)
    return (1 - low) * 4 + x, odd ^ low


SERVED = {hub_of(s): s for s in range(16)}


def moved(block, route):
    def index_of(m, c, z, h):
        return ((m % 8) * 2 + c) * 16 + (z % 8) * 2 + h

    places = [(m, c, z, h) for m in range(8) for c in range(2) for z in range(8) for h in range(2)]
    return lax.ppermute(block, BOTH, [(index_of(*at), index_of(*route(*at))) for at in places])


def onward(m, c, z, h):
    return (m, c, z + (1 if c == 0 else -1), h)


def along(step):
    return lambda m, c, z, h: (m, c, z + step, h)


def other_core(m, c, z, h):
    return (m, 1 - c, z, h)


def to_hub(m, c, z, h):
    column, half = hub_of(2 * m + c)
    return (column, h, z, half)


def hub_ahead(step):
    def route(m, c, z, h):
        column, half = hub_of(SERVED[m, h] + 1 + c)
        return (column, c, z + (step if c == 0 else -step), half)

    return route


def from_hub(turn):
    def route(m, c, z, h):
        t = (SERVED[m, h] - 1 - c) % 16
        return (t // 2, t % 2, z, c ^ turn)

    return route


WEIGHT = 3_000_000_000

VMEM = pl.BlockSpec(memory_space=pltpu.VMEM)
SMEM = pl.BlockSpec(memory_space=pltpu.SMEM)


def slices_of(count):
    return jax.ShapeDtypeStruct((count, 2, 128, 128), BF16)


def call(kernel, info, arrays, out_shape, flops, scratch=()):
    outs = jax.tree.map(lambda _: VMEM, out_shape)
    return pl.pallas_call(
        kernel,
        out_shape=out_shape,
        in_specs=[SMEM] + [VMEM] * len(arrays),
        out_specs=outs,
        scratch_shapes=scratch,
        compiler_params=pltpu.CompilerParams(vmem_limit_bytes=24 * 1024 * 1024),
        cost_estimate=pl.CostEstimate(flops=flops, bytes_accessed=1 << 20, transcendentals=0),
    )(info, *arrays)


def place_of(info, offset):
    return lax.rem(info[0] + jnp.where(info[1] == 0, 8 - offset, 8 + offset), 8)


def columns_of(info, offset):
    return pl.ds(pl.multiple_of(place_of(info, offset) * 128, 128), 128)


def halves(info, own, other):
    first = jnp.where(info[1] == 0, own, other)
    second = jnp.where(info[1] == 0, other, own)
    return first, second


def whole(info, own_ref, other_ref, momentum, part):
    return jnp.concatenate(halves(info, own_ref[momentum, part], other_ref[momentum, part]), axis=0)


def cut(info, own_ref, other_ref, offset, out):
    columns = columns_of(info, offset)
    for part in range(2):
        first, second = halves(info, own_ref[info[5], part, :, columns], other_ref[info[5], part, :, columns])
        out[part] = jnp.concatenate([first, second], axis=0).T


def first_cut_kernel(info, own, other, a):
    for part in range(2):
        a[part] = whole(info, own, other, info[2], part)


def cut_kernel(info, *refs):
    count = len(refs) // 2
    for k in range(count):
        cut(info, refs[k], refs[count + k], 0, refs[-1].at[k])


def left_side(info, a_ref, offset):
    columns = columns_of(info, offset)
    real, imag = a_ref[0, :, columns], a_ref[1, :, columns]
    return jnp.concatenate(
        [jnp.concatenate([real, -imag], axis=1), jnp.concatenate([imag, real], axis=1)], axis=0
    )


def products_kernel(offsets, info, a_ref, *refs):
    count = len(offsets)
    own, other, out = refs[:count], refs[count : 2 * count], refs[-1]
    total = refs[2 * count][...] if len(refs) > 2 * count + 1 else None
    for offset, one, two in zip(offsets, own, other):
        block = jnp.concatenate([whole(info, one, two, info[3], part) for part in range(2)], axis=0)
        term = jnp.dot(left_side(info, a_ref, offset), block, preferred_element_type=F32)
        total = term if total is None else total + term
    out[...] = total


OFFSETS = (0, 1, -1, 2, -2, 3, -3, 4)


def last_kernel(info, a_ref, acc, near, middle, *refs):
    own, other = refs[0:8], refs[8:16]
    keep, send, out, early, rounded_ref = refs[16:21]
    block = jnp.concatenate([whole(info, own[7], other[7], info[3], part) for part in range(2)], axis=0)
    product = acc[...] + jnp.dot(left_side(info, a_ref, 4), block, preferred_element_type=F32)
    rounded = product.astype(BF16)
    for part in range(2):
        rounded_ref[part] = rounded[part * 128 : part * 128 + 128]
        low, high = rounded[part * 128 : part * 128 + 64], rounded[part * 128 + 64 : part * 128 + 128]
        keep[part], send[part] = halves(info, low, high)
    total = None
    for offset, one, two in zip(OFFSETS, own, other):
        block = jnp.concatenate([whole(info, one, two, info[4], part) for part in range(2)], axis=0)
        term = jnp.dot(left_side(info, rounded_ref, offset), block, preferred_element_type=F32)
        total = term if total is None else total + term
    out[...] = total
    slices = [near.at[0], near.at[1], near.at[2], middle.at[0], middle.at[1]]
    early[0:1, :], early[1:2, :] = trace_sum(info, out, list(zip(OFFSETS, slices)))


def trace_sum(info, product, slices):
    re = im = None
    for offset, piece in slices:
        columns = columns_of(info, offset)
        q_re, q_im = product[0:128, columns], product[128:256, columns]
        d_re, d_im = piece[0].astype(F32), piece[1].astype(F32)
        more_re, more_im = q_re * d_re - q_im * d_im, q_re * d_im + q_im * d_re
        re = more_re if re is None else re + more_re
        im = more_im if im is None else im + more_im
    return [jnp.sum(part, axis=0, keepdims=True) for part in (re, im)]


def trace_kernel(info, product, early, late, trace):
    re, im = trace_sum(info, product, [(3, late.at[0]), (-3, late.at[1]), (4, late.at[2])])
    re = jnp.sum(re + early[0:1, :], axis=1, keepdims=True)
    im = jnp.sum(im + early[1:2, :], axis=1, keepdims=True)
    lane = lax.broadcasted_iota(jnp.int32, (1, 128), 1)
    trace[...] = jnp.where(lane == 2 * info[0], re, jnp.where(lane == 2 * info[0] + 1, im, 0.0))


def add_kernel(info, below, own, above, two, three):
    two[...] = own[...] + above[...]
    three[...] = below[...] + own[...] + above[...]


def shards(fields, mom_table):
    rows = fields[:, 0]
    tm, row = lax.axis_index("tm"), lax.axis_index("row")
    core, place, half = tm % 2, row // 2, row % 2
    momenta = lax.dynamic_index_in_dim(mom_table, core, 0, keepdims=False)[0]
    info = jnp.concatenate([jnp.stack([place, core]), momenta])
    wall = lax.optimization_barrier
    block_of_products = jax.ShapeDtypeStruct((256, 1024), F32)

    own = moved(rows, to_hub)

    ownx, p1 = moved(own, other_core), moved(own, onward)
    q1 = moved(ownx, onward)
    a = call(first_cut_kernel, info, [own, ownx], jax.ShapeDtypeStruct((2, 128, 1024), BF16), 1)
    a = moved(a, hub_ahead(0))

    p2, p1x = moved(p1, onward), moved(p1, other_core)
    q2, q1x = moved(q1, onward), moved(q1, other_core)
    three, three_x = [own, p1, q1x], [ownx, q1, p1x]
    near = call(cut_kernel, info, three + three_x, slices_of(3), 1)
    acc = call(lambda *refs: products_kernel(OFFSETS[:1], *refs), info, [a, own, ownx], block_of_products, WEIGHT)
    p2, a, acc = wall((p2, a, acc))

    near = moved(near, hub_ahead(0))
    p3, p2x = moved(p2, onward), moved(p2, other_core)
    q3, q2x = moved(q2, onward), moved(q2, other_core)
    p3, near = wall((p3, near))

    p4, p3x = moved(p3, onward), moved(p3, other_core)
    five, five_x = three + [p2, q2x], three_x + [q2, p2x]
    middle = moved(call(cut_kernel, info, five[3:] + five_x[3:], slices_of(2), 1), hub_ahead(0))
    acc = call(
        lambda *refs: products_kernel(OFFSETS[1:5], *refs), info, [a] + five[1:] + five_x[1:] + [acc], block_of_products, 1
    )
    q3, acc = wall((q3, acc))

    q3x = moved(q3, other_core)
    p4, middle = wall((p4, middle))

    p4x = moved(p4, other_core)
    two, two_x = [p3, q3x], [q3, p3x]
    acc = call(
        lambda *refs: products_kernel(OFFSETS[5:7], *refs), info, [a] + two + two_x + [acc], block_of_products, 1
    )
    late = moved(call(cut_kernel, info, two + [p4] + two_x + [p4x], slices_of(3), 1), hub_ahead(0))
    half_block = jax.ShapeDtypeStruct((2, 64, 1024), BF16)
    keep, send, product, early = call(
        last_kernel,
        info,
        [a, acc, near, middle] + five + two + [p4] + five_x + two_x + [p4x],
        (half_block, half_block, block_of_products, jax.ShapeDtypeStruct((8, 128), F32)),
        WEIGHT,
        [pltpu.VMEM((2, 128, 1024), BF16)],
    )
    trace = call(trace_kernel, info, [product, early, late], jax.ShapeDtypeStruct((1, 128), F32), WEIGHT)

    kept, sent = moved(keep, from_hub(0)), moved(send, from_hub(1))
    first, second = moved(trace, from_hub(0)), moved(trace, from_hub(1))
    both = jnp.where(half == 0, jnp.concatenate([first, second]), jnp.concatenate([second, first]))
    both, kept = wall((both, kept))
    below, above = moved(both, along(1)), moved(both, along(-1))
    pair = jax.ShapeDtypeStruct((2, 128), F32)
    two, three = call(add_kernel, info, [below, both, above], (pair, pair), WEIGHT)
    below, above = moved(two, along(3)), moved(three, along(-3))
    both = below + three + above
    products = jnp.where(half == 0, jnp.stack([kept, sent]), jnp.stack([sent, kept]))[:, None, None]
    correlator = jnp.sum(both[:, :16].reshape(2, 8, 2), axis=1)[:, None, None, :] / F32(1024)
    return products, correlator


def solution(mesh):
    return jax.shard_map(
        shards,
        mesh=mesh,
        in_specs=(P(None, "tm", None, "row", None), P()),
        out_specs=(P(None, None, "tm", None, "row", None), P(None, None, "tm", None)),
        check_vma=False,
    )
```

```python
import jax
import jax.numpy as jnp
from jax import lax
from jax.experimental import pallas as pl
from jax.experimental.pallas import tpu as pltpu
from jax.sharding import PartitionSpec as P

BOTH = ("tm", "row")
BF16 = jnp.bfloat16
F32 = jnp.float32


def hub_of(s):
    m, odd = divmod(s % 16, 2)
    low, x = divmod(m, 4)
    return (1 - low) * 4 + x, odd ^ low


SERVED = {hub_of(s): s for s in range(16)}


def moved(block, route):
    def index_of(m, c, z, h):
        return ((m % 8) * 2 + c) * 16 + (z % 8) * 2 + h

    places = [(m, c, z, h) for m in range(8) for c in range(2) for z in range(8) for h in range(2)]
    return lax.ppermute(block, BOTH, [(index_of(*at), index_of(*route(*at))) for at in places])


def onward(m, c, z, h):
    return (m, c, z + (1 if c == 0 else -1), h)


def along(step):
    return lambda m, c, z, h: (m, c, z + step, h)


def other_core(m, c, z, h):
    return (m, 1 - c, z, h)


def to_hub(m, c, z, h):
    column, half = hub_of(2 * m + c)
    return (column, h, z, half)


def hub_ahead(step):
    def route(m, c, z, h):
        column, half = hub_of(SERVED[m, h] + 1 + c)
        return (column, c, z + (step if c == 0 else -step), half)

    return route


def from_hub(turn):
    def route(m, c, z, h):
        t = (SERVED[m, h] - 1 - c) % 16
        return (t // 2, t % 2, z, c ^ turn)

    return route


WEIGHT = 3_000_000_000

VMEM = pl.BlockSpec(memory_space=pltpu.VMEM)
SMEM = pl.BlockSpec(memory_space=pltpu.SMEM)


def slices_of(count):
    return jax.ShapeDtypeStruct((count, 2, 128, 128), BF16)


def call(kernel, info, arrays, out_shape, flops, scratch=()):
    outs = jax.tree.map(lambda _: VMEM, out_shape)
    return pl.pallas_call(
        kernel,
        out_shape=out_shape,
        in_specs=[SMEM] + [VMEM] * len(arrays),
        out_specs=outs,
        scratch_shapes=scratch,
        compiler_params=pltpu.CompilerParams(vmem_limit_bytes=24 * 1024 * 1024),
        cost_estimate=pl.CostEstimate(flops=flops, bytes_accessed=1 << 20, transcendentals=0),
    )(info, *arrays)


def place_of(info, offset):
    return lax.rem(info[0] + jnp.where(info[1] == 0, 8 - offset, 8 + offset), 8)


def columns_of(info, offset):
    return pl.ds(pl.multiple_of(place_of(info, offset) * 128, 128), 128)


def halves(info, own, other):
    first = jnp.where(info[1] == 0, own, other)
    second = jnp.where(info[1] == 0, other, own)
    return first, second


def whole(info, own_ref, other_ref, momentum, part):
    return jnp.concatenate(halves(info, own_ref[momentum, part], other_ref[momentum, part]), axis=0)


def cut(info, own_ref, other_ref, offset, out):
    columns = columns_of(info, offset)
    for part in range(2):
        first, second = halves(info, own_ref[info[5], part, :, columns], other_ref[info[5], part, :, columns])
        out[part] = jnp.concatenate([first, second], axis=0).T


def first_cut_kernel(info, own, other, a):
    for part in range(2):
        a[part] = whole(info, own, other, info[2], part)


def cut_kernel(info, *refs):
    count = len(refs) // 2
    for k in range(count):
        cut(info, refs[k], refs[count + k], 0, refs[-1].at[k])


def left_side(info, a_ref, offset):
    columns = columns_of(info, offset)
    real, imag = a_ref[0, :, columns], a_ref[1, :, columns]
    return jnp.concatenate(
        [jnp.concatenate([real, -imag], axis=1), jnp.concatenate([imag, real], axis=1)], axis=0
    )


def products_kernel(offsets, info, a_ref, *refs):
    count = len(offsets)
    own, other, out = refs[:count], refs[count : 2 * count], refs[-1]
    total = refs[2 * count][...] if len(refs) > 2 * count + 1 else None
    for offset, one, two in zip(offsets, own, other):
        block = jnp.concatenate([whole(info, one, two, info[3], part) for part in range(2)], axis=0)
        term = jnp.dot(left_side(info, a_ref, offset), block, preferred_element_type=F32)
        total = term if total is None else total + term
    out[...] = total


OFFSETS = (0, 1, -1, 2, -2, 3, -3, 4)


def last_kernel(info, a_ref, acc, near, middle, *refs):
    own, other = refs[0:8], refs[8:16]
    keep, send, out, early, rounded_ref = refs[16:21]
    block = jnp.concatenate([whole(info, own[7], other[7], info[3], part) for part in range(2)], axis=0)
    product = acc[...] + jnp.dot(left_side(info, a_ref, 4), block, preferred_element_type=F32)
    rounded = product.astype(BF16)
    for part in range(2):
        rounded_ref[part] = rounded[part * 128 : part * 128 + 128]
        low, high = rounded[part * 128 : part * 128 + 64], rounded[part * 128 + 64 : part * 128 + 128]
        keep[part], send[part] = halves(info, low, high)
    total = None
    for offset, one, two in zip(OFFSETS, own, other):
        block = jnp.concatenate([whole(info, one, two, info[4], part) for part in range(2)], axis=0)
        term = jnp.dot(left_side(info, rounded_ref, offset), block, preferred_element_type=F32)
        total = term if total is None else total + term
    out[...] = total
    slices = [near.at[0], near.at[1], near.at[2], middle.at[0], middle.at[1]]
    early[0:1, :], early[1:2, :] = trace_sum(info, out, list(zip(OFFSETS, slices)))


def trace_sum(info, product, slices):
    re = im = None
    for offset, piece in slices:
        columns = columns_of(info, offset)
        q_re, q_im = product[0:128, columns], product[128:256, columns]
        d_re, d_im = piece[0].astype(F32), piece[1].astype(F32)
        more_re, more_im = q_re * d_re - q_im * d_im, q_re * d_im + q_im * d_re
        re = more_re if re is None else re + more_re
        im = more_im if im is None else im + more_im
    return [jnp.sum(part, axis=0, keepdims=True) for part in (re, im)]


def trace_kernel(info, product, early, late, trace):
    re, im = trace_sum(info, product, [(3, late.at[0]), (-3, late.at[1]), (4, late.at[2])])
    re = jnp.sum(re + early[0:1, :], axis=1, keepdims=True)
    im = jnp.sum(im + early[1:2, :], axis=1, keepdims=True)
    lane = lax.broadcasted_iota(jnp.int32, (1, 128), 1)
    trace[...] = jnp.where(lane == 2 * info[0], re, jnp.where(lane == 2 * info[0] + 1, im, 0.0))


def add_kernel(info, below, own, above, two, three):
    two[...] = below[...] + own[...]
    three[...] = below[...] + own[...] + above[...]


def shards(fields, mom_table):
    rows = fields[:, 0]
    tm, row = lax.axis_index("tm"), lax.axis_index("row")
    core, place, half = tm % 2, row // 2, row % 2
    momenta = lax.dynamic_index_in_dim(mom_table, core, 0, keepdims=False)[0]
    info = jnp.concatenate([jnp.stack([place, core]), momenta])
    wall = lax.optimization_barrier
    block_of_products = jax.ShapeDtypeStruct((256, 1024), F32)

    own = moved(rows, to_hub)

    ownx, p1 = moved(own, other_core), moved(own, onward)
    q1 = moved(ownx, onward)
    a = call(first_cut_kernel, info, [own, ownx], jax.ShapeDtypeStruct((2, 128, 1024), BF16), 1)
    a = moved(a, hub_ahead(0))

    p2, p1x = moved(p1, onward), moved(p1, other_core)
    q2, q1x = moved(q1, onward), moved(q1, other_core)
    three, three_x = [own, p1, q1x], [ownx, q1, p1x]
    near = call(cut_kernel, info, three + three_x, slices_of(3), 1)
    acc = call(lambda *refs: products_kernel(OFFSETS[:1], *refs), info, [a, own, ownx], block_of_products, WEIGHT)
    p2, a, acc = wall((p2, a, acc))

    near = moved(near, hub_ahead(0))
    p3, p2x = moved(p2, onward), moved(p2, other_core)
    q3, q2x = moved(q2, onward), moved(q2, other_core)
    p3, near = wall((p3, near))

    p4, p3x = moved(p3, onward), moved(p3, other_core)
    five, five_x = three + [p2, q2x], three_x + [q2, p2x]
    middle = moved(call(cut_kernel, info, five[3:] + five_x[3:], slices_of(2), 1), hub_ahead(0))
    acc = call(
        lambda *refs: products_kernel(OFFSETS[1:5], *refs), info, [a] + five[1:] + five_x[1:] + [acc], block_of_products, 1
    )
    q3, acc = wall((q3, acc))

    q3x = moved(q3, other_core)
    p4, middle = wall((p4, middle))

    p4x = moved(p4, other_core)
    two, two_x = [p3, q3x], [q3, p3x]
    acc = call(
        lambda *refs: products_kernel(OFFSETS[5:7], *refs), info, [a] + two + two_x + [acc], block_of_products, 1
    )
    late = moved(call(cut_kernel, info, two + [p4] + two_x + [p4x], slices_of(3), 1), hub_ahead(0))
    half_block = jax.ShapeDtypeStruct((2, 64, 1024), BF16)
    keep, send, product, early = call(
        last_kernel,
        info,
        [a, acc, near, middle] + five + two + [p4] + five_x + two_x + [p4x],
        (half_block, half_block, block_of_products, jax.ShapeDtypeStruct((8, 128), F32)),
        WEIGHT,
        [pltpu.VMEM((2, 128, 1024), BF16)],
    )
    trace = call(trace_kernel, info, [product, early, late], jax.ShapeDtypeStruct((1, 128), F32), WEIGHT)

    kept, sent = moved(keep, from_hub(0)), moved(send, from_hub(1))
    first, second = moved(trace, from_hub(0)), moved(trace, from_hub(1))
    both = jnp.where(half == 0, jnp.concatenate([first, second]), jnp.concatenate([second, first]))
    both, kept = wall((both, kept))
    below, above = moved(both, along(3)), moved(both, along(-3))
    pair = jax.ShapeDtypeStruct((2, 128), F32)
    two, three = call(add_kernel, info, [below, both, above], (pair, pair), WEIGHT)
    below, above = moved(three, along(1)), moved(two, along(-1))
    both = below + three + above
    products = jnp.where(half == 0, jnp.stack([kept, sent]), jnp.stack([sent, kept]))[:, None, None]
    correlator = jnp.sum(both[:, :16].reshape(2, 8, 2), axis=1)[:, None, None, :] / F32(1024)
    return products, correlator


def solution(mesh):
    return jax.shard_map(
        shards,
        mesh=mesh,
        in_specs=(P(None, "tm", None, "row", None), P()),
        out_specs=(P(None, None, "tm", None, "row", None), P(None, None, "tm", None)),
        check_vma=False,
    )
```

```python
import jax
import jax.numpy as jnp
from jax import lax
from jax.experimental import pallas as pl
from jax.experimental.pallas import tpu as pltpu
from jax.sharding import PartitionSpec as P

BOTH = ("tm", "row")
BF16 = jnp.bfloat16
F32 = jnp.float32


def hub_of(s):
    m, odd = divmod(s % 16, 2)
    low, x = divmod(m, 4)
    return (1 - low) * 4 + x, odd ^ low


SERVED = {hub_of(s): s for s in range(16)}


def moved(block, route):
    def index_of(m, c, z, h):
        return ((m % 8) * 2 + c) * 16 + (z % 8) * 2 + h

    places = [(m, c, z, h) for m in range(8) for c in range(2) for z in range(8) for h in range(2)]
    return lax.ppermute(block, BOTH, [(index_of(*at), index_of(*route(*at))) for at in places])


def onward(m, c, z, h):
    return (m, c, z + (1 if c == 0 else -1), h)


def along(step):
    return lambda m, c, z, h: (m, c, z + step, h)


def other_core(m, c, z, h):
    return (m, 1 - c, z, h)


def to_hub(m, c, z, h):
    column, half = hub_of(2 * m + c)
    return (column, h, z, half)


def hub_ahead(step):
    def route(m, c, z, h):
        column, half = hub_of(SERVED[m, h] + 1 + c)
        return (column, c, z + (step if c == 0 else -step), half)

    return route


def from_hub(turn):
    def route(m, c, z, h):
        t = (SERVED[m, h] - 1 - c) % 16
        return (t // 2, t % 2, z, c ^ turn)

    return route


WEIGHT = 3_000_000_000

VMEM = pl.BlockSpec(memory_space=pltpu.VMEM)
SMEM = pl.BlockSpec(memory_space=pltpu.SMEM)


def slices_of(count):
    return jax.ShapeDtypeStruct((count, 2, 128, 128), BF16)


def call(kernel, info, arrays, out_shape, flops, scratch=()):
    outs = jax.tree.map(lambda _: VMEM, out_shape)
    return pl.pallas_call(
        kernel,
        out_shape=out_shape,
        in_specs=[SMEM] + [VMEM] * len(arrays),
        out_specs=outs,
        scratch_shapes=scratch,
        compiler_params=pltpu.CompilerParams(vmem_limit_bytes=24 * 1024 * 1024),
        cost_estimate=pl.CostEstimate(flops=flops, bytes_accessed=1 << 20, transcendentals=0),
    )(info, *arrays)


def place_of(info, offset):
    return lax.rem(info[0] + jnp.where(info[1] == 0, 8 - offset, 8 + offset), 8)


def columns_of(info, offset):
    return pl.ds(pl.multiple_of(place_of(info, offset) * 128, 128), 128)


def halves(info, own, other):
    first = jnp.where(info[1] == 0, own, other)
    second = jnp.where(info[1] == 0, other, own)
    return first, second


def whole(info, own_ref, other_ref, momentum, part):
    return jnp.concatenate(halves(info, own_ref[momentum, part], other_ref[momentum, part]), axis=0)


def cut(info, own_ref, other_ref, offset, out):
    columns = columns_of(info, offset)
    for part in range(2):
        first, second = halves(info, own_ref[info[5], part, :, columns], other_ref[info[5], part, :, columns])
        out[part] = jnp.concatenate([first, second], axis=0).T


def first_cut_kernel(info, own, other, a):
    for part in range(2):
        a[part] = whole(info, own, other, info[2], part)


def cut_kernel(info, *refs):
    count = len(refs) // 2
    for k in range(count):
        cut(info, refs[k], refs[count + k], 0, refs[-1].at[k])


def left_side(info, a_ref, offset):
    columns = columns_of(info, offset)
    real, imag = a_ref[0, :, columns], a_ref[1, :, columns]
    return jnp.concatenate(
        [jnp.concatenate([real, -imag], axis=1), jnp.concatenate([imag, real], axis=1)], axis=0
    )


def products_kernel(offsets, info, a_ref, *refs):
    count = len(offsets)
    own, other, out = refs[:count], refs[count : 2 * count], refs[-1]
    total = refs[2 * count][...] if len(refs) > 2 * count + 1 else None
    for offset, one, two in zip(offsets, own, other):
        block = jnp.concatenate([whole(info, one, two, info[3], part) for part in range(2)], axis=0)
        term = jnp.dot(left_side(info, a_ref, offset), block, preferred_element_type=F32)
        total = term if total is None else total + term
    out[...] = total


OFFSETS = (0, 1, -1, 2, -2, 3, -3, 4)


def last_kernel(info, a_ref, acc, near, middle, *refs):
    own, other = refs[0:8], refs[8:16]
    keep, send, out, early, rounded_ref = refs[16:21]
    block = jnp.concatenate([whole(info, own[7], other[7], info[3], part) for part in range(2)], axis=0)
    product = acc[...] + jnp.dot(left_side(info, a_ref, 4), block, preferred_element_type=F32)
    rounded = product.astype(BF16)
    for part in range(2):
        rounded_ref[part] = rounded[part * 128 : part * 128 + 128]
        low, high = rounded[part * 128 : part * 128 + 64], rounded[part * 128 + 64 : part * 128 + 128]
        keep[part], send[part] = halves(info, low, high)
    total = None
    for offset, one, two in zip(OFFSETS, own, other):
        block = jnp.concatenate([whole(info, one, two, info[4], part) for part in range(2)], axis=0)
        term = jnp.dot(left_side(info, rounded_ref, offset), block, preferred_element_type=F32)
        total = term if total is None else total + term
    out[...] = total
    slices = [near.at[0], near.at[1], near.at[2], middle.at[0], middle.at[1]]
    early[0:1, :], early[1:2, :] = trace_sum(info, out, list(zip(OFFSETS, slices)))


def trace_sum(info, product, slices):
    re = im = None
    for offset, piece in slices:
        columns = columns_of(info, offset)
        q_re, q_im = product[0:128, columns], product[128:256, columns]
        d_re, d_im = piece[0].astype(F32), piece[1].astype(F32)
        more_re, more_im = q_re * d_re - q_im * d_im, q_re * d_im + q_im * d_re
        re = more_re if re is None else re + more_re
        im = more_im if im is None else im + more_im
    return [jnp.sum(part, axis=0, keepdims=True) for part in (re, im)]


def trace_kernel(info, product, early, late, trace):
    re, im = trace_sum(info, product, [(3, late.at[0]), (-3, late.at[1]), (4, late.at[2])])
    re = jnp.sum(re + early[0:1, :], axis=1, keepdims=True)
    im = jnp.sum(im + early[1:2, :], axis=1, keepdims=True)
    lane = lax.broadcasted_iota(jnp.int32, (1, 128), 1)
    trace[...] = jnp.where(lane == 2 * info[0], re, jnp.where(lane == 2 * info[0] + 1, im, 0.0))


def shards(fields, mom_table):
    rows = fields[:, 0]
    tm, row = lax.axis_index("tm"), lax.axis_index("row")
    core, place, half = tm % 2, row // 2, row % 2
    momenta = lax.dynamic_index_in_dim(mom_table, core, 0, keepdims=False)[0]
    info = jnp.concatenate([jnp.stack([place, core]), momenta])
    wall = lax.optimization_barrier
    block_of_products = jax.ShapeDtypeStruct((256, 1024), F32)

    own = moved(rows, to_hub)

    ownx, p1 = moved(own, other_core), moved(own, onward)
    q1 = moved(ownx, onward)
    a = call(first_cut_kernel, info, [own, ownx], jax.ShapeDtypeStruct((2, 128, 1024), BF16), 1)
    a = moved(a, hub_ahead(0))

    p2, p1x = moved(p1, onward), moved(p1, other_core)
    q2, q1x = moved(q1, onward), moved(q1, other_core)
    three, three_x = [own, p1, q1x], [ownx, q1, p1x]
    near = call(cut_kernel, info, three + three_x, slices_of(3), 1)
    acc = call(lambda *refs: products_kernel(OFFSETS[:1], *refs), info, [a, own, ownx], block_of_products, WEIGHT)
    p2, a, acc = wall((p2, a, acc))

    near = moved(near, hub_ahead(0))
    p3, p2x = moved(p2, onward), moved(p2, other_core)
    q3, q2x = moved(q2, onward), moved(q2, other_core)
    p3, near = wall((p3, near))

    p4, p3x = moved(p3, onward), moved(p3, other_core)
    five, five_x = three + [p2, q2x], three_x + [q2, p2x]
    middle = moved(call(cut_kernel, info, five[3:] + five_x[3:], slices_of(2), 1), hub_ahead(0))
    acc = call(
        lambda *refs: products_kernel(OFFSETS[1:5], *refs), info, [a] + five[1:] + five_x[1:] + [acc], block_of_products, 1
    )
    q3, acc = wall((q3, acc))

    q3x = moved(q3, other_core)
    p4, middle = wall((p4, middle))

    p4x = moved(p4, other_core)
    two, two_x = [p3, q3x], [q3, p3x]
    acc = call(
        lambda *refs: products_kernel(OFFSETS[5:7], *refs), info, [a] + two + two_x + [acc], block_of_products, 1
    )
    late = moved(call(cut_kernel, info, two + [p4] + two_x + [p4x], slices_of(3), 1), hub_ahead(0))
    half_block = jax.ShapeDtypeStruct((2, 64, 1024), BF16)
    keep, send, product, early = call(
        last_kernel,
        info,
        [a, acc, near, middle] + five + two + [p4] + five_x + two_x + [p4x],
        (half_block, half_block, block_of_products, jax.ShapeDtypeStruct((8, 128), F32)),
        WEIGHT,
        [pltpu.VMEM((2, 128, 1024), BF16)],
    )
    trace = call(trace_kernel, info, [product, early, late], jax.ShapeDtypeStruct((1, 128), F32), WEIGHT)

    kept, sent = moved(keep, from_hub(0)), moved(send, from_hub(1))
    first, second = moved(trace, from_hub(0)), moved(trace, from_hub(1))
    both = jnp.where(half == 0, jnp.concatenate([first, second]), jnp.concatenate([second, first]))
    both, kept = wall((both, kept))
    below, above = moved(both, along(3)), moved(both, along(-3))
    two, three = below + both, below + both + above
    below, above = moved(three, along(1)), moved(two, along(-1))
    both = below + three + above
    products = jnp.where(half == 0, jnp.stack([kept, sent]), jnp.stack([sent, kept]))[:, None, None]
    correlator = jnp.sum(both[:, :16].reshape(2, 8, 2), axis=1)[:, None, None, :] / F32(1024)
    return products, correlator


def solution(mesh):
    return jax.shard_map(
        shards,
        mesh=mesh,
        in_specs=(P(None, "tm", None, "row", None), P()),
        out_specs=(P(None, None, "tm", None, "row", None), P(None, None, "tm", None)),
        check_vma=False,
    )
```
